128 devices in a mesh: dp: 4 (over x), expert: 32 (over y, z, core).
Axes of the slice: x: 4, y: 4, z: 4, core: 2. Of those that a mesh axis runs over, the one named last changes fastest.
Arguments:
- tokens: bfloat16 [32768, 2048], P(('dp', 'expert')), may hold values from -6 to 6
- out_grad: bfloat16 [32768, 2048], P(('dp', 'expert')), may hold values from -6 to 6
- token_picks: int32 [128, 64, 8], P(('dp', 'expert')), may hold values from 0 to 255, as said below
- router: bfloat16 [2048, 64], P(None, 'expert'), may hold values from -0.125 to 0.125
- kept_blocks: int32 [64, 3, 128], P('expert'), may hold values from 0 to 384, as said below
- masters: float32 [64, 3, 128, 4096], P('expert', None, 'dp'), may hold values from -0.25 to 0.25
- scores: float32 [64, 3, 128], P('expert', None, 'dp'), may hold values from -6 to 6
Outputs:
- layer_out: bfloat16 [32768, 2048], P(('dp', 'expert'))
- input_grad: bfloat16 [32768, 2048], P(('dp', 'expert'))
- master_new: float32 [64, 3, 128, 4096], P('expert', None, 'dp')
- score_new: float32 [64, 3, 128], P('expert', None, 'dp')
- router_grad: float32 [2048, 64], P('dp', 'expert')
The draws below stay inside these ranges and needn't reach their ends.
Inputs may be any that keep to these rules, and one draw needn't show every extreme that they name: `token_picks`: within one source block and one expert the 8 picks are distinct tokens. `kept_blocks`: each list of 128 slots holds, in ascending order, between 64 and 128 distinct block numbers below 384, then 384 in the remaining slots; for each of the three matrices the list of some expert is full.
All inputs are finite; a program needn't handle non-finite values.
Results may differ from the reference program's by a relative error of at most 0.0081.
Values may be sent and summed in bfloat16 or wider, within the bound.
No kernel may reach another device: no remote copies, remote signals or barrier semaphores. Data moves between devices by JAX's collectives and lax.ppermute only.
A program may use at most 192 MiB of HBM per device.

```python
import jax
import jax.numpy as jnp
from jax import lax

D = 2048
FF = 768
BS = 64
MAXB = 128
TOK_DEV = 256
CAP = 8
E = 64
GROUP = 32
SOURCES = 128
TOKENS = 32768
N_DP = 4


def draw_token_picks(key, part):
    keys = jax.random.split(jax.random.fold_in(key, 11), SOURCES * E)
    chosen = jax.vmap(lambda single: jax.random.permutation(single, TOK_DEV)[:CAP])(keys)
    return chosen.reshape(SOURCES, E, CAP).astype(jnp.int32)


def draw_kept_blocks(key, part):
    blocks_total = D // BS * (FF // BS)
    count_key = jax.random.fold_in(key, 21)
    full_key = jax.random.fold_in(key, 22)
    order_key = jax.random.fold_in(key, 23)
    counts = jax.random.randint(count_key, (E, 3), MAXB // 2, MAXB + 1)
    fullest = jax.random.randint(full_key, (3,), 0, E)
    counts = jnp.where(jnp.arange(E)[:, None] == fullest[None, :], MAXB, counts)
    keys = jax.random.split(order_key, E * 3)
    chosen = jax.vmap(lambda single: jax.random.permutation(single, blocks_total)[:MAXB])(keys)
    chosen = chosen.reshape(E, 3, MAXB).astype(jnp.int32)
    slots = jnp.arange(MAXB)[None, None, :]
    chosen = jnp.where(slots < counts[:, :, None], chosen, blocks_total)
    return jnp.sort(chosen, axis=-1).astype(jnp.int32)


def block_scale(rng, dims, shards, smallest, top_value):
    factor_of, own = 1.0, jax.random.fold_in(rng, 6)
    for dim, blocks in shards:
        heights = jnp.exp(jax.random.uniform(jax.random.fold_in(own, dim), (blocks,), jnp.float32, smallest / len(shards), top_value / len(shards)))
        factor_of = factor_of * jnp.repeat(heights, dims[dim] // blocks).reshape([-1 if axis == dim else 1 for axis in range(len(dims))])
    return factor_of


def gaussian(stream_key, shape, deviation, limit, cuts=(), held_as=jnp.bfloat16):
    drawn = deviation * jax.random.normal(stream_key, shape, jnp.float32)
    if cuts:
        drawn = drawn * block_scale(stream_key, shape, cuts, -0.22, 0.18)
    return jnp.clip(drawn, -limit, limit).astype(held_as)


def setup_inputs(seed: int = 0) -> dict:
    arg_keys = jax.random.split(jax.random.key(seed), 8)
    return {
        "tokens": gaussian(arg_keys[0], (TOKENS, D), 1.0, 6.0, ((0, 128),)),
        "out_grad": gaussian(arg_keys[1], (TOKENS, D), 1.0, 6.0, ((0, 128),)),
        "token_picks": draw_token_picks(jax.random.fold_in(arg_keys[7], 71), 0),
        "router": gaussian(arg_keys[3], (D, E), D ** -0.5, 0.125, ((1, 32),)),
        "kept_blocks": draw_kept_blocks(jax.random.fold_in(arg_keys[7], 71), 0),
        "masters": gaussian(arg_keys[5], (E, 3, MAXB, BS * BS), (D // 4) ** -0.5, 0.25, ((0, 32), (2, 4)), jnp.float32),
        "scores": gaussian(arg_keys[6], (E, 3, MAXB), 1.0, 6.0, ((0, 32), (2, 4)), jnp.float32),
    }


LEARN_RATE = 0.005
SCORE_RATE = 0.05

def layouts(kept_rows, in_blocks, hid_blocks):
    blocks_total = in_blocks * hid_blocks
    plan_list = []
    for matrix, col_count in ((0, hid_blocks), (1, hid_blocks), (2, in_blocks)):
        usable = kept_rows[matrix] < blocks_total
        safe_index = jnp.where(usable, kept_rows[matrix], 0).astype(jnp.int32)
        plan_list.append((safe_index // col_count, safe_index % col_count, usable, safe_index))
    return plan_list

def masked_tiles(tile_stack, plan_list):
    return [jnp.where(plan_list[matrix][2][:, None, None], tile_stack[matrix], jnp.zeros_like(tile_stack[matrix])) for matrix in range(3)]

def sparse_apply(operand, tile_set, src_blocks, dst_blocks, usable, out_blocks):
    row_count = operand.shape[0]
    tile_width = tile_set.shape[-1]
    pieces = jnp.take(operand.reshape(row_count, -1, tile_width), src_blocks, axis=1)
    partial_out = jnp.einsum('rmk,mkn->rmn', pieces.astype(jnp.float32), tile_set.astype(jnp.float32), precision=lax.Precision.HIGHEST)
    placer = ((dst_blocks[:, None] == jnp.arange(out_blocks)[None, :]) & usable[:, None]).astype(jnp.float32)
    placed = jnp.einsum('rmn,mc->rcn', partial_out, placer, precision=lax.Precision.HIGHEST)
    return placed.reshape(row_count, out_blocks * tile_width)

def project(operand, weight, flipped, row_blocks, col_blocks):
    tile_set, block_plan = weight
    if flipped:
        return sparse_apply(operand, jnp.swapaxes(tile_set, 1, 2), block_plan[1], block_plan[0], block_plan[2], row_blocks)
    return sparse_apply(operand, tile_set, block_plan[0], block_plan[1], block_plan[2], col_blocks)

def weight_grad(operand, cotangent, weight):
    tile_set, block_plan = weight
    tile_width = tile_set.shape[-1]
    row_count = operand.shape[0]
    left_part = jnp.take(operand.reshape(row_count, -1, tile_width), block_plan[0], axis=1).astype(jnp.float32)
    right_part = jnp.take(cotangent.reshape(row_count, -1, tile_width), block_plan[1], axis=1).astype(jnp.float32)
    gradient = jnp.einsum('rmk,rmn->mkn', left_part, right_part, precision=lax.Precision.HIGHEST)
    gradient = jnp.where(block_plan[2][:, None, None], gradient, jnp.zeros_like(gradient))
    return gradient.reshape(-1, tile_width * tile_width)

def expert_forward(rows_in, weights, router_col, in_blocks, hid_blocks):
    gate_pre = project(rows_in, weights[0], False, in_blocks, hid_blocks)
    up_pre = project(rows_in, weights[1], False, in_blocks, hid_blocks)
    hidden = (jax.nn.silu(gate_pre) * up_pre).astype(jnp.bfloat16)
    output = project(hidden, weights[2], False, hid_blocks, in_blocks)
    gating = jax.nn.sigmoid(jnp.dot(rows_in, router_col, preferred_element_type=jnp.float32))
    part_out = (gating[:, None] * output).astype(jnp.bfloat16)
    return (part_out, (gate_pre, up_pre, hidden, output, gating))

def expert_down_grad(grad_rows, saved_state, weights, in_blocks, hid_blocks):
    gate_pre, up_pre, hidden, output, gating = saved_state
    grad_float = grad_rows.astype(jnp.float32)
    logit_grad = lax.optimization_barrier(jnp.sum(grad_float * output, axis=1)) * gating * (1.0 - gating)
    scaled = (gating[:, None] * grad_float).astype(jnp.bfloat16)
    down_grad = weight_grad(hidden, scaled, weights[2])
    hidden_grad = project(scaled, weights[2], True, hid_blocks, in_blocks)
    return (down_grad, (hidden_grad, logit_grad))

def expert_rest_grad(rows_in, carried, saved_state, weights, router_col, in_blocks, hid_blocks):
    hidden_grad, logit_grad = carried
    gate_pre, up_pre = (saved_state[0], saved_state[1])
    sigmoid = jax.nn.sigmoid(gate_pre)
    gate_grad = (hidden_grad * up_pre * sigmoid * (1.0 + gate_pre * (1.0 - sigmoid))).astype(jnp.bfloat16)
    up_grad = (hidden_grad * gate_pre * sigmoid).astype(jnp.bfloat16)
    gate_weight = weight_grad(rows_in, gate_grad, weights[0])
    up_weight = weight_grad(rows_in, up_grad, weights[1])
    input_part = project(gate_grad, weights[0], True, in_blocks, hid_blocks) + project(up_grad, weights[1], True, in_blocks, hid_blocks)
    input_part = input_part + logit_grad[:, None] * router_col.astype(jnp.float32)[None, :]
    router_part = jnp.dot(logit_grad, rows_in.astype(jnp.float32), precision=lax.Precision.HIGHEST)
    return (input_part.astype(jnp.bfloat16), gate_weight, up_weight, router_part)

def reference(tokens, out_grad, token_picks, router, kept_blocks, masters, scores):
    in_blocks = D // BS
    hid_blocks = FF // BS
    copies = masters.astype(jnp.bfloat16).reshape(E, 3, MAXB, BS, BS)
    starts = (jnp.arange(SOURCES) * TOK_DEV).astype(jnp.int32)[:, None]
    picks_by_expert = jnp.transpose(token_picks, (1, 0, 2))

    def one_expert(carried_sums, expert_item):
        out_sum, input_sum = carried_sums
        kept_rows, tile_stack, router_col, chosen = expert_item
        plan_list = layouts(kept_rows, in_blocks, hid_blocks)
        tile_list = masked_tiles(tile_stack, plan_list)
        weights = [(tile_list[matrix], plan_list[matrix]) for matrix in range(3)]
        index_all = (chosen.astype(jnp.int32) + starts).astype(jnp.int32)
        grads = jnp.zeros((3, MAXB, BS * BS), jnp.float32)
        router_sum = jnp.zeros((D,), jnp.float32)
        for dp_group in range(N_DP):
            row_index = index_all[dp_group * GROUP:(dp_group + 1) * GROUP].reshape(-1)
            rows_in = tokens[row_index]
            grad_rows = out_grad[row_index]
            part_out, saved_state = expert_forward(rows_in, weights, router_col, in_blocks, hid_blocks)
            down_grad, inner_state = expert_down_grad(grad_rows, saved_state, weights, in_blocks, hid_blocks)
            input_part, gate_weight, up_weight, router_part = expert_rest_grad(rows_in, inner_state, saved_state, weights, router_col, in_blocks, hid_blocks)
            grads = grads + jnp.stack([gate_weight, up_weight, down_grad])
            router_sum = router_sum + router_part
            out_sum = out_sum.at[row_index].add(part_out.astype(jnp.float32))
            input_sum = input_sum.at[row_index].add(input_part.astype(jnp.float32))
        return ((out_sum, input_sum), (grads, router_sum))
    zeros_init = (jnp.zeros((TOKENS, D), jnp.float32), jnp.zeros((TOKENS, D), jnp.float32))
    sums, stacked = lax.scan(one_expert, zeros_init, (kept_blocks, copies, router.T, picks_by_expert))
    grads, router_rows = stacked
    master_new = masters - LEARN_RATE * grads
    score_new = scores - SCORE_RATE * lax.optimization_barrier(jnp.sum(masters * grads, axis=-1))
    return (sums[0].astype(jnp.bfloat16), sums[1].astype(jnp.bfloat16), master_new, score_new, router_rows.T)
```

```python
import functools

import jax
import jax.numpy as jnp
from jax import lax
from jax.experimental import pallas as pl
from jax.experimental.pallas import tpu as pltpu
from jax.sharding import PartitionSpec as P

D = 2048
FF = 768
BS = 64
MAXB = 128
BLOCKS = (D // BS) * (FF // BS)
LEARN_RATE = 0.005
SCORE_RATE = 0.05
CHUNK = 256
F32 = jnp.float32
BF16 = jnp.bfloat16
NN = (((1,), (0,)), ((), ()))
NT = (((1,), (1,)), ((), ()))
TN = (((0,), (0,)), ((), ()))


def dot(left, right, dims=NN):
    return lax.dot_general(left, right, dims, preferred_element_type=F32)


def iota(shape, dim):
    return lax.broadcasted_iota(jnp.int32, shape, dim)


def one_hot(flag):
    return jnp.where(flag, 1.0, 0.0).astype(BF16)


def split_matrix(size):
    col = iota((size, size), 1)
    source = ((col >> 6) << 6) + 2 * (col & 31) + ((col >> 5) & 1)
    return one_hot(iota((size, size), 0) == source)


def pick_columns(picks_ref, member, locals_count):
    peers = picks_ref.shape[0] // locals_count
    rows = 16 * peers
    row = iota((rows, picks_ref.shape[0]), 0)
    expert = (row >> 4) * locals_count + member
    spread = one_hot(iota((rows, picks_ref.shape[0]), 1) == expert)
    table = picks_ref[...].astype(F32).astype(BF16)
    wide = dot(spread, table)
    keep = iota(wide.shape, 1) == (iota(wide.shape, 0) & 7)
    return jnp.sum(jnp.where(keep, wide, 0.0), axis=1, keepdims=True).astype(jnp.int32)


def pick_kernel(picks_ref, tokens_ref, grads_ref, *rest, locals_count):
    out_refs, hot_ref = rest[:locals_count], rest[locals_count]
    rows = hot_ref.shape[1]
    count = tokens_ref.shape[0]

    @pl.when(pl.program_id(0) == 0)
    def _():
        for member in range(locals_count):
            index = pick_columns(picks_ref, member, locals_count)
            row = iota((rows, 1), 0)
            index = index + jnp.where((row & 8) > 0, count, 0)
            hot_ref[member] = one_hot(iota((rows, 2 * count), 1) == index)

    split = split_matrix(CHUNK)
    both = jnp.concatenate([dot(tokens_ref[...], split).astype(BF16), grads_ref[...]], axis=0)
    for member in range(locals_count):
        picked = dot(hot_ref[member], both).astype(BF16)
        out_refs[member][...] = picked.reshape(out_refs[member].shape)


def pack_kernel(masters_ref, out_ref, lines_ref):
    for group in range(masters_ref.shape[0] // 8):
        for k in range(32):
            lines_ref[group, 8 * k : 8 * k + 8, :] = masters_ref[
                8 * group : 8 * group + 8, 128 * k : 128 * k + 128
            ]
        for s in range(8):
            out_ref[8 * group + s] = lines_ref[group, pl.ds(s, 32, stride=8), :].astype(BF16)


def expert_kernel(
    inverse_ref, row_ref, lane_ref, valid_ref,
    copies_ref, arrived_ref, router_ref,
    send_ref, packed_ref, router_out_ref,
    wide_ref, down_ref, rows_ref, grads_ref, pre_ref, part_ref, both_ref,
    grad_wide_ref, grad_down_ref,
    *, base,
):
    lane = iota((32, 128), 1)
    half = lane < 64

    def place(target_ref, matrix, block, row, col):
        first = inverse_ref[base + matrix * BLOCKS + block]
        second = inverse_ref[base + matrix * BLOCKS + block + 1]
        one = copies_ref[jnp.maximum(first, 0)]
        two = copies_ref[jnp.maximum(second, 0)]
        one = jnp.where(lane < jnp.where(first >= 0, 128, 0), one, jnp.zeros_like(one))
        two = jnp.where(lane < jnp.where(second >= 0, 128, 0), two, jnp.zeros_like(two))
        target_ref[pl.ds(row, 32), col : col + 128] = jnp.where(half, one, pltpu.roll(two, 64, 1))
        target_ref[pl.ds(row + 32, 32), col : col + 128] = jnp.where(half, pltpu.roll(one, 64, 1), two)

    @pl.loop(0, D // BS)
    def _(r):
        row = pl.multiple_of(r * BS, BS)
        for matrix in range(2):
            for pair in range(FF // BS // 2):
                place(wide_ref, matrix, r * (FF // BS) + 2 * pair, row, matrix * FF + 128 * pair)

    @pl.loop(0, FF // BS)
    def _(r):
        row = pl.multiple_of(r * BS, BS)
        for pair in range(D // BS // 2):
            place(down_ref, 2, r * (D // BS) + 2 * pair, row, 128 * pair)

    count = rows_ref.shape[0]
    wanted = iota((count, 2 * count), 0)
    wanted = ((wanted >> 3) << 4) + (wanted & 7)
    first_rows = one_hot(iota((count, 2 * count), 1) == wanted)
    second_rows = one_hot(iota((count, 2 * count), 1) == wanted + 8)
    chunks = D // CHUNK

    def take(n, logit):
        cols = pl.ds(pl.multiple_of(n * CHUNK, CHUNK), CHUNK)
        block = arrived_ref[:, :, cols].reshape(2 * count, CHUNK)
        rows = dot(first_rows, block)
        rows_ref[:, cols] = rows.astype(BF16)
        grads_ref[:, cols] = dot(second_rows, block).astype(BF16)
        return logit + jnp.sum(rows * router_ref[:, cols], axis=1, keepdims=True)

    logit = lax.fori_loop(0, chunks, take, jnp.zeros((count, 1), F32))
    gating = 1.0 / (1.0 + jnp.exp(-logit))

    @pl.loop(0, 2 * FF // 512)
    def _(n):
        cols = pl.ds(pl.multiple_of(n * 512, 512), 512)
        pre_ref[:, cols] = dot(rows_ref[...], wide_ref[:, cols])

    split = split_matrix(CHUNK)
    hidden_list = []
    for n in range(FF // CHUNK):
        gate_pre = pre_ref[:, n * CHUNK : (n + 1) * CHUNK]
        up_pre = pre_ref[:, FF + n * CHUNK : FF + (n + 1) * CHUNK]
        hidden = (gate_pre / (1.0 + jnp.exp(-gate_pre)) * up_pre).astype(BF16)
        hidden_list.append(dot(hidden, split).astype(BF16))
    hidden_split = jnp.concatenate(hidden_list, axis=1)

    @pl.loop(0, D // 512)
    def _(n):
        cols = pl.ds(pl.multiple_of(n * 512, 512), 512)
        part_ref[:, cols] = (gating * dot(hidden_split, down_ref[:, cols])).astype(BF16)
        grads_ref[:, cols] = (gating * grads_ref[:, cols].astype(F32)).astype(BF16)

    logit_sum = jnp.zeros((count, 1), F32)
    for n in range(FF // CHUNK):
        spread = dot(grads_ref[...], down_ref[n * CHUNK : (n + 1) * CHUNK, :], NT)
        high = spread.astype(BF16)
        low = (spread - high.astype(F32)).astype(BF16)
        hidden_grad = dot(high, split, NT) + dot(low, split, NT)
        logit_sum = logit_sum + jnp.sum(
            hidden_list[n].astype(F32) * spread, axis=1, keepdims=True
        )
        gate_pre = pre_ref[:, n * CHUNK : (n + 1) * CHUNK]
        up_pre = pre_ref[:, FF + n * CHUNK : FF + (n + 1) * CHUNK]
        sigma = 1.0 / (1.0 + jnp.exp(-gate_pre))
        gate_grad = hidden_grad * up_pre * sigma * (1.0 + gate_pre * (1.0 - sigma))
        both_ref[:, n * CHUNK : (n + 1) * CHUNK] = gate_grad.astype(BF16)
        both_ref[:, FF + n * CHUNK : FF + (n + 1) * CHUNK] = (hidden_grad * gate_pre * sigma).astype(BF16)
        grad_down_ref[n * CHUNK : (n + 1) * CHUNK, :] = dot(hidden_list[n], grads_ref[...], TN).astype(BF16)
    logit_grad = logit_sum * (1.0 - gating)

    @pl.loop(0, chunks)
    def _(n):
        cols = pl.ds(pl.multiple_of(n * CHUNK, CHUNK), CHUNK)
        part = dot(both_ref[...], wide_ref[cols, :], NT) + logit_grad * router_ref[:, cols]
        pair = jnp.concatenate(
            [part_ref[:, cols].astype(F32).reshape(-1, 8, CHUNK), part.reshape(-1, 8, CHUNK)], axis=1
        )
        send_ref[:, :, cols] = pair.astype(BF16)
        rows = rows_ref[:, cols]
        router_out_ref[:, cols] = jnp.sum(logit_grad * rows.astype(F32), axis=0, keepdims=True)
        grad_wide_ref[cols, :] = dot(rows, both_ref[...], TN).astype(BF16)

    def cut(source_ref, matrix, slot, place_in):
        at = matrix * MAXB + slot
        row = pl.multiple_of(row_ref[at], 32)
        other = pl.multiple_of(row ^ 32, 32)
        cols = pl.ds(pl.multiple_of(lane_ref[at], 128), 128)
        odd = row & 32
        stay = source_ref[pl.ds(row, 32), cols]
        move = pltpu.roll(source_ref[pl.ds(other, 32), cols], 64, 1)
        tile = jnp.where((lane & 64) == 2 * odd, stay, move)
        limit = jnp.where(valid_ref[at] > 0, 128, 0)
        packed_ref[place_in] = jnp.where(lane < limit, tile, jnp.zeros_like(tile))

    slots = MAXB // (packed_ref.shape[0] // (3 * (MAXB // 4)))
    per = MAXB // 4

    for owner in range(4):
        for matrix in range(3):
            source_ref = grad_down_ref if matrix == 2 else grad_wide_ref

            @pl.loop(0, per // 4)
            def _(group, owner=owner, matrix=matrix, source_ref=source_ref):
                for step in range(4):
                    s = group * 4 + step
                    cut(source_ref, matrix, owner * per + s, (owner * 3 + matrix) * per + s)


def update_kernel(summed_ref, masters_ref, out_ref, total_ref, lines_ref):
    for group in range(masters_ref.shape[0] // 8):
        for s in range(8):
            lines_ref[group, pl.ds(s, 32, stride=8), :] = summed_ref[8 * group + s].astype(F32)
        total = jnp.zeros((8, 128), F32)
        rows = slice(8 * group, 8 * group + 8)
        for k in range(32):
            cols = slice(128 * k, 128 * k + 128)
            gradient = lines_ref[group, 8 * k : 8 * k + 8, :]
            held = masters_ref[rows, cols]
            out_ref[rows, cols] = held - LEARN_RATE * gradient
            total = total + held * gradient
        total_ref[rows, :] = jnp.sum(total, axis=1, keepdims=True)


def combine_kernel(picks_ref, *rest, locals_count):
    back_refs = rest[:locals_count]
    out_ref, in_ref, hot_ref = rest[locals_count:]
    rows, count = hot_ref.shape[2], hot_ref.shape[3]

    @pl.when(pl.program_id(0) == 0)
    def _():
        for member in range(locals_count):
            index = pick_columns(picks_ref, member, locals_count)
            late = (iota((rows, 1), 0) & 8) > 0
            for side in range(2):
                mine = jnp.where(late == (side == 1), index, -1)
                hot_ref[side, member] = one_hot(iota((rows, count), 1) == mine)

    sums = [jnp.zeros((count, CHUNK), F32), jnp.zeros((count, CHUNK), F32)]
    for member in range(locals_count):
        block = back_refs[member][...].reshape(rows, CHUNK)
        for side in range(2):
            sums[side] = sums[side] + dot(hot_ref[side, member], block, TN)
    out_ref[...] = sums[0].astype(BF16)
    in_ref[...] = dot(sums[1].astype(BF16), split_matrix(CHUNK), NT).astype(BF16)


def params(mib):
    return pltpu.CompilerParams(vmem_limit_bytes=mib * 1024 * 1024)


def cost(flops, moved):
    return pl.CostEstimate(flops=flops, bytes_accessed=moved, transcendentals=0)


def pick(picks, tokens, grads, locals_count, peers):
    count, width = tokens.shape
    rows = 16 * peers
    column = pl.BlockSpec((count, CHUNK), lambda n: (0, n))
    return pl.pallas_call(
        functools.partial(pick_kernel, locals_count=locals_count),
        grid=(width // CHUNK,),
        in_specs=[pl.BlockSpec(picks.shape, lambda n: (0, 0)), column, column],
        out_specs=[pl.BlockSpec((peers, 16, CHUNK), lambda n: (0, 0, n))] * locals_count,
        out_shape=[jax.ShapeDtypeStruct((peers, 16, width), BF16)] * locals_count,
        scratch_shapes=[pltpu.VMEM((locals_count, rows, 2 * count), BF16)],
        compiler_params=params(32),
        cost_estimate=cost(2 * rows * 2 * count * width * locals_count, 12 << 20),
        name="pick",
    )(picks, tokens, grads)


def pack(masters):
    slots = masters.shape[0]
    return pl.pallas_call(
        pack_kernel,
        grid=(slots // 32,),
        in_specs=[pl.BlockSpec((32, BS * BS), lambda n: (n, 0))],
        out_specs=pl.BlockSpec((32, 32, 128), lambda n: (n, 0, 0)),
        out_shape=jax.ShapeDtypeStruct((slots, 32, 128), BF16),
        scratch_shapes=[pltpu.VMEM((4, 256, 128), F32)],
        compiler_params=params(32),
        cost_estimate=cost(0, slots * BS * BS * 6),
        name="pack",
    )(masters)


def run_expert(member, tables, copies, arrived, router_row):
    inverse, rows, lanes, valid = tables
    peers = arrived.shape[0]
    count = 8 * peers
    whole = pl.BlockSpec(memory_space=pltpu.VMEM)
    scalar = pl.BlockSpec(memory_space=pltpu.SMEM)
    return pl.pallas_call(
        functools.partial(expert_kernel, base=0),
        in_specs=[scalar] * 4 + [whole] * 3,
        out_specs=[whole] * 3,
        out_shape=[
            jax.ShapeDtypeStruct((peers, 16, D), BF16),
            jax.ShapeDtypeStruct((3 * MAXB, 32, 128), BF16),
            jax.ShapeDtypeStruct((1, D), F32),
        ],
        scratch_shapes=[
            pltpu.VMEM((D, 2 * FF), BF16),
            pltpu.VMEM((FF, D), BF16),
            pltpu.VMEM((count, D), BF16),
            pltpu.VMEM((count, D), BF16),
            pltpu.VMEM((count, 2 * FF), F32),
            pltpu.VMEM((count, D), BF16),
            pltpu.VMEM((count, 2 * FF), BF16),
            pltpu.VMEM((D, 2 * FF), BF16),
            pltpu.VMEM((FF, D), BF16),
        ],
        compiler_params=params(56),
        cost_estimate=cost(9 * 2 * count * D * FF * 2, 60 << 20),
        name="expert_%d" % member,
    )(inverse[member], rows[member], lanes[member], valid[member], copies, arrived, router_row)


def update(summed, masters):
    slots = masters.shape[0]
    return pl.pallas_call(
        update_kernel,
        grid=(slots // 32,),
        in_specs=[
            pl.BlockSpec((32, 32, 128), lambda n: (n, 0, 0)),
            pl.BlockSpec((32, BS * BS), lambda n: (n, 0)),
        ],
        out_specs=[
            pl.BlockSpec((32, BS * BS), lambda n: (n, 0)),
            pl.BlockSpec((32, 1), lambda n: (n, 0)),
        ],
        out_shape=[
            jax.ShapeDtypeStruct((slots, BS * BS), F32),
            jax.ShapeDtypeStruct((slots, 1), F32),
        ],
        scratch_shapes=[pltpu.VMEM((4, 256, 128), F32)],
        compiler_params=params(32),
        cost_estimate=cost(4 * slots * BS * BS, slots * BS * BS * 10),
        name="update",
    )(summed, masters)


def combine(picks, back, count):
    locals_count = len(back)
    peers, _, width = back[0].shape
    rows = 16 * peers
    column = pl.BlockSpec((count, CHUNK), lambda n: (0, n))
    return pl.pallas_call(
        functools.partial(combine_kernel, locals_count=locals_count),
        grid=(width // CHUNK,),
        in_specs=[pl.BlockSpec(picks.shape, lambda n: (0, 0))]
        + [pl.BlockSpec((peers, 16, CHUNK), lambda n: (0, 0, n))] * locals_count,
        out_specs=[column, column],
        out_shape=[jax.ShapeDtypeStruct((count, width), BF16)] * 2,
        scratch_shapes=[pltpu.VMEM((2, locals_count, rows, count), BF16)],
        compiler_params=params(32),
        cost_estimate=cost(4 * rows * count * width * locals_count, 6 << 20),
        name="combine",
    )(picks, *back)


def slot_tables(kept, owners):
    numbers = jnp.arange(BLOCKS, dtype=jnp.int32)
    slots = jnp.arange(MAXB, dtype=jnp.int32)
    per = MAXB // owners
    matrix = jnp.arange(3, dtype=jnp.int32)[None, :, None]
    place = (slots // per) * (3 * per) + slots % per + matrix * per
    hits = kept[:, :, None, :] == numbers[None, None, :, None]
    inverse = jnp.sum(jnp.where(hits, place[:, :, None, :] + 1, 0), axis=-1) - 1
    valid = kept < BLOCKS
    block = jnp.where(valid, kept, 0)
    width = jnp.array([FF // BS, FF // BS, D // BS], jnp.int32)[None, :, None]
    block_row, block_col = block // width, block % width
    rows = block_row * BS + 32 * (block_col & 1)
    lanes = (block_col >> 1) * 128 + jnp.where(matrix == 1, FF, 0)
    flat = lambda table: table.reshape(table.shape[0], -1).astype(jnp.int32)
    return flat(inverse), flat(rows), flat(lanes), flat(valid)


def body(tokens, out_grad, token_picks, router, kept_blocks, masters, scores):
    locals_count = kept_blocks.shape[0]
    owners = lax.axis_size("dp")
    peers = lax.axis_size("expert")
    count, width = tokens.shape
    per = masters.shape[2]
    picks = token_picks[0]
    flat_masters = masters.reshape(locals_count * 3 * per, BS * BS)

    packed = pack(flat_masters)
    sent = pick(picks, tokens, out_grad, locals_count, peers)
    tables = slot_tables(kept_blocks, owners)
    router_rows = router.T.reshape(locals_count, width // BS, 32, 2).transpose(0, 1, 3, 2)
    router_rows = router_rows.reshape(locals_count, 1, width).astype(F32)

    copies, arrived = [], []
    for member in range(locals_count):
        mine = packed[member * 3 * per : (member + 1) * 3 * per]
        copies.append(lax.all_gather(mine, "dp", axis=0, tiled=True))
        arrived.append(lax.all_to_all(sent[member], "expert", split_axis=0, concat_axis=0, tiled=True))
    summed, back, router_parts = [], [], []
    for member in range(locals_count):
        send, gradient, router_part = run_expert(
            member, tables, copies[member], arrived[member], router_rows[member]
        )
        summed.append(lax.psum_scatter(gradient, "dp", scatter_dimension=0, tiled=True))
        back.append(lax.all_to_all(send, "expert", split_axis=0, concat_axis=0, tiled=True))
        router_parts.append(router_part)
    router_sum = jnp.stack(router_parts, axis=1).reshape(locals_count, owners, width // owners)
    router_sum = lax.psum_scatter(router_sum.transpose(1, 0, 2), "dp", scatter_dimension=0, tiled=True)
    router_new = router_sum.reshape(locals_count, width // owners // BS, 2, 32)
    router_new = router_new.transpose(1, 3, 2, 0).reshape(width // owners, locals_count)

    new_list, total_list = [], []
    for member in range(locals_count):
        mine = flat_masters[member * 3 * per : (member + 1) * 3 * per]
        new, total = update(summed[member], mine)
        new_list.append(new)
        total_list.append(total)
    layer_out, input_grad = combine(picks, back, count)
    master_new = jnp.stack(new_list).reshape(masters.shape)
    score_new = scores - SCORE_RATE * jnp.stack(total_list).reshape(scores.shape)
    return layer_out, input_grad, master_new, score_new, router_new


def solution(mesh):
    return jax.shard_map(
        body,
        mesh=mesh,
        in_specs=(
            P(("dp", "expert"), None),
            P(("dp", "expert"), None),
            P(("dp", "expert"), None, None),
            P(None, "expert"),
            P("expert", None, None),
            P("expert", None, "dp", None),
            P("expert", None, "dp"),
        ),
        out_specs=(
            P(("dp", "expert"), None),
            P(("dp", "expert"), None),
            P("expert", None, "dp", None),
            P("expert", None, "dp"),
            P("dp", "expert"),
        ),
        check_vma=False,
    )
```

```python
import functools

import jax
import jax.numpy as jnp
from jax import lax
from jax.experimental import pallas as pl
from jax.experimental.pallas import tpu as pltpu
from jax.sharding import PartitionSpec as P

D = 2048
FF = 768
BS = 64
MAXB = 128
OWNERS = 4
BLOCKS = (D // BS) * (FF // BS)
LEARN_RATE = 0.005
SCORE_RATE = 0.05
CHUNK = 256
F32 = jnp.float32
BF16 = jnp.bfloat16
NN = (((1,), (0,)), ((), ()))
NT = (((1,), (1,)), ((), ()))
TN = (((0,), (0,)), ((), ()))


def dot(left, right, dims=NN):
    return lax.dot_general(left, right, dims, preferred_element_type=F32)


def iota(shape, dim):
    return lax.broadcasted_iota(jnp.int32, shape, dim)


def one_hot(flag):
    return jnp.where(flag, 1.0, 0.0).astype(BF16)


def split_matrix(size):
    col = iota((size, size), 1)
    source = ((col >> 6) << 6) + 2 * (col & 31) + ((col >> 5) & 1)
    return one_hot(iota((size, size), 0) == source)


def pick_columns(picks_ref, member, locals_count):
    experts = picks_ref.shape[0]
    rows = 8 * experts // locals_count
    expert = (iota((rows, experts), 0) >> 3) * locals_count + member
    spread = one_hot(iota((rows, experts), 1) == expert)
    wide = dot(spread, picks_ref[...].astype(F32).astype(BF16))
    keep = iota(wide.shape, 1) == (iota(wide.shape, 0) & 7)
    return jnp.sum(jnp.where(keep, wide, 0.0), axis=1, keepdims=True).astype(jnp.int32)


def interleave(first, second):
    width = first.shape[1]
    pair = [first.reshape(-1, 8, width), second.reshape(-1, 8, width)]
    return jnp.concatenate(pair, axis=1).astype(BF16)


def apart(block):
    wide = block.astype(F32)
    width = wide.shape[2]
    return wide[:, :8, :].reshape(-1, width), wide[:, 8:, :].reshape(-1, width)


def pick_kernel(picks_ref, tokens_ref, grads_ref, *rest, locals_count):
    out_refs, hot_ref = rest[:locals_count], rest[locals_count]

    @pl.when(pl.program_id(0) == 0)
    def _():
        for member in range(locals_count):
            index = pick_columns(picks_ref, member, locals_count)
            hot_ref[member] = one_hot(iota(hot_ref.shape[1:], 1) == index)

    tokens = dot(tokens_ref[...], split_matrix(CHUNK)).astype(BF16)
    for member in range(locals_count):
        hot = hot_ref[member]
        out_refs[member][...] = interleave(dot(hot, tokens), dot(hot, grads_ref[...]))


def pack_kernel(masters_ref, first_ref, second_ref, lines_ref):
    def fill(out_ref):
        for group in range(masters_ref.shape[0] // 8):
            for k in range(32):
                lines_ref[group, 8 * k : 8 * k + 8, :] = masters_ref[
                    8 * group : 8 * group + 8, 128 * k : 128 * k + 128
                ]
            for s in range(8):
                out_ref[8 * group + s] = lines_ref[group, pl.ds(s, 32, stride=8), :].astype(BF16)

    step, steps = pl.program_id(0), pl.num_programs(0)

    @pl.when(step < steps // 2)
    def _():
        fill(first_ref)

    @pl.when(step >= steps // 2)
    def _():
        fill(second_ref)


def expert_kernel(
    inverse_ref, row_ref, lane_ref, valid_ref,
    copies_ref, arrived_ref, router_ref,
    send_ref, packed_ref,
    wide_ref, down_ref, rows_ref, grads_ref, pre_ref, part_ref, both_ref,
    grad_wide_ref, grad_down_ref, router_out_ref,
    *, member,
):
    base, slot_base = member * 3 * BLOCKS, member * 3 * MAXB
    lane = iota((32, 128), 1)
    half = lane < 64

    def place(target_ref, matrix, block, row, col):
        first = inverse_ref[base + matrix * BLOCKS + block]
        second = inverse_ref[base + matrix * BLOCKS + block + 1]
        one = copies_ref[jnp.maximum(first, 0)]
        two = copies_ref[jnp.maximum(second, 0)]
        one = jnp.where(lane < jnp.where(first >= 0, 128, 0), one, jnp.zeros_like(one))
        two = jnp.where(lane < jnp.where(second >= 0, 128, 0), two, jnp.zeros_like(two))
        target_ref[pl.ds(row, 32), col : col + 128] = jnp.where(half, one, pltpu.roll(two, 64, 1))
        target_ref[pl.ds(row + 32, 32), col : col + 128] = jnp.where(half, pltpu.roll(one, 64, 1), two)

    @pl.loop(0, D // BS)
    def _(r):
        row = pl.multiple_of(r * BS, BS)
        for matrix in range(2):
            for pair in range(FF // BS // 2):
                place(wide_ref, matrix, r * (FF // BS) + 2 * pair, row, matrix * FF + 128 * pair)

    @pl.loop(0, FF // BS)
    def _(r):
        row = pl.multiple_of(r * BS, BS)
        for pair in range(D // BS // 2):
            place(down_ref, 2, r * (D // BS) + 2 * pair, row, 128 * pair)

    count = rows_ref.shape[0]
    chunks = D // CHUNK
    mine = slice(member, member + 1)

    def take(n, logit):
        cols = pl.ds(pl.multiple_of(n * CHUNK, CHUNK), CHUNK)
        rows, grads = apart(arrived_ref[:, :, cols])
        rows_ref[:, cols] = rows.astype(BF16)
        grads_ref[:, cols] = grads.astype(BF16)
        return logit + jnp.sum(rows * router_ref[mine, cols], axis=1, keepdims=True)

    logit = lax.fori_loop(0, chunks, take, jnp.zeros((count, 1), F32))
    gating = 1.0 / (1.0 + jnp.exp(-logit))

    @pl.loop(0, 2 * FF // 512)
    def _(n):
        cols = pl.ds(pl.multiple_of(n * 512, 512), 512)
        pre_ref[:, cols] = dot(rows_ref[...], wide_ref[:, cols])

    split = split_matrix(CHUNK)
    hidden_list = []
    for n in range(FF // CHUNK):
        gate_pre = pre_ref[:, n * CHUNK : (n + 1) * CHUNK]
        up_pre = pre_ref[:, FF + n * CHUNK : FF + (n + 1) * CHUNK]
        hidden = (gate_pre / (1.0 + jnp.exp(-gate_pre)) * up_pre).astype(BF16)
        hidden_list.append(dot(hidden, split).astype(BF16))
    hidden_split = jnp.concatenate(hidden_list, axis=1)

    @pl.loop(0, D // 512)
    def _(n):
        cols = pl.ds(pl.multiple_of(n * 512, 512), 512)
        part_ref[:, cols] = (gating * dot(hidden_split, down_ref[:, cols])).astype(BF16)
        grads_ref[:, cols] = (gating * grads_ref[:, cols].astype(F32)).astype(BF16)

    logit_sum = jnp.zeros((count, 1), F32)
    for n in range(FF // CHUNK):
        spread = dot(grads_ref[...], down_ref[n * CHUNK : (n + 1) * CHUNK, :], NT)
        high = spread.astype(BF16)
        low = (spread - high.astype(F32)).astype(BF16)
        hidden_grad = dot(high, split, NT) + dot(low, split, NT)
        logit_sum = logit_sum + jnp.sum(
            hidden_list[n].astype(F32) * spread, axis=1, keepdims=True
        )
        gate_pre = pre_ref[:, n * CHUNK : (n + 1) * CHUNK]
        up_pre = pre_ref[:, FF + n * CHUNK : FF + (n + 1) * CHUNK]
        sigma = 1.0 / (1.0 + jnp.exp(-gate_pre))
        gate_grad = hidden_grad * up_pre * sigma * (1.0 + gate_pre * (1.0 - sigma))
        both_ref[:, n * CHUNK : (n + 1) * CHUNK] = gate_grad.astype(BF16)
        both_ref[:, FF + n * CHUNK : FF + (n + 1) * CHUNK] = (hidden_grad * gate_pre * sigma).astype(BF16)
        grad_down_ref[n * CHUNK : (n + 1) * CHUNK, :] = dot(hidden_list[n], grads_ref[...], TN).astype(BF16)
    logit_grad = logit_sum * (1.0 - gating)

    @pl.loop(0, chunks)
    def _(n):
        cols = pl.ds(pl.multiple_of(n * CHUNK, CHUNK), CHUNK)
        part = dot(both_ref[...], wide_ref[cols, :], NT) + logit_grad * router_ref[mine, cols]
        send_ref[:, :, cols] = interleave(part_ref[:, cols].astype(F32), part)
        rows = rows_ref[:, cols]
        router_out_ref[:, cols] = jnp.sum(logit_grad * rows.astype(F32), axis=0, keepdims=True)
        grad_wide_ref[cols, :] = dot(rows, both_ref[...], TN).astype(BF16)

    def cut(source_ref, matrix, slot, place_in):
        at = slot_base + matrix * MAXB + slot
        row = pl.multiple_of(row_ref[at], 32)
        other = pl.multiple_of(row ^ 32, 32)
        cols = pl.ds(pl.multiple_of(lane_ref[at], 128), 128)
        odd = row & 32
        stay = source_ref[pl.ds(row, 32), cols]
        move = pltpu.roll(source_ref[pl.ds(other, 32), cols], 64, 1)
        tile = jnp.where((lane & 64) == 2 * odd, stay, move)
        limit = jnp.where(valid_ref[at] > 0, 128, 0)
        packed_ref[place_in] = jnp.where(lane < limit, tile, jnp.zeros_like(tile))

    per = MAXB // OWNERS
    part = packed_ref.shape[0] // OWNERS
    for owner in range(OWNERS):
        for matrix in range(3):
            source_ref = grad_down_ref if matrix == 2 else grad_wide_ref

            @pl.loop(0, per // 4)
            def _(group, owner=owner, matrix=matrix, source_ref=source_ref):
                for step in range(4):
                    s = group * 4 + step
                    cut(source_ref, matrix, owner * per + s, owner * part + matrix * per + s)

        start = owner * (D // OWNERS)
        lines = [router_out_ref[:, start + at : start + at + 128] for at in range(0, D // OWNERS, 128)]
        lines.append(jnp.zeros((32 - len(lines), 128), F32))
        packed_ref[owner * part + 3 * per] = jnp.concatenate(lines, axis=0).astype(BF16)


def update_kernel(summed_ref, masters_ref, *rest):
    out_ref, total_ref, lines_ref = rest[-3:]
    for group in range(masters_ref.shape[0] // 8):
        for s in range(8):
            lines_ref[group, pl.ds(s, 32, stride=8), :] = summed_ref[8 * group + s].astype(F32)
        total = jnp.zeros((8, 128), F32)
        rows = slice(8 * group, 8 * group + 8)
        for k in range(32):
            cols = slice(128 * k, 128 * k + 128)
            gradient = lines_ref[group, 8 * k : 8 * k + 8, :]
            held = masters_ref[rows, cols]
            out_ref[rows, cols] = held - LEARN_RATE * gradient
            total = total + held * gradient
        total_ref[rows, :] = jnp.sum(total, axis=1, keepdims=True)


def combine_kernel(picks_ref, *rest, locals_count):
    back_refs = rest[:locals_count]
    out_ref, in_ref, hot_ref = rest[locals_count:]
    count = out_ref.shape[0]

    @pl.when(pl.program_id(0) == 0)
    def _():
        same = one_hot(iota((count, count), 0) == iota((count, count), 1))
        for member in range(locals_count):
            index = pick_columns(picks_ref, member, locals_count)
            hot = one_hot(iota((index.shape[0], count), 1) == index)
            hot_ref[member] = dot(hot, same, TN).astype(BF16)

    out_sum = jnp.zeros(out_ref.shape, F32)
    in_sum = jnp.zeros(in_ref.shape, F32)
    for member in range(locals_count):
        out_rows, in_rows = apart(back_refs[member][...])
        out_sum = out_sum + dot(hot_ref[member], out_rows.astype(BF16))
        in_sum = in_sum + dot(hot_ref[member], in_rows.astype(BF16))
    out_ref[...] = out_sum.astype(BF16)
    in_ref[...] = dot(in_sum.astype(BF16), split_matrix(CHUNK), NT).astype(BF16)


def params(mib):
    return pltpu.CompilerParams(vmem_limit_bytes=mib * 1024 * 1024)


def cost(flops, moved):
    return pl.CostEstimate(flops=flops, bytes_accessed=moved, transcendentals=0)


def pick(picks, tokens, grads, locals_count, peers):
    count, width = tokens.shape
    column = pl.BlockSpec((count, CHUNK), lambda n: (0, n))
    return pl.pallas_call(
        functools.partial(pick_kernel, locals_count=locals_count),
        grid=(width // CHUNK,),
        in_specs=[pl.BlockSpec(picks.shape, lambda n: (0, 0)), column, column],
        out_specs=[pl.BlockSpec((peers, 16, CHUNK), lambda n: (0, 0, n))] * locals_count,
        out_shape=[jax.ShapeDtypeStruct((peers, 16, width), BF16)] * locals_count,
        scratch_shapes=[pltpu.VMEM((locals_count, 8 * peers, count), BF16)],
        compiler_params=params(56),
        cost_estimate=cost(0, 1 << 20),
        name="pick",
    )(picks, tokens, grads)


def pack(masters):
    half = masters.shape[0] // 2
    steps = 4
    rows = 2 * half // steps
    return pl.pallas_call(
        pack_kernel,
        grid=(steps,),
        in_specs=[pl.BlockSpec((rows, BS * BS), lambda n: (n, 0))],
        out_specs=[
            pl.BlockSpec((rows, 32, 128), lambda n: (jnp.minimum(n, steps // 2 - 1), 0, 0)),
            pl.BlockSpec((rows, 32, 128), lambda n: (jnp.maximum(n - steps // 2, 0), 0, 0)),
        ],
        out_shape=[jax.ShapeDtypeStruct((half, 32, 128), BF16)] * 2,
        scratch_shapes=[pltpu.VMEM((rows // 8, 256, 128), F32)],
        compiler_params=params(56),
        cost_estimate=cost(0, 1 << 20),
        name="pack",
    )(masters)


def run_expert(member, tables, copies, arrived, router_rows):
    peers = arrived.shape[0]
    count = 8 * peers
    whole = pl.BlockSpec(memory_space=pltpu.VMEM)
    scalar = pl.BlockSpec(memory_space=pltpu.SMEM)
    return pl.pallas_call(
        functools.partial(expert_kernel, member=member),
        in_specs=[scalar] * 4 + [whole] * 3,
        out_specs=[whole] * 2,
        out_shape=[
            jax.ShapeDtypeStruct((peers, 16, D), BF16),
            jax.ShapeDtypeStruct((3 * MAXB + OWNERS, 32, 128), BF16),
        ],
        scratch_shapes=[
            pltpu.VMEM((D, 2 * FF), BF16),
            pltpu.VMEM((FF, D), BF16),
            pltpu.VMEM((count, D), BF16),
            pltpu.VMEM((count, D), BF16),
            pltpu.VMEM((count, 2 * FF), F32),
            pltpu.VMEM((count, D), BF16),
            pltpu.VMEM((count, 2 * FF), BF16),
            pltpu.VMEM((D, 2 * FF), BF16),
            pltpu.VMEM((FF, D), BF16),
            pltpu.VMEM((1, D), F32),
        ],
        compiler_params=params(56),
        cost_estimate=cost(150 * 10**9, 1 << 20),
        name="expert_%d" % member,
    )(*tables, copies, arrived, router_rows)


def update(member, summed, masters, held):
    slots = masters.shape[0]
    mine = summed.shape[0] - 1
    steps = 3
    rows = mine // steps
    return pl.pallas_call(
        update_kernel,
        grid=(steps,),
        in_specs=[
            pl.BlockSpec((rows, 32, 128), lambda n: (n, 0, 0)),
            pl.BlockSpec((rows, BS * BS), lambda n: (member * steps + n, 0)),
        ]
        + [pl.BlockSpec(memory_space=pl.ANY)] * len(held),
        out_specs=[
            pl.BlockSpec((rows, BS * BS), lambda n: (member * steps + n, 0)),
            pl.BlockSpec((rows, 1), lambda n: (member * steps + n, 0)),
        ],
        out_shape=[
            jax.ShapeDtypeStruct((slots, BS * BS), F32),
            jax.ShapeDtypeStruct((slots, 1), F32),
        ],
        input_output_aliases={2 + at: at for at in range(len(held))},
        scratch_shapes=[pltpu.VMEM((rows // 8, 256, 128), F32)],
        compiler_params=params(56),
        cost_estimate=cost(0, 1 << 20),
        name="update_%d" % member,
    )(summed, masters, *held)


def combine(picks, back, count):
    locals_count = len(back)
    peers, _, width = back[0].shape
    column = pl.BlockSpec((count, CHUNK), lambda n: (0, n))
    return pl.pallas_call(
        functools.partial(combine_kernel, locals_count=locals_count),
        grid=(width // CHUNK,),
        in_specs=[pl.BlockSpec(picks.shape, lambda n: (0, 0))]
        + [pl.BlockSpec((peers, 16, CHUNK), lambda n: (0, 0, n))] * locals_count,
        out_specs=[column, column],
        out_shape=[jax.ShapeDtypeStruct((count, width), BF16)] * 2,
        scratch_shapes=[pltpu.VMEM((locals_count, count, 8 * peers), BF16)],
        compiler_params=params(56),
        cost_estimate=cost(150 * 10**9, 1 << 20),
        name="combine",
    )(picks, *back)


def slot_tables(kept, owners):
    numbers = jnp.arange(BLOCKS, dtype=jnp.int32)
    slots = jnp.arange(MAXB, dtype=jnp.int32)
    per = MAXB // owners
    matrix = jnp.arange(3, dtype=jnp.int32)[None, :, None]
    place = (slots // per) * (3 * per) + slots % per + matrix * per
    hits = kept[:, :, None, :] == numbers[None, None, :, None]
    inverse = jnp.sum(jnp.where(hits, place[:, :, None, :] + 1, 0), axis=-1) - 1
    valid = kept < BLOCKS
    block = jnp.where(valid, kept, 0)
    width = jnp.array([FF // BS, FF // BS, D // BS], jnp.int32)[None, :, None]
    block_row, block_col = block // width, block % width
    rows = block_row * BS + 32 * (block_col & 1)
    lanes = (block_col >> 1) * 128 + jnp.where(matrix == 1, FF, 0)
    flat = lambda table: table.reshape(-1).astype(jnp.int32)
    return flat(inverse), flat(rows), flat(lanes), flat(valid)


def body(tokens, out_grad, token_picks, router, kept_blocks, masters, scores):
    locals_count = kept_blocks.shape[0]
    owners = lax.axis_size("dp")
    peers = lax.axis_size("expert")
    count, width = tokens.shape
    per = masters.shape[2]
    picks = token_picks[0]
    flat_masters = masters.reshape(locals_count * 3 * per, BS * BS)

    packed = pack(flat_masters)
    sent = pick(picks, tokens, out_grad, locals_count, peers)
    tables = slot_tables(kept_blocks, owners)
    router_rows = router.T.reshape(locals_count, width // BS, 32, 2).transpose(0, 1, 3, 2)
    router_rows = router_rows.reshape(locals_count, width).astype(F32)
    tables, router_rows, sent = lax.optimization_barrier((tables, router_rows, sent))

    copies, arrived = [], []
    for member in range(locals_count):
        copies.append(lax.all_gather(packed[member], "dp", axis=0, tiled=True))
        arrived.append(lax.all_to_all(sent[member], "expert", split_axis=0, concat_axis=0, tiled=True))
    summed, back = [], []
    for member in range(locals_count):
        send, gradient = run_expert(member, tables, copies[member], arrived[member], router_rows)
        summed.append(lax.psum_scatter(gradient, "dp", scatter_dimension=0, tiled=True))
        back.append(lax.all_to_all(send, "expert", split_axis=0, concat_axis=0, tiled=True))
    held = ()
    for member in range(locals_count):
        held = update(member, summed[member], flat_masters, held)
    layer_out, input_grad = combine(picks, back, count)
    master_new = held[0].reshape(masters.shape)
    score_new = scores - SCORE_RATE * held[1].reshape(scores.shape)
    router_new = jnp.stack([part[-1, : width // owners // 128] for part in summed])
    router_new = router_new.reshape(locals_count, width // owners // BS, 2, 32).astype(F32)
    router_new = router_new.transpose(1, 3, 2, 0).reshape(width // owners, locals_count)
    return layer_out, input_grad, master_new, score_new, router_new


def solution(mesh):
    return jax.shard_map(
        body,
        mesh=mesh,
        in_specs=(
            P(("dp", "expert"), None),
            P(("dp", "expert"), None),
            P(("dp", "expert"), None, None),
            P(None, "expert"),
            P("expert", None, None),
            P("expert", None, "dp", None),
            P("expert", None, "dp"),
        ),
        out_specs=(
            P(("dp", "expert"), None),
            P(("dp", "expert"), None),
            P("expert", None, "dp", None),
            P("expert", None, "dp"),
            P("dp", "expert"),
        ),
        check_vma=False,
    )
```

```python
import functools

import jax
import jax.numpy as jnp
from jax import lax
from jax.experimental import pallas as pl
from jax.experimental.pallas import tpu as pltpu
from jax.sharding import PartitionSpec as P

D = 2048
FF = 768
BS = 64
MAXB = 128
OWNERS = 4
BLOCKS = (D // BS) * (FF // BS)
LEARN_RATE = 0.005
SCORE_RATE = 0.05
CHUNK = 256
STEP = 512
F32 = jnp.float32
BF16 = jnp.bfloat16
NN = (((1,), (0,)), ((), ()))
NT = (((1,), (1,)), ((), ()))
TN = (((0,), (0,)), ((), ()))


def dot(left, right, dims=NN):
    return lax.dot_general(left, right, dims, preferred_element_type=F32)


def iota(shape, dim):
    return lax.broadcasted_iota(jnp.int32, shape, dim)


def one_hot(flag):
    return jnp.where(flag, 1.0, 0.0).astype(BF16)


def split_matrix(size):
    col = iota((size, size), 1)
    source = ((col >> 6) << 6) + 2 * (col & 31) + ((col >> 5) & 1)
    return one_hot(iota((size, size), 0) == source)


def pick_columns(picks_ref, member, locals_count):
    experts = picks_ref.shape[0]
    rows = 8 * experts // locals_count
    expert = (iota((rows, experts), 0) >> 3) * locals_count + member
    spread = one_hot(iota((rows, experts), 1) == expert)
    wide = dot(spread, picks_ref[...].astype(F32).astype(BF16))
    keep = iota(wide.shape, 1) == (iota(wide.shape, 0) & 7)
    return jnp.sum(jnp.where(keep, wide, 0.0), axis=1, keepdims=True).astype(jnp.int32)


def interleave(first, second):
    width = first.shape[1]
    pair = [first.reshape(-1, 8, width), second.reshape(-1, 8, width)]
    return jnp.concatenate(pair, axis=1).astype(BF16)


def apart(block):
    wide = block.astype(F32)
    width = wide.shape[2]
    return wide[:, :8, :].reshape(-1, width), wide[:, 8:, :].reshape(-1, width)


def pick_kernel(picks_ref, tokens_ref, grads_ref, *rest, locals_count):
    out_refs, hot_ref = rest[:locals_count], rest[locals_count]
    rows = hot_ref.shape[0] // locals_count

    @pl.when(pl.program_id(0) == 0)
    def _():
        for member in range(locals_count):
            index = pick_columns(picks_ref, member, locals_count)
            hot_ref[member * rows : (member + 1) * rows, :] = one_hot(
                iota((rows, hot_ref.shape[1]), 1) == index
            )

    split = split_matrix(CHUNK)
    for start in range(0, tokens_ref.shape[1], CHUNK):
        cols = slice(start, start + CHUNK)
        tokens = dot(hot_ref[...], dot(tokens_ref[:, cols], split).astype(BF16))
        grads = dot(hot_ref[...], grads_ref[:, cols])
        for member in range(locals_count):
            mine = slice(member * rows, (member + 1) * rows)
            out_refs[member][:, :, cols] = interleave(tokens[mine], grads[mine])


def pack_kernel(masters_ref, out_ref, lines_ref):
    for group in range(masters_ref.shape[0] // 8):
        for k in range(32):
            lines_ref[group, 8 * k : 8 * k + 8, :] = masters_ref[
                8 * group : 8 * group + 8, 128 * k : 128 * k + 128
            ]
        for s in range(8):
            out_ref[8 * group + s] = lines_ref[group, pl.ds(s, 32, stride=8), :].astype(BF16)


def expert_kernel(
    inverse_ref, row_ref, lane_ref, valid_ref,
    copies_ref, arrived_ref, router_ref,
    send_ref, packed_ref,
    wide_ref, down_ref, rows_ref, grads_ref, pre_ref, part_ref, both_ref,
    grad_wide_ref, grad_down_ref, router_out_ref,
    *, member,
):
    base, slot_base = member * 3 * BLOCKS, member * 3 * MAXB
    lane = iota((32, 128), 1)
    half = lane < 64

    def place(target_ref, matrix, block, row, col):
        first = inverse_ref[base + matrix * BLOCKS + block]
        second = inverse_ref[base + matrix * BLOCKS + block + 1]
        one = copies_ref[jnp.maximum(first, 0)]
        two = copies_ref[jnp.maximum(second, 0)]
        one = jnp.where(lane < jnp.where(first >= 0, 128, 0), one, jnp.zeros_like(one))
        two = jnp.where(lane < jnp.where(second >= 0, 128, 0), two, jnp.zeros_like(two))
        target_ref[pl.ds(row, 32), col : col + 128] = jnp.where(half, one, pltpu.roll(two, 64, 1))
        target_ref[pl.ds(row + 32, 32), col : col + 128] = jnp.where(half, pltpu.roll(one, 64, 1), two)

    @pl.loop(0, D // BS)
    def _(r):
        row = pl.multiple_of(r * BS, BS)
        for matrix in range(2):
            for pair in range(FF // BS // 2):
                place(wide_ref, matrix, r * (FF // BS) + 2 * pair, row, matrix * FF + 128 * pair)

    @pl.loop(0, FF // BS)
    def _(r):
        row = pl.multiple_of(r * BS, BS)
        for pair in range(D // BS // 2):
            place(down_ref, 2, r * (D // BS) + 2 * pair, row, 128 * pair)

    count = rows_ref.shape[0]
    chunks = D // CHUNK
    mine = slice(member, member + 1)

    def take(n, logit):
        cols = pl.ds(pl.multiple_of(n * CHUNK, CHUNK), CHUNK)
        rows, grads = apart(arrived_ref[:, :, cols])
        rows_ref[:, cols] = rows.astype(BF16)
        grads_ref[:, cols] = grads.astype(BF16)
        return logit + jnp.sum(rows * router_ref[mine, cols], axis=1, keepdims=True)

    logit = lax.fori_loop(0, chunks, take, jnp.zeros((count, 1), F32))
    gating = 1.0 / (1.0 + jnp.exp(-logit))

    @pl.loop(0, 2 * FF // 512)
    def _(n):
        cols = pl.ds(pl.multiple_of(n * 512, 512), 512)
        pre_ref[:, cols] = dot(rows_ref[...], wide_ref[:, cols])

    split = split_matrix(CHUNK)
    hidden_list = []
    for n in range(FF // CHUNK):
        gate_pre = pre_ref[:, n * CHUNK : (n + 1) * CHUNK]
        up_pre = pre_ref[:, FF + n * CHUNK : FF + (n + 1) * CHUNK]
        hidden = (gate_pre / (1.0 + jnp.exp(-gate_pre)) * up_pre).astype(BF16)
        hidden_list.append(dot(hidden, split).astype(BF16))
    hidden_split = jnp.concatenate(hidden_list, axis=1)

    @pl.loop(0, D // 512)
    def _(n):
        cols = pl.ds(pl.multiple_of(n * 512, 512), 512)
        part_ref[:, cols] = (gating * dot(hidden_split, down_ref[:, cols])).astype(BF16)
        grads_ref[:, cols] = (gating * grads_ref[:, cols].astype(F32)).astype(BF16)

    logit_sum = jnp.zeros((count, 1), F32)
    for n in range(FF // CHUNK):
        spread = dot(grads_ref[...], down_ref[n * CHUNK : (n + 1) * CHUNK, :], NT)
        high = spread.astype(BF16)
        low = (spread - high.astype(F32)).astype(BF16)
        hidden_grad = dot(high, split, NT) + dot(low, split, NT)
        logit_sum = logit_sum + jnp.sum(
            hidden_list[n].astype(F32) * spread, axis=1, keepdims=True
        )
        gate_pre = pre_ref[:, n * CHUNK : (n + 1) * CHUNK]
        up_pre = pre_ref[:, FF + n * CHUNK : FF + (n + 1) * CHUNK]
        sigma = 1.0 / (1.0 + jnp.exp(-gate_pre))
        gate_grad = hidden_grad * up_pre * sigma * (1.0 + gate_pre * (1.0 - sigma))
        both_ref[:, n * CHUNK : (n + 1) * CHUNK] = gate_grad.astype(BF16)
        both_ref[:, FF + n * CHUNK : FF + (n + 1) * CHUNK] = (hidden_grad * gate_pre * sigma).astype(BF16)
        grad_down_ref[n * CHUNK : (n + 1) * CHUNK, :] = dot(hidden_list[n], grads_ref[...], TN).astype(BF16)
    logit_grad = logit_sum * (1.0 - gating)

    @pl.loop(0, chunks)
    def _(n):
        cols = pl.ds(pl.multiple_of(n * CHUNK, CHUNK), CHUNK)
        part = dot(both_ref[...], wide_ref[cols, :], NT) + logit_grad * router_ref[mine, cols]
        send_ref[:, :, cols] = interleave(part_ref[:, cols].astype(F32), part)
        rows = rows_ref[:, cols]
        router_out_ref[:, cols] = jnp.sum(logit_grad * rows.astype(F32), axis=0, keepdims=True)
        grad_wide_ref[cols, :] = dot(rows, both_ref[...], TN).astype(BF16)

    def cut(source_ref, matrix, slot, place_in):
        at = slot_base + matrix * MAXB + slot
        row = pl.multiple_of(row_ref[at], 32)
        other = pl.multiple_of(row ^ 32, 32)
        cols = pl.ds(pl.multiple_of(lane_ref[at], 128), 128)
        odd = row & 32
        stay = source_ref[pl.ds(row, 32), cols]
        move = pltpu.roll(source_ref[pl.ds(other, 32), cols], 64, 1)
        tile = jnp.where((lane & 64) == 2 * odd, stay, move)
        limit = jnp.where(valid_ref[at] > 0, 128, 0)
        packed_ref[place_in] = jnp.where(lane < limit, tile, jnp.zeros_like(tile))

    per = MAXB // OWNERS
    part = packed_ref.shape[0] // OWNERS
    for owner in range(OWNERS):
        for matrix in range(3):
            source_ref = grad_down_ref if matrix == 2 else grad_wide_ref

            @pl.loop(0, per // 4)
            def _(group, owner=owner, matrix=matrix, source_ref=source_ref):
                for step in range(4):
                    s = group * 4 + step
                    cut(source_ref, matrix, owner * per + s, owner * part + matrix * per + s)

        start = owner * (D // OWNERS)
        lines = [router_out_ref[:, start + at : start + at + 128] for at in range(0, D // OWNERS, 128)]
        lines.append(jnp.zeros((32 - len(lines), 128), F32))
        packed_ref[owner * part + 3 * per] = jnp.concatenate(lines, axis=0).astype(BF16)


def update_kernel(summed_ref, masters_ref, *rest):
    out_ref, total_ref, lines_ref = rest[-3:]
    for group in range(masters_ref.shape[0] // 8):
        for s in range(8):
            lines_ref[group, pl.ds(s, 32, stride=8), :] = summed_ref[8 * group + s].astype(F32)
        total = jnp.zeros((8, 128), F32)
        rows = slice(8 * group, 8 * group + 8)
        for k in range(32):
            cols = slice(128 * k, 128 * k + 128)
            gradient = lines_ref[group, 8 * k : 8 * k + 8, :]
            held = masters_ref[rows, cols]
            out_ref[rows, cols] = held - LEARN_RATE * gradient
            total = total + held * gradient
        total_ref[rows, :] = jnp.sum(total, axis=1, keepdims=True)


def combine_kernel(picks_ref, *rest, locals_count):
    back_refs = rest[:locals_count]
    out_ref, in_ref, hot_ref = rest[locals_count:]
    count = out_ref.shape[0]

    @pl.when(pl.program_id(0) == 0)
    def _():
        same = one_hot(iota((count, count), 0) == iota((count, count), 1))
        for member in range(locals_count):
            index = pick_columns(picks_ref, member, locals_count)
            hot = one_hot(iota((index.shape[0], count), 1) == index)
            rows = index.shape[0]
            hot_ref[:, member * rows : (member + 1) * rows] = dot(hot, same, TN).astype(BF16)

    split = split_matrix(CHUNK)
    for start in range(0, out_ref.shape[1], CHUNK):
        cols = slice(start, start + CHUNK)
        pairs = [apart(back_ref[:, :, cols]) for back_ref in back_refs]
        out_rows = jnp.concatenate([pair[0].astype(BF16) for pair in pairs], axis=0)
        in_rows = jnp.concatenate([pair[1].astype(BF16) for pair in pairs], axis=0)
        out_ref[:, cols] = dot(hot_ref[...], out_rows).astype(BF16)
        in_ref[:, cols] = dot(dot(hot_ref[...], in_rows).astype(BF16), split, NT).astype(BF16)


def params(mib):
    return pltpu.CompilerParams(vmem_limit_bytes=mib * 1024 * 1024)


def cost(flops, moved):
    return pl.CostEstimate(flops=flops, bytes_accessed=moved, transcendentals=0)


def pick(picks, tokens, grads, locals_count, peers):
    count, width = tokens.shape
    column = pl.BlockSpec((count, STEP), lambda n: (0, n))
    return pl.pallas_call(
        functools.partial(pick_kernel, locals_count=locals_count),
        grid=(width // STEP,),
        in_specs=[pl.BlockSpec(picks.shape, lambda n: (0, 0)), column, column],
        out_specs=[pl.BlockSpec((peers, 16, STEP), lambda n: (0, 0, n))] * locals_count,
        out_shape=[jax.ShapeDtypeStruct((peers, 16, width), BF16)] * locals_count,
        scratch_shapes=[pltpu.VMEM((locals_count * 8 * peers, count), BF16)],
        compiler_params=params(56),
        cost_estimate=cost(0, 1 << 20),
        name="pick",
    )(picks, tokens, grads)


def pack(masters, member, locals_count):
    mine = masters.shape[0] // locals_count
    steps = 3
    rows = mine // steps
    return pl.pallas_call(
        pack_kernel,
        grid=(steps,),
        in_specs=[pl.BlockSpec((rows, BS * BS), lambda n: (member * steps + n, 0))],
        out_specs=pl.BlockSpec((rows, 32, 128), lambda n: (n, 0, 0)),
        out_shape=jax.ShapeDtypeStruct((mine, 32, 128), BF16),
        scratch_shapes=[pltpu.VMEM((rows // 8, 256, 128), F32)],
        compiler_params=params(56),
        cost_estimate=cost(0, 1 << 20),
        name="pack_%d" % member,
    )(masters)


def run_expert(member, tables, copies, arrived, router_rows):
    peers = arrived.shape[0]
    count = 8 * peers
    whole = pl.BlockSpec(memory_space=pltpu.VMEM)
    scalar = pl.BlockSpec(memory_space=pltpu.SMEM)
    return pl.pallas_call(
        functools.partial(expert_kernel, member=member),
        in_specs=[scalar] * 4 + [whole] * 3,
        out_specs=[whole] * 2,
        out_shape=[
            jax.ShapeDtypeStruct((peers, 16, D), BF16),
            jax.ShapeDtypeStruct((3 * MAXB + OWNERS, 32, 128), BF16),
        ],
        scratch_shapes=[
            pltpu.VMEM((D, 2 * FF), BF16),
            pltpu.VMEM((FF, D), BF16),
            pltpu.VMEM((count, D), BF16),
            pltpu.VMEM((count, D), BF16),
            pltpu.VMEM((count, 2 * FF), F32),
            pltpu.VMEM((count, D), BF16),
            pltpu.VMEM((count, 2 * FF), BF16),
            pltpu.VMEM((D, 2 * FF), BF16),
            pltpu.VMEM((FF, D), BF16),
            pltpu.VMEM((1, D), F32),
        ],
        compiler_params=params(56),
        cost_estimate=cost(150 * 10**9, 1 << 20),
        name="expert_%d" % member,
    )(*tables, copies, arrived, router_rows)


def update(member, summed, masters, held):
    slots = masters.shape[0]
    mine = summed.shape[0] - 1
    steps = 3
    rows = mine // steps
    return pl.pallas_call(
        update_kernel,
        grid=(steps,),
        in_specs=[
            pl.BlockSpec((rows, 32, 128), lambda n: (n, 0, 0)),
            pl.BlockSpec((rows, BS * BS), lambda n: (member * steps + n, 0)),
        ]
        + [pl.BlockSpec(memory_space=pl.ANY)] * len(held),
        out_specs=[
            pl.BlockSpec((rows, BS * BS), lambda n: (member * steps + n, 0)),
            pl.BlockSpec((rows, 1), lambda n: (member * steps + n, 0)),
        ],
        out_shape=[
            jax.ShapeDtypeStruct((slots, BS * BS), F32),
            jax.ShapeDtypeStruct((slots, 1), F32),
        ],
        input_output_aliases={2 + at: at for at in range(len(held))},
        scratch_shapes=[pltpu.VMEM((rows // 8, 256, 128), F32)],
        compiler_params=params(56),
        cost_estimate=cost(0, 1 << 20),
        name="update_%d" % member,
    )(summed, masters, *held)


def combine(picks, back, count):
    locals_count = len(back)
    peers, _, width = back[0].shape
    column = pl.BlockSpec((count, STEP), lambda n: (0, n))
    return pl.pallas_call(
        functools.partial(combine_kernel, locals_count=locals_count),
        grid=(width // STEP,),
        in_specs=[pl.BlockSpec(picks.shape, lambda n: (0, 0))]
        + [pl.BlockSpec((peers, 16, STEP), lambda n: (0, 0, n))] * locals_count,
        out_specs=[column, column],
        out_shape=[jax.ShapeDtypeStruct((count, width), BF16)] * 2,
        scratch_shapes=[pltpu.VMEM((count, locals_count * 8 * peers), BF16)],
        compiler_params=params(56),
        cost_estimate=cost(150 * 10**9, 1 << 20),
        name="combine",
    )(picks, *back)


def slot_tables(kept, owners):
    numbers = jnp.arange(BLOCKS, dtype=jnp.int32)
    slots = jnp.arange(MAXB, dtype=jnp.int32)
    per = MAXB // owners
    matrix = jnp.arange(3, dtype=jnp.int32)[None, :, None]
    place = (slots // per) * (3 * per) + slots % per + matrix * per
    hits = kept[:, :, None, :] == numbers[None, None, :, None]
    inverse = jnp.sum(jnp.where(hits, place[:, :, None, :] + 1, 0), axis=-1) - 1
    valid = kept < BLOCKS
    block = jnp.where(valid, kept, 0)
    width = jnp.array([FF // BS, FF // BS, D // BS], jnp.int32)[None, :, None]
    block_row, block_col = block // width, block % width
    rows = block_row * BS + 32 * (block_col & 1)
    lanes = (block_col >> 1) * 128 + jnp.where(matrix == 1, FF, 0)
    flat = lambda table: table.reshape(-1).astype(jnp.int32)
    return flat(inverse), flat(rows), flat(lanes), flat(valid)


def body(tokens, out_grad, token_picks, router, kept_blocks, masters, scores):
    locals_count = kept_blocks.shape[0]
    owners = lax.axis_size("dp")
    peers = lax.axis_size("expert")
    count, width = tokens.shape
    per = masters.shape[2]
    picks = token_picks[0]
    flat_masters = masters.reshape(locals_count * 3 * per, BS * BS)

    after = lax.optimization_barrier
    packed = [pack(flat_masters, 0, locals_count)]
    tokens, packed[0] = after((tokens, packed[0]))
    sent = list(pick(picks, tokens, out_grad, locals_count, peers))
    sent[0], rest_masters, kept_blocks, router = after((sent[0], flat_masters, kept_blocks, router))
    packed += [pack(rest_masters, member, locals_count) for member in range(1, locals_count)]
    tables = slot_tables(kept_blocks, owners)
    router_rows = router.T.reshape(locals_count, width // BS, 32, 2).transpose(0, 1, 3, 2)
    router_rows = router_rows.reshape(locals_count, width).astype(F32)

    copies, arrived = [], []
    for member in range(locals_count):
        copies.append(lax.all_gather(packed[member], "dp", axis=0, tiled=True))
        rows = sent[member]
        if member:
            rows, arrived[-1] = after((rows, arrived[-1]))
        arrived.append(lax.all_to_all(rows, "expert", split_axis=0, concat_axis=0, tiled=True))
    summed, back = [], []
    for member in range(locals_count):
        rows = arrived[member]
        if member:
            rows, send = after((rows, send))
            back.append(lax.all_to_all(send, "expert", split_axis=0, concat_axis=0, tiled=True))
        send, gradient = run_expert(member, tables, copies[member], rows, router_rows)
        summed.append(lax.psum_scatter(gradient, "dp", scatter_dimension=0, tiled=True))
    send, back = after((send, back))
    back.append(lax.all_to_all(send, "expert", split_axis=0, concat_axis=0, tiled=True))
    held = ()
    for member in range(locals_count - 1):
        held = update(member, summed[member], flat_masters, held)
    held, picks = after((held, picks))
    layer_out, input_grad = combine(picks, back, count)
    summed[-1], layer_out = after((summed[-1], layer_out))
    held = update(locals_count - 1, summed[-1], flat_masters, held)
    master_new = held[0].reshape(masters.shape)
    score_new = scores - SCORE_RATE * held[1].reshape(scores.shape)
    router_new = jnp.stack([part[-1, : width // owners // 128] for part in summed])
    router_new = router_new.reshape(locals_count, width // owners // BS, 2, 32).astype(F32)
    router_new = router_new.transpose(1, 3, 2, 0).reshape(width // owners, locals_count)
    return layer_out, input_grad, master_new, score_new, router_new


def solution(mesh):
    return jax.shard_map(
        body,
        mesh=mesh,
        in_specs=(
            P(("dp", "expert"), None),
            P(("dp", "expert"), None),
            P(("dp", "expert"), None, None),
            P(None, "expert"),
            P("expert", None, None),
            P("expert", None, "dp", None),
            P("expert", None, "dp"),
        ),
        out_specs=(
            P(("dp", "expert"), None),
            P(("dp", "expert"), None),
            P("expert", None, "dp", None),
            P("expert", None, "dp"),
            P("dp", "expert"),
        ),
        check_vma=False,
    )
```

```python
import functools

import jax
import jax.numpy as jnp
from jax import lax
from jax.experimental import pallas as pl
from jax.experimental.pallas import tpu as pltpu
from jax.sharding import PartitionSpec as P

D = 2048
FF = 768
BS = 64
MAXB = 128
OWNERS = 4
BLOCKS = (D // BS) * (FF // BS)
LEARN_RATE = 0.005
SCORE_RATE = 0.05
CHUNK = 256
STEP = 512
F32 = jnp.float32
BF16 = jnp.bfloat16
NN = (((1,), (0,)), ((), ()))
NT = (((1,), (1,)), ((), ()))
TN = (((0,), (0,)), ((), ()))


def dot(left, right, dims=NN):
    return lax.dot_general(left, right, dims, preferred_element_type=F32)


def iota(shape, dim):
    return lax.broadcasted_iota(jnp.int32, shape, dim)


def one_hot(flag):
    return jnp.where(flag, 1.0, 0.0).astype(BF16)


def split_matrix(size):
    col = iota((size, size), 1)
    source = ((col >> 6) << 6) + 2 * (col & 31) + ((col >> 5) & 1)
    return one_hot(iota((size, size), 0) == source)


def pick_columns(picks_ref, member, locals_count):
    experts = picks_ref.shape[0]
    rows = 8 * experts // locals_count
    expert = (iota((rows, experts), 0) >> 3) * locals_count + member
    spread = one_hot(iota((rows, experts), 1) == expert)
    wide = dot(spread, picks_ref[...].astype(F32).astype(BF16))
    keep = iota(wide.shape, 1) == (iota(wide.shape, 0) & 7)
    return jnp.sum(jnp.where(keep, wide, 0.0), axis=1, keepdims=True).astype(jnp.int32)


def interleave(first, second):
    width = first.shape[1]
    pair = [first.reshape(-1, 8, width), second.reshape(-1, 8, width)]
    return jnp.concatenate(pair, axis=1).astype(BF16)


def apart(block):
    wide = block.astype(F32)
    width = wide.shape[2]
    return wide[:, :8, :].reshape(-1, width), wide[:, 8:, :].reshape(-1, width)


def pick_kernel(picks_ref, tokens_ref, grads_ref, *rest, locals_count):
    out_refs, hot_ref = rest[:locals_count], rest[locals_count]
    rows = hot_ref.shape[0] // locals_count

    @pl.when(pl.program_id(0) == 0)
    def _():
        for member in range(locals_count):
            index = pick_columns(picks_ref, member, locals_count)
            hot_ref[member * rows : (member + 1) * rows, :] = one_hot(
                iota((rows, hot_ref.shape[1]), 1) == index
            )

    split = split_matrix(CHUNK)
    for start in range(0, tokens_ref.shape[1], CHUNK):
        cols = slice(start, start + CHUNK)
        tokens = dot(hot_ref[...], dot(tokens_ref[:, cols], split).astype(BF16))
        grads = dot(hot_ref[...], grads_ref[:, cols])
        for member in range(locals_count):
            mine = slice(member * rows, (member + 1) * rows)
            out_refs[member][:, :, cols] = interleave(tokens[mine], grads[mine])


def pack_kernel(masters_ref, *rest):
    out_refs, lines_ref = rest[:-1], rest[-1]
    for at, out_ref in enumerate(out_refs):

        @pl.when(pl.program_id(0) == at)
        def _(out_ref=out_ref):
            for group in range(masters_ref.shape[0] // 8):
                for k in range(32):
                    lines_ref[group, 8 * k : 8 * k + 8, :] = masters_ref[
                        8 * group : 8 * group + 8, 128 * k : 128 * k + 128
                    ]
                for s in range(8):
                    line = lines_ref[group, pl.ds(s, 32, stride=8), :]
                    out_ref[8 * group + s] = line.astype(BF16)


def expert_kernel(
    inverse_ref, row_ref, lane_ref, valid_ref, me_ref,
    arrived_ref, router_ref, *rest,
    member,
):
    piece_refs, send_ref, grad_refs = rest[:8], rest[8], rest[9:16]
    (
    copies_ref, packed_ref, in_sems, out_sems,
    wide_ref, down_ref, rows_ref, grads_ref, pre_ref, part_ref, both_ref,
    grad_wide_ref, grad_down_ref, router_out_ref,
    ) = rest[16:]
    length = piece_refs[0].shape[0]
    loads = [
        pltpu.make_async_copy(piece, copies_ref.at[pl.ds(at * length, length)], in_sems.at[at])
        for at, piece in enumerate(piece_refs)
    ]
    for load in loads:
        load.start()
    for load in loads:
        load.wait()
    base, slot_base = member * 3 * BLOCKS, member * 3 * MAXB
    lane = iota((32, 128), 1)
    half = lane < 64

    def place(target_ref, matrix, block, row, col):
        first = inverse_ref[base + matrix * BLOCKS + block]
        second = inverse_ref[base + matrix * BLOCKS + block + 1]
        one = copies_ref[jnp.maximum(first, 0)]
        two = copies_ref[jnp.maximum(second, 0)]
        one = jnp.where(lane < jnp.where(first >= 0, 128, 0), one, jnp.zeros_like(one))
        two = jnp.where(lane < jnp.where(second >= 0, 128, 0), two, jnp.zeros_like(two))
        target_ref[pl.ds(row, 32), col : col + 128] = jnp.where(half, one, pltpu.roll(two, 64, 1))
        target_ref[pl.ds(row + 32, 32), col : col + 128] = jnp.where(half, pltpu.roll(one, 64, 1), two)

    @pl.loop(0, D // BS)
    def _(r):
        row = pl.multiple_of(r * BS, BS)
        for matrix in range(2):
            for pair in range(FF // BS // 2):
                place(wide_ref, matrix, r * (FF // BS) + 2 * pair, row, matrix * FF + 128 * pair)

    @pl.loop(0, FF // BS)
    def _(r):
        row = pl.multiple_of(r * BS, BS)
        for pair in range(D // BS // 2):
            place(down_ref, 2, r * (D // BS) + 2 * pair, row, 128 * pair)

    count = rows_ref.shape[0]
    chunks = D // CHUNK
    mine = slice(member, member + 1)

    def take(n, logit):
        cols = pl.ds(pl.multiple_of(n * CHUNK, CHUNK), CHUNK)
        rows, grads = apart(arrived_ref[:, :, cols])
        rows_ref[:, cols] = rows.astype(BF16)
        grads_ref[:, cols] = grads.astype(BF16)
        return logit + jnp.sum(rows * router_ref[mine, cols], axis=1, keepdims=True)

    logit = lax.fori_loop(0, chunks, take, jnp.zeros((count, 1), F32))
    gating = 1.0 / (1.0 + jnp.exp(-logit))

    @pl.loop(0, 2 * FF // 512)
    def _(n):
        cols = pl.ds(pl.multiple_of(n * 512, 512), 512)
        pre_ref[:, cols] = dot(rows_ref[...], wide_ref[:, cols])

    split = split_matrix(CHUNK)
    hidden_list = []
    for n in range(FF // CHUNK):
        gate_pre = pre_ref[:, n * CHUNK : (n + 1) * CHUNK]
        up_pre = pre_ref[:, FF + n * CHUNK : FF + (n + 1) * CHUNK]
        hidden = (gate_pre / (1.0 + jnp.exp(-gate_pre)) * up_pre).astype(BF16)
        hidden_list.append(dot(hidden, split).astype(BF16))
    hidden_split = jnp.concatenate(hidden_list, axis=1)

    @pl.loop(0, D // 512)
    def _(n):
        cols = pl.ds(pl.multiple_of(n * 512, 512), 512)
        part_ref[:, cols] = (gating * dot(hidden_split, down_ref[:, cols])).astype(BF16)
        grads_ref[:, cols] = (gating * grads_ref[:, cols].astype(F32)).astype(BF16)

    logit_sum = jnp.zeros((count, 1), F32)
    for n in range(FF // CHUNK):
        spread = dot(grads_ref[...], down_ref[n * CHUNK : (n + 1) * CHUNK, :], NT)
        high = spread.astype(BF16)
        low = (spread - high.astype(F32)).astype(BF16)
        hidden_grad = dot(high, split, NT) + dot(low, split, NT)
        logit_sum = logit_sum + jnp.sum(
            hidden_list[n].astype(F32) * spread, axis=1, keepdims=True
        )
        gate_pre = pre_ref[:, n * CHUNK : (n + 1) * CHUNK]
        up_pre = pre_ref[:, FF + n * CHUNK : FF + (n + 1) * CHUNK]
        sigma = 1.0 / (1.0 + jnp.exp(-gate_pre))
        gate_grad = hidden_grad * up_pre * sigma * (1.0 + gate_pre * (1.0 - sigma))
        both_ref[:, n * CHUNK : (n + 1) * CHUNK] = gate_grad.astype(BF16)
        both_ref[:, FF + n * CHUNK : FF + (n + 1) * CHUNK] = (hidden_grad * gate_pre * sigma).astype(BF16)
        grad_down_ref[n * CHUNK : (n + 1) * CHUNK, :] = dot(hidden_list[n], grads_ref[...], TN).astype(BF16)
    logit_grad = logit_sum * (1.0 - gating)

    @pl.loop(0, chunks)
    def _(n):
        cols = pl.ds(pl.multiple_of(n * CHUNK, CHUNK), CHUNK)
        part = dot(both_ref[...], wide_ref[cols, :], NT) + logit_grad * router_ref[mine, cols]
        send_ref[:, :, cols] = interleave(part_ref[:, cols].astype(F32), part)
        rows = rows_ref[:, cols]
        router_out_ref[:, cols] = jnp.sum(logit_grad * rows.astype(F32), axis=0, keepdims=True)
        grad_wide_ref[cols, :] = dot(rows, both_ref[...], TN).astype(BF16)

    def cut(source_ref, matrix, slot, place_in):
        at = slot_base + matrix * MAXB + slot
        row = pl.multiple_of(row_ref[at], 32)
        other = pl.multiple_of(row ^ 32, 32)
        cols = pl.ds(pl.multiple_of(lane_ref[at], 128), 128)
        odd = row & 32
        stay = source_ref[pl.ds(row, 32), cols]
        move = pltpu.roll(source_ref[pl.ds(other, 32), cols], 64, 1)
        tile = jnp.where((lane & 64) == 2 * odd, stay, move)
        limit = jnp.where(valid_ref[at] > 0, 128, 0)
        packed_ref[place_in] = jnp.where(lane < limit, tile, jnp.zeros_like(tile))

    per = MAXB // OWNERS
    part = packed_ref.shape[0] // OWNERS
    half = 3 * per // 2
    stores = []
    for ahead in (2, 1, 3, 0):
        owner = (me_ref[0] + ahead) & (OWNERS - 1)
        first = ahead * part
        for matrix in range(3):
            source_ref = grad_down_ref if matrix == 2 else grad_wide_ref

            @pl.loop(0, per // 4)
            def _(group, first=first, matrix=matrix, source_ref=source_ref, owner=owner):
                for step in range(4):
                    s = group * 4 + step
                    cut(source_ref, matrix, owner * per + s, first + matrix * per + s)

        start = owner * (D // OWNERS)
        lines = [
            router_out_ref[:, pl.ds(pl.multiple_of(start + at, 128), 128)]
            for at in range(0, D // OWNERS, 128)
        ]
        lines.append(jnp.zeros((32 - len(lines), 128), F32))
        packed_ref[first + 3 * per] = jnp.concatenate(lines, axis=0).astype(BF16)
        cuts = [(0, part)] if ahead == 0 else [(0, half), (half, part - half)]
        for at, (begin, size) in enumerate(cuts):
            number = 0 if ahead == 0 else 2 * ahead - 1 + at
            store = pltpu.make_async_copy(
                packed_ref.at[pl.ds(first + begin, size)], grad_refs[number], out_sems.at[number]
            )
            store.start()
            stores.append(store)
    for store in stores:
        store.wait()


def update_kernel(
    own_ref, left_a_ref, right_a_ref, left_b_ref, right_b_ref,
    own_last_ref, left_last_ref, right_last_ref,
    masters_ref, scores_ref, router_ref, *rest,
    member,
):
    out_ref, scores_out_ref, router_out_ref, lines_ref, total_ref = rest[-5:]
    step, steps = pl.program_id(0), pl.num_programs(0)
    rows = masters_ref.shape[0]

    def gather(left_ref, right_ref):
        for s in range(rows):
            summed = own_ref[s].astype(F32) + left_ref[s].astype(F32) + right_ref[s].astype(F32)
            lines_ref[s // 8, pl.ds(s % 8, 32, stride=8), :] = summed

    @pl.when(step < steps // 2)
    def _():
        gather(left_a_ref, right_a_ref)

    @pl.when(step >= steps // 2)
    def _():
        gather(left_b_ref, right_b_ref)

    for group in range(rows // 8):
        total = jnp.zeros((8, 128), F32)
        here = slice(8 * group, 8 * group + 8)
        for k in range(32):
            cols = slice(128 * k, 128 * k + 128)
            gradient = lines_ref[group, 8 * k : 8 * k + 8, :]
            held = masters_ref[here, cols]
            out_ref[here, cols] = held - LEARN_RATE * gradient
            total = total + held * gradient
        total_ref[pl.ds(pl.multiple_of(step * rows + 8 * group, 8), 8), :] = total

    @pl.when(step == steps - 1)
    def _():
        exact = functools.partial(
            lax.dot_general, dimension_numbers=NT, precision=lax.Precision.HIGHEST, preferred_element_type=F32
        )
        count, experts, per = scores_ref.shape
        mine = iota((experts, per), 0) == member
        for matrix in range(count):
            sums = exact(jnp.ones((8, 128), F32), total_ref[matrix * per : (matrix + 1) * per, :])
            change = jnp.where(mine, jnp.broadcast_to(sums[:1], mine.shape), 0.0)
            scores_out_ref[matrix] = scores_ref[matrix] - SCORE_RATE * change
        last = own_last_ref[0].astype(F32) + left_last_ref[0].astype(F32) + right_last_ref[0].astype(F32)
        last = exact(last, split_matrix(128).astype(F32))
        width = router_ref.shape[1]
        line = jnp.concatenate([last[at : at + 1] for at in range(width // 128)], axis=1)
        held = iota(router_ref.shape, 0) == member
        router_out_ref[...] = jnp.where(held, jnp.broadcast_to(line, router_ref.shape), router_ref[...])


def combine_kernel(picks_ref, *rest, locals_count):
    back_refs = rest[:locals_count]
    out_ref, in_ref, hot_ref = rest[locals_count:]
    count = out_ref.shape[0]

    @pl.when(pl.program_id(0) == 0)
    def _():
        same = one_hot(iota((count, count), 0) == iota((count, count), 1))
        for member in range(locals_count):
            index = pick_columns(picks_ref, member, locals_count)
            hot = one_hot(iota((index.shape[0], count), 1) == index)
            rows = index.shape[0]
            hot_ref[:, member * rows : (member + 1) * rows] = dot(hot, same, TN).astype(BF16)

    split = split_matrix(CHUNK)
    for start in range(0, out_ref.shape[1], CHUNK):
        cols = slice(start, start + CHUNK)
        pairs = [apart(back_ref[:, :, cols]) for back_ref in back_refs]
        out_rows = jnp.concatenate([pair[0].astype(BF16) for pair in pairs], axis=0)
        in_rows = jnp.concatenate([pair[1].astype(BF16) for pair in pairs], axis=0)
        out_ref[:, cols] = dot(hot_ref[...], out_rows).astype(BF16)
        in_ref[:, cols] = dot(dot(hot_ref[...], in_rows).astype(BF16), split, NT).astype(BF16)


def params(mib):
    return pltpu.CompilerParams(vmem_limit_bytes=mib * 1024 * 1024)


def cost(flops, moved):
    return pl.CostEstimate(flops=flops, bytes_accessed=moved, transcendentals=0)


def pick(picks, tokens, grads, locals_count, peers):
    count, width = tokens.shape
    column = pl.BlockSpec((count, STEP), lambda n: (0, n))
    return pl.pallas_call(
        functools.partial(pick_kernel, locals_count=locals_count),
        grid=(width // STEP,),
        in_specs=[pl.BlockSpec(picks.shape, lambda n: (0, 0)), column, column],
        out_specs=[pl.BlockSpec((peers, 16, STEP), lambda n: (0, 0, n))] * locals_count,
        out_shape=[jax.ShapeDtypeStruct((peers, 16, width), BF16)] * locals_count,
        scratch_shapes=[pltpu.VMEM((locals_count * 8 * peers, count), BF16)],
        compiler_params=params(56),
        cost_estimate=cost(0, 1 << 20),
        name="pick",
    )(picks, tokens, grads)


def pack(masters, parts):
    mine = masters.shape[0] // parts
    return pl.pallas_call(
        pack_kernel,
        grid=(parts,),
        in_specs=[pl.BlockSpec((mine, BS * BS), lambda n: (n, 0))],
        out_specs=[pl.BlockSpec((mine, 32, 128), lambda n: (0, 0, 0))] * parts,
        out_shape=[jax.ShapeDtypeStruct((mine, 32, 128), BF16)] * parts,
        scratch_shapes=[pltpu.VMEM((mine // 8, 256, 128), F32)],
        compiler_params=params(56),
        cost_estimate=cost(0, 1 << 20),
        name="pack",
    )(masters)


def run_expert(member, tables, place, pieces, arrived, router_rows):
    peers = arrived.shape[0]
    count = 8 * peers
    whole = pl.BlockSpec(memory_space=pltpu.VMEM)
    scalar = pl.BlockSpec(memory_space=pltpu.SMEM)
    anywhere = pl.BlockSpec(memory_space=pl.ANY)
    part = 3 * MAXB // OWNERS + 1
    half = part // 2
    lengths = [part] + [half, part - half] * 3
    return pl.pallas_call(
        functools.partial(expert_kernel, member=member),
        in_specs=[scalar] * 5 + [whole] * 2 + [anywhere] * len(pieces),
        out_specs=[whole] + [anywhere] * len(lengths),
        out_shape=[jax.ShapeDtypeStruct((peers, 16, D), BF16)]
        + [jax.ShapeDtypeStruct((length, 32, 128), BF16) for length in lengths],
        scratch_shapes=[
            pltpu.VMEM((3 * MAXB, 32, 128), BF16),
            pltpu.VMEM((OWNERS * part, 32, 128), BF16),
            pltpu.SemaphoreType.DMA((len(pieces),)),
            pltpu.SemaphoreType.DMA((len(lengths),)),
            pltpu.VMEM((D, 2 * FF), BF16),
            pltpu.VMEM((FF, D), BF16),
            pltpu.VMEM((count, D), BF16),
            pltpu.VMEM((count, D), BF16),
            pltpu.VMEM((count, 2 * FF), F32),
            pltpu.VMEM((count, D), BF16),
            pltpu.VMEM((count, 2 * FF), BF16),
            pltpu.VMEM((D, 2 * FF), BF16),
            pltpu.VMEM((FF, D), BF16),
            pltpu.VMEM((1, D), F32),
        ],
        compiler_params=params(56),
        cost_estimate=cost(150 * 10**9, 1 << 20),
        name="expert_%d" % member,
    )(*tables, place, arrived, router_rows, *pieces)


def update(member, summed, masters, scores, router_sum, held):
    own, left_a, right_a, left_b, right_b = summed
    mine = own.shape[0] - 1
    steps = 6
    rows = mine // steps
    tile = lambda index: pl.BlockSpec((rows, 32, 128), index)
    early = tile(lambda n: (jnp.minimum(n, steps // 2 - 1), 0, 0))
    late = tile(lambda n: (jnp.maximum(n - steps // 2, 0), 0, 0))
    last = lambda array: pl.BlockSpec((1, 32, 128), lambda n: (array.shape[0] - 1, 0, 0))
    block = pl.BlockSpec((rows, BS * BS), lambda n: (member * steps + n, 0))
    whole = lambda array: pl.BlockSpec(array.shape, lambda n: (0,) * array.ndim)
    return pl.pallas_call(
        functools.partial(update_kernel, member=member),
        grid=(steps,),
        in_specs=[tile(lambda n: (n, 0, 0)), early, early, late, late]
        + [last(own), last(left_b), last(right_b), block, whole(scores), whole(router_sum)]
        + [pl.BlockSpec(memory_space=pl.ANY)] * len(held),
        out_specs=[block, whole(scores), whole(router_sum)],
        out_shape=[
            jax.ShapeDtypeStruct(masters.shape, F32),
            jax.ShapeDtypeStruct(scores.shape, F32),
            jax.ShapeDtypeStruct(router_sum.shape, F32),
        ],
        input_output_aliases={11 + at: at for at in range(len(held))},
        scratch_shapes=[pltpu.VMEM((rows // 8, 256, 128), F32), pltpu.VMEM((mine, 128), F32)],
        compiler_params=params(56),
        cost_estimate=cost(0, 1 << 20),
        name="update_%d" % member,
    )(own, left_a, right_a, left_b, right_b, own, left_b, right_b, masters, scores, router_sum, *held)


def combine(picks, back, count):
    locals_count = len(back)
    peers, _, width = back[0].shape
    column = pl.BlockSpec((count, STEP), lambda n: (0, n))
    return pl.pallas_call(
        functools.partial(combine_kernel, locals_count=locals_count),
        grid=(width // STEP,),
        in_specs=[pl.BlockSpec(picks.shape, lambda n: (0, 0))]
        + [pl.BlockSpec((peers, 16, STEP), lambda n: (0, 0, n))] * locals_count,
        out_specs=[column, column],
        out_shape=[jax.ShapeDtypeStruct((count, width), BF16)] * 2,
        scratch_shapes=[pltpu.VMEM((count, locals_count * 8 * peers), BF16)],
        compiler_params=params(56),
        cost_estimate=cost(150 * 10**9, 1 << 20),
        name="combine",
    )(picks, *back)


def slot_tables(kept, owners, me):
    numbers = jnp.arange(BLOCKS, dtype=jnp.int32)
    slots = jnp.arange(MAXB, dtype=jnp.int32)
    per = MAXB // owners
    matrix = jnp.arange(3, dtype=jnp.int32)[None, :, None]
    ahead = (slots // per - me) % owners
    order = jnp.where(ahead == 0, 0, jnp.where(ahead == owners - 1, 1, ahead + 1))
    place = order * (3 * per) + slots % per + matrix * per
    hits = kept[:, :, None, :] == numbers[None, None, :, None]
    inverse = jnp.sum(jnp.where(hits, place[:, :, None, :] + 1, 0), axis=-1) - 1
    valid = kept < BLOCKS
    block = jnp.where(valid, kept, 0)
    width = jnp.array([FF // BS, FF // BS, D // BS], jnp.int32)[None, :, None]
    block_row, block_col = block // width, block % width
    rows = block_row * BS + 32 * (block_col & 1)
    lanes = (block_col >> 1) * 128 + jnp.where(matrix == 1, FF, 0)
    flat = lambda table: table.reshape(-1).astype(jnp.int32)
    return flat(inverse), flat(rows), flat(lanes), flat(valid)


def shift(array, step):
    owners = lax.axis_size("dp")
    return lax.ppermute(array, "dp", [(i, (i + step) % owners) for i in range(owners)])


def gather_pieces(first, second):
    left_a, right_b = shift(first, 1), shift(second, -1)
    left_b, right_a = shift(second, 1), shift(first, -1)
    return [first, second, left_a, left_b, right_a, right_b, shift(left_a, 1), shift(right_b, -1)]


def scatter_first(own, right_a, right_b, far_a, far_b, left_a, left_b):
    moving = [shift(far_a, 1), shift(far_b, -1), shift(right_b, 1), shift(left_a, -1)]
    return own, right_a, left_b, moving


def scatter_second(own, right_a, left_b, moving):
    passing_a, passing_b, from_left_b, from_right_a = moving
    from_left_a = shift(right_a + passing_a, 1)
    from_right_b = shift(left_b + passing_b, -1)
    return own, from_left_a, from_right_a, from_left_b, from_right_b


def body(tokens, out_grad, token_picks, router, kept_blocks, masters, scores):
    locals_count = kept_blocks.shape[0]
    owners = lax.axis_size("dp")
    peers = lax.axis_size("expert")
    me = lax.axis_index("dp").astype(jnp.int32)
    count, width = tokens.shape
    per = masters.shape[2]
    picks = token_picks[0]
    flat_masters = masters.reshape(locals_count * 3 * per, BS * BS)
    after = lax.optimization_barrier

    def exchange(array):
        return lax.all_to_all(array, "expert", split_axis=0, concat_axis=0, tiled=True)

    sent = list(pick(picks, tokens, out_grad, locals_count, peers))
    sent[0], rest_masters, kept_blocks, router = after((sent[0], flat_masters, kept_blocks, router))
    halves = pack(rest_masters, 2 * locals_count)
    tables = slot_tables(kept_blocks, owners, me)
    router_rows = router.T.reshape(locals_count, width // BS, 32, 2).transpose(0, 1, 3, 2)
    router_rows = router_rows.reshape(locals_count, width).astype(F32)
    place = me.reshape(1)

    pieces, arrived = [], []
    for member in range(locals_count):
        pieces.append(gather_pieces(halves[2 * member], halves[2 * member + 1]))
        rows = sent[member]
        if member:
            rows, arrived[-1] = after((rows, arrived[-1]))
        arrived.append(exchange(rows))
    summed, back = [], []
    for member in range(locals_count):
        rows = arrived[member]
        if member:
            rows, send = after((rows, send))
            back.append(exchange(send))
        send, *gradients = run_expert(member, tables, place, pieces[member], rows, router_rows)
        summed.append(scatter_first(*gradients))
    send, back, summed[:-1] = after((send, back, summed[:-1]))
    back.append(exchange(send))
    summed = [scatter_second(*terms) for terms in summed]
    score_sum = scores.transpose(1, 0, 2)
    router_sum = jnp.zeros((locals_count, width // owners), F32)
    held = ()
    for member in range(locals_count - 1):
        new, score_sum, router_sum = update(member, summed[member], flat_masters, score_sum, router_sum, held)
        held = (new,)
    held, picks = after((held, picks))
    layer_out, input_grad = combine(picks, back, count)
    last, layer_out = after((summed[-1], layer_out))
    new, score_sum, router_sum = update(locals_count - 1, last, flat_masters, score_sum, router_sum, held)
    return layer_out, input_grad, new.reshape(masters.shape), score_sum.transpose(1, 0, 2), router_sum.T


def solution(mesh):
    return jax.shard_map(
        body,
        mesh=mesh,
        in_specs=(
            P(("dp", "expert"), None),
            P(("dp", "expert"), None),
            P(("dp", "expert"), None, None),
            P(None, "expert"),
            P("expert", None, None),
            P("expert", None, "dp", None),
            P("expert", None, "dp"),
        ),
        out_specs=(
            P(("dp", "expert"), None),
            P(("dp", "expert"), None),
            P("expert", None, "dp", None),
            P("expert", None, "dp"),
            P("dp", "expert"),
        ),
        check_vma=False,
    )
```

```python
import functools

import jax
import jax.numpy as jnp
from jax import lax
from jax.experimental import pallas as pl
from jax.experimental.pallas import tpu as pltpu
from jax.sharding import PartitionSpec as P

D = 2048
FF = 768
BS = 64
MAXB = 128
OWNERS = 4
BLOCKS = (D // BS) * (FF // BS)
LEARN_RATE = 0.005
SCORE_RATE = 0.05
CHUNK = 256
STEP = 1024
UNROLL = 32
F32 = jnp.float32
BF16 = jnp.bfloat16
NN = (((1,), (0,)), ((), ()))
NT = (((1,), (1,)), ((), ()))
TN = (((0,), (0,)), ((), ()))


def dot(left, right, dims=NN):
    return lax.dot_general(left, right, dims, preferred_element_type=F32)


def iota(shape, dim):
    return lax.broadcasted_iota(jnp.int32, shape, dim)


def one_hot(flag):
    return jnp.where(flag, 1.0, 0.0).astype(BF16)


def split_matrix(size):
    col = iota((size, size), 1)
    source = ((col >> 6) << 6) + 2 * (col & 31) + ((col >> 5) & 1)
    return one_hot(iota((size, size), 0) == source)


def pick_columns(picks_ref, member, locals_count):
    experts = picks_ref.shape[1]
    rows = 8 * experts // locals_count
    expert = (iota((rows, experts), 0) >> 3) * locals_count + member
    spread = one_hot(iota((rows, experts), 1) == expert)
    wide = dot(spread, picks_ref[...].astype(F32).astype(BF16), NT)
    keep = iota(wide.shape, 1) == (iota(wide.shape, 0) & 7)
    return jnp.sum(jnp.where(keep, wide, 0.0), axis=1, keepdims=True).astype(jnp.int32)


def interleave(first, second):
    width = first.shape[1]
    pair = [first.reshape(-1, 8, width), second.reshape(-1, 8, width)]
    return jnp.concatenate(pair, axis=1).astype(BF16)


def apart(block):
    wide = block.astype(F32)
    width = wide.shape[2]
    return wide[:, :8, :].reshape(-1, width), wide[:, 8:, :].reshape(-1, width)


def pick_kernel(picks_ref, tokens_ref, grads_ref, *rest, locals_count):
    out_refs, hot_ref = rest[:locals_count], rest[locals_count]
    rows = hot_ref.shape[0] // locals_count

    @pl.when(pl.program_id(0) == 0)
    def _():
        for member in range(locals_count):
            index = pick_columns(picks_ref, member, locals_count)
            hot_ref[member * rows : (member + 1) * rows, :] = one_hot(
                iota((rows, hot_ref.shape[1]), 1) == index
            )

    split = split_matrix(CHUNK)
    for start in range(0, tokens_ref.shape[1], CHUNK):
        cols = slice(start, start + CHUNK)
        tokens = dot(hot_ref[...], dot(tokens_ref[:, cols], split).astype(BF16))
        grads = dot(hot_ref[...], grads_ref[:, cols])
        for member in range(locals_count):
            mine = slice(member * rows, (member + 1) * rows)
            out_refs[member][:, :, cols] = interleave(tokens[mine], grads[mine])


def pack_kernel(masters_ref, *rest):
    out_refs, lines_ref = rest[:-1], rest[-1]
    for at, out_ref in enumerate(out_refs):

        @pl.when(pl.program_id(0) == at)
        def _(out_ref=out_ref):
            for group in range(masters_ref.shape[0] // 8):
                for k in range(32):
                    lines_ref[group, 8 * k : 8 * k + 8, :] = masters_ref[
                        8 * group : 8 * group + 8, 128 * k : 128 * k + 128
                    ]
                for s in range(8):
                    line = lines_ref[group, pl.ds(s, 32, stride=8), :]
                    out_ref[8 * group + s] = line.astype(BF16)


def expert_kernel(
    inverse_ref, row_ref, lane_ref, me_ref,
    arrived_ref, router_ref, *rest,
    member,
):
    piece_refs, send_ref, grad_refs = rest[:8], rest[8], rest[9:16]
    (
    copies_ref, packed_ref, in_sems, out_sems,
    wide_ref, down_ref, rows_ref, grads_ref, pre_ref, part_ref, both_ref,
    grad_wide_ref, grad_down_ref, router_out_ref,
    ) = rest[16:]
    length = piece_refs[0].shape[0]
    loads = [
        pltpu.make_async_copy(piece, copies_ref.at[pl.ds(at * length, length)], in_sems.at[at])
        for at, piece in enumerate(piece_refs)
    ]
    for load in loads:
        load.start()
    copies_ref[3 * MAXB] = jnp.zeros((32, 128), BF16)
    grad_wide_ref[D:, :] = jnp.zeros((BS, 2 * FF), BF16)
    grad_down_ref[FF:, :] = jnp.zeros((BS, D), BF16)
    base, slot_base = member * 3 * BLOCKS, member * 3 * MAXB
    lane = iota((32, 128), 1)
    half = lane < 64

    count = rows_ref.shape[0]
    chunks = D // CHUNK
    mine = slice(member, member + 1)

    def take(n, logit):
        cols = pl.ds(pl.multiple_of(n * CHUNK, CHUNK), CHUNK)
        rows, grads = apart(arrived_ref[:, :, cols])
        rows_ref[:, cols] = rows.astype(BF16)
        grads_ref[:, cols] = grads.astype(BF16)
        return logit + jnp.sum(rows * router_ref[mine, cols], axis=1, keepdims=True)

    logit = lax.fori_loop(0, chunks, take, jnp.zeros((count, 1), F32))
    gating = 1.0 / (1.0 + jnp.exp(-logit))

    for load in loads:
        load.wait()

    def place(target_ref, matrix, block, row, col):
        one = copies_ref[inverse_ref[base + matrix * BLOCKS + block]]
        two = copies_ref[inverse_ref[base + matrix * BLOCKS + block + 1]]
        crossed = pltpu.roll(jnp.where(half, two, one), 64, 1)
        target_ref[pl.ds(row, 32), col : col + 128] = jnp.where(half, one, crossed)
        target_ref[pl.ds(row + 32, 32), col : col + 128] = jnp.where(half, crossed, two)

    @pl.loop(0, D // BS)
    def _(r):
        row = pl.multiple_of(r * BS, BS)
        for matrix in range(2):
            for pair in range(FF // BS // 2):
                place(wide_ref, matrix, r * (FF // BS) + 2 * pair, row, matrix * FF + 128 * pair)

    @pl.loop(0, FF // BS)
    def _(r):
        row = pl.multiple_of(r * BS, BS)
        for pair in range(D // BS // 2):
            place(down_ref, 2, r * (D // BS) + 2 * pair, row, 128 * pair)

    @pl.loop(0, 2 * FF // 512)
    def _(n):
        cols = pl.ds(pl.multiple_of(n * 512, 512), 512)
        pre_ref[:, cols] = dot(rows_ref[...], wide_ref[:, cols])

    split = split_matrix(CHUNK)
    hidden_list = []
    for n in range(FF // CHUNK):
        gate_pre = pre_ref[:, n * CHUNK : (n + 1) * CHUNK]
        up_pre = pre_ref[:, FF + n * CHUNK : FF + (n + 1) * CHUNK]
        hidden = (gate_pre / (1.0 + jnp.exp(-gate_pre)) * up_pre).astype(BF16)
        hidden_list.append(dot(hidden, split).astype(BF16))
    hidden_split = jnp.concatenate(hidden_list, axis=1)

    @pl.loop(0, D // 512)
    def _(n):
        cols = pl.ds(pl.multiple_of(n * 512, 512), 512)
        part_ref[:, cols] = (gating * dot(hidden_split, down_ref[:, cols])).astype(BF16)
        grads_ref[:, cols] = (gating * grads_ref[:, cols].astype(F32)).astype(BF16)

    logit_sum = jnp.zeros((count, 1), F32)
    for n in range(FF // CHUNK):
        spread = dot(grads_ref[...], down_ref[n * CHUNK : (n + 1) * CHUNK, :], NT)
        high = spread.astype(BF16)
        low = (spread - high.astype(F32)).astype(BF16)
        hidden_grad = dot(high, split, NT) + dot(low, split, NT)
        logit_sum = logit_sum + jnp.sum(
            hidden_list[n].astype(F32) * spread, axis=1, keepdims=True
        )
        gate_pre = pre_ref[:, n * CHUNK : (n + 1) * CHUNK]
        up_pre = pre_ref[:, FF + n * CHUNK : FF + (n + 1) * CHUNK]
        sigma = 1.0 / (1.0 + jnp.exp(-gate_pre))
        gate_grad = hidden_grad * up_pre * sigma * (1.0 + gate_pre * (1.0 - sigma))
        both_ref[:, n * CHUNK : (n + 1) * CHUNK] = gate_grad.astype(BF16)
        both_ref[:, FF + n * CHUNK : FF + (n + 1) * CHUNK] = (hidden_grad * gate_pre * sigma).astype(BF16)
        grad_down_ref[n * CHUNK : (n + 1) * CHUNK, :] = dot(hidden_list[n], grads_ref[...], TN).astype(BF16)
    logit_grad = logit_sum * (1.0 - gating)

    @pl.loop(0, chunks)
    def _(n):
        cols = pl.ds(pl.multiple_of(n * CHUNK, CHUNK), CHUNK)
        part = dot(both_ref[...], wide_ref[cols, :], NT) + logit_grad * router_ref[mine, cols]
        send_ref[:, :, cols] = interleave(part_ref[:, cols].astype(F32), part)
        rows = rows_ref[:, cols]
        router_out_ref[:, cols] = jnp.sum(logit_grad * rows.astype(F32), axis=0, keepdims=True)
        grad_wide_ref[cols, :] = dot(rows, both_ref[...], TN).astype(BF16)

    def cut(source_ref, matrix, slot, place_in):
        at = slot_base + matrix * MAXB + slot
        row = pl.multiple_of(row_ref[at], 32)
        other = pl.multiple_of(row ^ 32, 32)
        cols = pl.ds(pl.multiple_of(lane_ref[at], 128), 128)
        stay = source_ref[pl.ds(row, 32), cols]
        move = pltpu.roll(source_ref[pl.ds(other, 32), cols], 64, 1)
        packed_ref[place_in] = jnp.where((lane & 64) == 2 * (row & 32), stay, move)

    per = MAXB // OWNERS
    part = packed_ref.shape[0] // OWNERS
    half = 3 * per // 2
    stores = []
    for ahead in (2, 1, 3, 0):
        owner = (me_ref[0] + ahead) & (OWNERS - 1)
        first = ahead * part
        for matrix in range(3):
            source_ref = grad_down_ref if matrix == 2 else grad_wide_ref

            @pl.loop(0, per // UNROLL)
            def _(group, first=first, matrix=matrix, source_ref=source_ref, owner=owner):
                for step in range(UNROLL):
                    s = group * UNROLL + step
                    cut(source_ref, matrix, owner * per + s, first + matrix * per + s)

        start = owner * (D // OWNERS)
        lines = [
            router_out_ref[:, pl.ds(pl.multiple_of(start + at, 128), 128)]
            for at in range(0, D // OWNERS, 128)
        ]
        lines.append(jnp.zeros((32 - len(lines), 128), F32))
        packed_ref[first + 3 * per] = jnp.concatenate(lines, axis=0).astype(BF16)
        cuts = [(0, part)] if ahead == 0 else [(0, half), (half, part - half)]
        for at, (begin, size) in enumerate(cuts):
            number = 0 if ahead == 0 else 2 * ahead - 1 + at
            store = pltpu.make_async_copy(
                packed_ref.at[pl.ds(first + begin, size)], grad_refs[number], out_sems.at[number]
            )
            store.start()
            stores.append(store)
    for store in stores:
        store.wait()


def update_kernel(
    own_ref, left_a_ref, right_a_ref, left_b_ref, right_b_ref,
    own_last_ref, left_last_ref, right_last_ref,
    masters_ref, scores_ref, router_ref, *rest,
    member,
):
    out_ref, scores_out_ref, router_out_ref, lines_ref, total_ref = rest[-5:]
    step, steps = pl.program_id(0), pl.num_programs(0)
    rows = masters_ref.shape[0]

    def gather(left_ref, right_ref):
        for s in range(rows):
            summed = own_ref[s].astype(F32) + left_ref[s].astype(F32) + right_ref[s].astype(F32)
            lines_ref[s // 8, pl.ds(s % 8, 32, stride=8), :] = summed

    @pl.when(step < steps // 2)
    def _():
        gather(left_a_ref, right_a_ref)

    @pl.when(step >= steps // 2)
    def _():
        gather(left_b_ref, right_b_ref)

    for group in range(rows // 8):
        total = jnp.zeros((8, 128), F32)
        here = slice(8 * group, 8 * group + 8)
        for k in range(32):
            cols = slice(128 * k, 128 * k + 128)
            gradient = lines_ref[group, 8 * k : 8 * k + 8, :]
            held = masters_ref[here, cols]
            out_ref[here, cols] = held - LEARN_RATE * gradient
            total = total + held * gradient
        total_ref[pl.ds(pl.multiple_of(step * rows + 8 * group, 8), 8), :] = total

    @pl.when(step == steps - 1)
    def _():
        exact = functools.partial(
            lax.dot_general, dimension_numbers=NT, precision=lax.Precision.HIGHEST, preferred_element_type=F32
        )
        count, experts, per = scores_ref.shape
        mine = iota((experts, per), 0) == member
        for matrix in range(count):
            sums = exact(jnp.ones((8, 128), F32), total_ref[matrix * per : (matrix + 1) * per, :])
            change = jnp.where(mine, jnp.broadcast_to(sums[:1], mine.shape), 0.0)
            scores_out_ref[matrix] = scores_ref[matrix] - SCORE_RATE * change
        last = own_last_ref[0].astype(F32) + left_last_ref[0].astype(F32) + right_last_ref[0].astype(F32)
        last = exact(last, split_matrix(128).astype(F32))
        width = router_ref.shape[1]
        line = jnp.concatenate([last[at : at + 1] for at in range(width // 128)], axis=1)
        held = iota(router_ref.shape, 0) == member
        router_out_ref[...] = jnp.where(held, jnp.broadcast_to(line, router_ref.shape), router_ref[...])


def combine_kernel(picks_ref, *rest, locals_count):
    back_refs = rest[:locals_count]
    out_ref, in_ref, hot_ref = rest[locals_count:]
    count = out_ref.shape[0]

    @pl.when(pl.program_id(0) == 0)
    def _():
        same = one_hot(iota((count, count), 0) == iota((count, count), 1))
        for member in range(locals_count):
            index = pick_columns(picks_ref, member, locals_count)
            hot = one_hot(iota((index.shape[0], count), 1) == index)
            rows = index.shape[0]
            hot_ref[:, member * rows : (member + 1) * rows] = dot(hot, same, TN).astype(BF16)

    split = split_matrix(CHUNK)
    for start in range(0, out_ref.shape[1], CHUNK):
        cols = slice(start, start + CHUNK)
        pairs = [apart(back_ref[:, :, cols]) for back_ref in back_refs]
        out_rows = jnp.concatenate([pair[0].astype(BF16) for pair in pairs], axis=0)
        in_rows = jnp.concatenate([pair[1].astype(BF16) for pair in pairs], axis=0)
        out_ref[:, cols] = dot(hot_ref[...], out_rows).astype(BF16)
        in_ref[:, cols] = dot(dot(hot_ref[...], in_rows).astype(BF16), split, NT).astype(BF16)


def params(mib):
    return pltpu.CompilerParams(vmem_limit_bytes=mib * 1024 * 1024)


def cost(flops, moved):
    return pl.CostEstimate(flops=flops, bytes_accessed=moved, transcendentals=0)


def pick(picks, tokens, grads, locals_count, peers):
    count, width = tokens.shape
    column = pl.BlockSpec((count, STEP), lambda n: (0, n))
    return pl.pallas_call(
        functools.partial(pick_kernel, locals_count=locals_count),
        grid=(width // STEP,),
        in_specs=[pl.BlockSpec(picks.shape, lambda n: (0, 0)), column, column],
        out_specs=[pl.BlockSpec((peers, 16, STEP), lambda n: (0, 0, n))] * locals_count,
        out_shape=[jax.ShapeDtypeStruct((peers, 16, width), BF16)] * locals_count,
        scratch_shapes=[pltpu.VMEM((locals_count * 8 * peers, count), BF16)],
        compiler_params=params(56),
        cost_estimate=cost(0, 1 << 20),
        name="pick",
    )(picks, tokens, grads)


def pack(masters, parts):
    mine = masters.shape[0] // parts
    return pl.pallas_call(
        pack_kernel,
        grid=(parts,),
        in_specs=[pl.BlockSpec((mine, BS * BS), lambda n: (n, 0))],
        out_specs=[pl.BlockSpec((mine, 32, 128), lambda n: (0, 0, 0))] * parts,
        out_shape=[jax.ShapeDtypeStruct((mine, 32, 128), BF16)] * parts,
        scratch_shapes=[pltpu.VMEM((mine // 8, 256, 128), F32)],
        compiler_params=params(56),
        cost_estimate=cost(0, 1 << 20),
        name="pack",
    )(masters)


def run_expert(member, tables, place, pieces, arrived, router_rows):
    peers = arrived.shape[0]
    count = 8 * peers
    whole = pl.BlockSpec(memory_space=pltpu.VMEM)
    scalar = pl.BlockSpec(memory_space=pltpu.SMEM)
    anywhere = pl.BlockSpec(memory_space=pl.ANY)
    part = 3 * MAXB // OWNERS + 1
    half = part // 2
    lengths = [part] + [half, part - half] * 3
    return pl.pallas_call(
        functools.partial(expert_kernel, member=member),
        in_specs=[scalar] * 4 + [whole] * 2 + [anywhere] * len(pieces),
        out_specs=[whole] + [anywhere] * len(lengths),
        out_shape=[jax.ShapeDtypeStruct((peers, 16, D), BF16)]
        + [jax.ShapeDtypeStruct((length, 32, 128), BF16) for length in lengths],
        scratch_shapes=[
            pltpu.VMEM((3 * MAXB + 1, 32, 128), BF16),
            pltpu.VMEM((OWNERS * part, 32, 128), BF16),
            pltpu.SemaphoreType.DMA((len(pieces),)),
            pltpu.SemaphoreType.DMA((len(lengths),)),
            pltpu.VMEM((D, 2 * FF), BF16),
            pltpu.VMEM((FF, D), BF16),
            pltpu.VMEM((count, D), BF16),
            pltpu.VMEM((count, D), BF16),
            pltpu.VMEM((count, 2 * FF), F32),
            pltpu.VMEM((count, D), BF16),
            pltpu.VMEM((count, 2 * FF), BF16),
            pltpu.VMEM((D + BS, 2 * FF), BF16),
            pltpu.VMEM((FF + BS, D), BF16),
            pltpu.VMEM((1, D), F32),
        ],
        compiler_params=params(56),
        cost_estimate=cost(150 * 10**9, 1 << 20),
        name="expert_%d" % member,
    )(*tables, place, arrived, router_rows, *pieces)


def update(member, summed, masters, scores, router_sum, held):
    own, left_a, right_a, left_b, right_b = summed
    mine = own.shape[0] - 1
    steps = 2
    rows = mine // steps
    tile = lambda index: pl.BlockSpec((rows, 32, 128), index)
    early = tile(lambda n: (jnp.minimum(n, steps // 2 - 1), 0, 0))
    late = tile(lambda n: (jnp.maximum(n - steps // 2, 0), 0, 0))
    last = lambda array: pl.BlockSpec((1, 32, 128), lambda n: (array.shape[0] - 1, 0, 0))
    block = pl.BlockSpec((rows, BS * BS), lambda n: (member * steps + n, 0))
    whole = lambda array: pl.BlockSpec(array.shape, lambda n: (0,) * array.ndim)
    return pl.pallas_call(
        functools.partial(update_kernel, member=member),
        grid=(steps,),
        in_specs=[tile(lambda n: (n, 0, 0)), early, early, late, late]
        + [last(own), last(left_b), last(right_b), block, whole(scores), whole(router_sum)]
        + [pl.BlockSpec(memory_space=pl.ANY)] * len(held),
        out_specs=[block, whole(scores), whole(router_sum)],
        out_shape=[
            jax.ShapeDtypeStruct(masters.shape, F32),
            jax.ShapeDtypeStruct(scores.shape, F32),
            jax.ShapeDtypeStruct(router_sum.shape, F32),
        ],
        input_output_aliases={11 + at: at for at in range(len(held))},
        scratch_shapes=[pltpu.VMEM((rows // 8, 256, 128), F32), pltpu.VMEM((mine, 128), F32)],
        compiler_params=params(56),
        cost_estimate=cost(0, 1 << 20),
        name="update_%d" % member,
    )(own, left_a, right_a, left_b, right_b, own, left_b, right_b, masters, scores, router_sum, *held)


def combine(picks, back, count):
    locals_count = len(back)
    peers, _, width = back[0].shape
    column = pl.BlockSpec((count, STEP), lambda n: (0, n))
    return pl.pallas_call(
        functools.partial(combine_kernel, locals_count=locals_count),
        grid=(width // STEP,),
        in_specs=[pl.BlockSpec(picks.shape, lambda n: (0, 0))]
        + [pl.BlockSpec((peers, 16, STEP), lambda n: (0, 0, n))] * locals_count,
        out_specs=[column, column],
        out_shape=[jax.ShapeDtypeStruct((count, width), BF16)] * 2,
        scratch_shapes=[pltpu.VMEM((count, locals_count * 8 * peers), BF16)],
        compiler_params=params(56),
        cost_estimate=cost(150 * 10**9, 1 << 20),
        name="combine",
    )(picks, *back)


def slot_tables(kept, owners, me):
    numbers = jnp.arange(BLOCKS, dtype=jnp.int32)
    slots = jnp.arange(MAXB, dtype=jnp.int32)
    per = MAXB // owners
    matrix = jnp.arange(3, dtype=jnp.int32)[None, :, None]
    ahead = (slots // per - me) % owners
    order = jnp.where(ahead == 0, 0, jnp.where(ahead == owners - 1, 1, ahead + 1))
    place = order * (3 * per) + slots % per + matrix * per
    hits = kept[:, :, None, :] == numbers[None, None, :, None]
    inverse = 3 * MAXB + jnp.sum(jnp.where(hits, place[:, :, None, :] - 3 * MAXB, 0), axis=-1)
    valid = kept < BLOCKS
    block = jnp.where(valid, kept, 0)
    width = jnp.array([FF // BS, FF // BS, D // BS], jnp.int32)[None, :, None]
    block_row, block_col = block // width, block % width
    empty = jnp.where(matrix == 2, FF, D)
    rows = jnp.where(valid, block_row * BS + 32 * (block_col & 1), empty)
    lanes = (block_col >> 1) * 128 + jnp.where(matrix == 1, FF, 0)
    flat = lambda table: table.reshape(-1).astype(jnp.int32)
    return flat(inverse), flat(rows), flat(lanes)


def shift(array, step):
    owners = lax.axis_size("dp")
    return lax.ppermute(array, "dp", [(i, (i + step) % owners) for i in range(owners)])


def gather_pieces(first, second):
    left_a, right_b = shift(first, 1), shift(second, -1)
    left_b, right_a = shift(second, 1), shift(first, -1)
    return [first, second, left_a, left_b, right_a, right_b, shift(left_a, 1), shift(right_b, -1)]


def scatter_first(own, right_a, right_b, far_a, far_b, left_a, left_b):
    moving = [shift(far_a, 1), shift(far_b, -1), shift(right_b, 1), shift(left_a, -1)]
    return own, right_a, left_b, moving


def scatter_second(own, right_a, left_b, moving):
    passing_a, passing_b, from_left_b, from_right_a = moving
    from_left_a = shift(right_a + passing_a, 1)
    from_right_b = shift(left_b + passing_b, -1)
    return own, from_left_a, from_right_a, from_left_b, from_right_b


def body(tokens, out_grad, token_picks, router, kept_blocks, masters, scores):
    locals_count = kept_blocks.shape[0]
    owners = lax.axis_size("dp")
    peers = lax.axis_size("expert")
    me = lax.axis_index("dp").astype(jnp.int32)
    count, width = tokens.shape
    per = masters.shape[2]
    picks = token_picks[0].T
    flat_masters = masters.reshape(locals_count * 3 * per, BS * BS)
    after = lax.optimization_barrier

    def exchange(array):
        return lax.all_to_all(array, "expert", split_axis=0, concat_axis=0, tiled=True)

    sent = list(pick(picks, tokens, out_grad, locals_count, peers))
    sent[0], rest_masters, kept_blocks, router = after((sent[0], flat_masters, kept_blocks, router))
    halves = pack(rest_masters, 2 * locals_count)
    tables = slot_tables(kept_blocks, owners, me)
    router_rows = router.T.reshape(locals_count, width // BS, 32, 2).transpose(0, 1, 3, 2)
    router_rows = router_rows.reshape(locals_count, width).astype(F32)
    place = me.reshape(1)

    pieces, arrived = [], []
    for member in range(locals_count):
        pieces.append(gather_pieces(halves[2 * member], halves[2 * member + 1]))
        rows = sent[member]
        if member:
            rows, arrived[-1] = after((rows, arrived[-1]))
        arrived.append(exchange(rows))
    summed, back = [], []
    for member in range(locals_count):
        rows = arrived[member]
        if member:
            rows, send = after((rows, send))
            back.append(exchange(send))
        send, *gradients = run_expert(member, tables, place, pieces[member], rows, router_rows)
        summed.append(scatter_first(*gradients))
    send, back, summed[:-1] = after((send, back, summed[:-1]))
    back.append(exchange(send))
    summed = [scatter_second(*terms) for terms in summed]
    score_sum = scores.transpose(1, 0, 2)
    router_sum = jnp.zeros((locals_count, width // owners), F32)
    held = ()
    for member in range(locals_count - 1):
        new, score_sum, router_sum = update(member, summed[member], flat_masters, score_sum, router_sum, held)
        held = (new,)
    held, picks = after((held, picks))
    layer_out, input_grad = combine(picks, back, count)
    last, layer_out = after((summed[-1], layer_out))
    new, score_sum, router_sum = update(locals_count - 1, last, flat_masters, score_sum, router_sum, held)
    return layer_out, input_grad, new.reshape(masters.shape), score_sum.transpose(1, 0, 2), router_sum.T


def solution(mesh):
    return jax.shard_map(
        body,
        mesh=mesh,
        in_specs=(
            P(("dp", "expert"), None),
            P(("dp", "expert"), None),
            P(("dp", "expert"), None, None),
            P(None, "expert"),
            P("expert", None, None),
            P("expert", None, "dp", None),
            P("expert", None, "dp"),
        ),
        out_specs=(
            P(("dp", "expert"), None),
            P(("dp", "expert"), None),
            P("expert", None, "dp", None),
            P("expert", None, "dp"),
            P("dp", "expert"),
        ),
        check_vma=False,
    )
```

```python
import functools

import jax
import jax.numpy as jnp
from jax import lax
from jax.experimental import pallas as pl
from jax.experimental.pallas import tpu as pltpu
from jax.sharding import PartitionSpec as P

D = 2048
FF = 768
BS = 64
MAXB = 128
OWNERS = 4
BLOCKS = (D // BS) * (FF // BS)
LEARN_RATE = 0.005
SCORE_RATE = 0.05
CHUNK = 256
STEP = 1024
UNROLL = 32
F32 = jnp.float32
BF16 = jnp.bfloat16
NN = (((1,), (0,)), ((), ()))
NT = (((1,), (1,)), ((), ()))
TN = (((0,), (0,)), ((), ()))


def dot(left, right, dims=NN):
    return lax.dot_general(left, right, dims, preferred_element_type=F32)


def iota(shape, dim):
    return lax.broadcasted_iota(jnp.int32, shape, dim)


def one_hot(flag):
    return jnp.where(flag, 1.0, 0.0).astype(BF16)


def split_matrix(size):
    col = iota((size, size), 1)
    source = ((col >> 6) << 6) + 2 * (col & 31) + ((col >> 5) & 1)
    return one_hot(iota((size, size), 0) == source)


def pick_columns(picks_ref, member, locals_count):
    experts = picks_ref.shape[1]
    rows = 8 * experts // locals_count
    expert = (iota((rows, experts), 0) >> 3) * locals_count + member
    spread = one_hot(iota((rows, experts), 1) == expert)
    wide = dot(spread, picks_ref[...].astype(F32).astype(BF16), NT)
    keep = iota(wide.shape, 1) == (iota(wide.shape, 0) & 7)
    return jnp.sum(jnp.where(keep, wide, 0.0), axis=1, keepdims=True).astype(jnp.int32)


def interleave(first, second):
    width = first.shape[1]
    pair = [first.reshape(-1, 8, width), second.reshape(-1, 8, width)]
    return jnp.concatenate(pair, axis=1).astype(BF16)


def apart(block):
    wide = block.astype(F32)
    width = wide.shape[2]
    return wide[:, :8, :].reshape(-1, width), wide[:, 8:, :].reshape(-1, width)


def pick_kernel(picks_ref, tokens_ref, grads_ref, *rest, locals_count):
    out_refs, hot_ref = rest[:locals_count], rest[locals_count]
    rows = hot_ref.shape[0] // locals_count

    @pl.when(pl.program_id(0) == 0)
    def _():
        for member in range(locals_count):
            index = pick_columns(picks_ref, member, locals_count)
            hot_ref[member * rows : (member + 1) * rows, :] = one_hot(
                iota((rows, hot_ref.shape[1]), 1) == index
            )

    split = split_matrix(CHUNK)
    for start in range(0, tokens_ref.shape[1], CHUNK):
        cols = slice(start, start + CHUNK)
        tokens = dot(hot_ref[...], dot(tokens_ref[:, cols], split).astype(BF16))
        grads = dot(hot_ref[...], grads_ref[:, cols])
        for member in range(locals_count):
            mine = slice(member * rows, (member + 1) * rows)
            out_refs[member][:, :, cols] = interleave(tokens[mine], grads[mine])


def pack_kernel(masters_ref, *rest):
    out_refs, lines_ref = rest[:-1], rest[-1]
    for at, out_ref in enumerate(out_refs):

        @pl.when(pl.program_id(0) == at)
        def _(out_ref=out_ref):
            for group in range(masters_ref.shape[0] // 8):
                for k in range(32):
                    lines_ref[group, 8 * k : 8 * k + 8, :] = masters_ref[
                        8 * group : 8 * group + 8, 128 * k : 128 * k + 128
                    ]
                for s in range(8):
                    line = lines_ref[group, pl.ds(s, 32, stride=8), :]
                    out_ref[8 * group + s] = line.astype(BF16)


def expert_kernel(
    inverse_ref, row_ref, lane_ref, me_ref,
    arrived_ref, router_ref, *rest,
    member,
):
    piece_refs, send_ref, grad_refs = rest[:8], rest[8], rest[9:16]
    (
    copies_ref, packed_ref, in_sems, out_sems,
    wide_ref, down_ref, rows_ref, grads_ref, pre_ref, part_ref, both_ref,
    grad_wide_ref, grad_down_ref, router_out_ref,
    ) = rest[16:]
    length = piece_refs[0].shape[0]
    loads = [
        pltpu.make_async_copy(piece, copies_ref.at[pl.ds(at * length, length)], in_sems.at[at])
        for at, piece in enumerate(piece_refs)
    ]
    for load in loads:
        load.start()
    copies_ref[3 * MAXB] = jnp.zeros((32, 128), BF16)
    grad_wide_ref[D:, :] = jnp.zeros((BS, 2 * FF), BF16)
    grad_down_ref[FF:, :] = jnp.zeros((BS, D), BF16)
    base, slot_base = member * 3 * BLOCKS, member * 3 * MAXB
    lane = iota((32, 128), 1)
    half = lane < 64

    count = rows_ref.shape[0]
    chunks = D // CHUNK
    mine = slice(member, member + 1)

    def take(n, logit):
        cols = pl.ds(pl.multiple_of(n * CHUNK, CHUNK), CHUNK)
        rows, grads = apart(arrived_ref[:, :, cols])
        rows_ref[:, cols] = rows.astype(BF16)
        grads_ref[:, cols] = grads.astype(BF16)
        return logit + jnp.sum(rows * router_ref[mine, cols], axis=1, keepdims=True)

    logit = lax.fori_loop(0, chunks, take, jnp.zeros((count, 1), F32))
    gating = 1.0 / (1.0 + jnp.exp(-logit))

    for load in loads:
        load.wait()

    def place(target_ref, matrix, block, row, col):
        one = copies_ref[inverse_ref[base + matrix * BLOCKS + block]]
        two = copies_ref[inverse_ref[base + matrix * BLOCKS + block + 1]]
        crossed = pltpu.roll(jnp.where(half, two, one), 64, 1)
        target_ref[pl.ds(row, 32), col : col + 128] = jnp.where(half, one, crossed)
        target_ref[pl.ds(row + 32, 32), col : col + 128] = jnp.where(half, crossed, two)

    @pl.loop(0, D // BS)
    def _(r):
        row = pl.multiple_of(r * BS, BS)
        for matrix in range(2):
            for pair in range(FF // BS // 2):
                place(wide_ref, matrix, r * (FF // BS) + 2 * pair, row, matrix * FF + 128 * pair)

    @pl.loop(0, FF // BS)
    def _(r):
        row = pl.multiple_of(r * BS, BS)
        for pair in range(D // BS // 2):
            place(down_ref, 2, r * (D // BS) + 2 * pair, row, 128 * pair)

    @pl.loop(0, 2 * FF // 512)
    def _(n):
        cols = pl.ds(pl.multiple_of(n * 512, 512), 512)
        pre_ref[:, cols] = dot(rows_ref[...], wide_ref[:, cols])

    split = split_matrix(CHUNK)
    hidden_list = []
    for n in range(FF // CHUNK):
        gate_pre = pre_ref[:, n * CHUNK : (n + 1) * CHUNK]
        up_pre = pre_ref[:, FF + n * CHUNK : FF + (n + 1) * CHUNK]
        hidden = (gate_pre / (1.0 + jnp.exp(-gate_pre)) * up_pre).astype(BF16)
        hidden_list.append(dot(hidden, split).astype(BF16))
    hidden_split = jnp.concatenate(hidden_list, axis=1)

    @pl.loop(0, D // 512)
    def _(n):
        cols = pl.ds(pl.multiple_of(n * 512, 512), 512)
        part_ref[:, cols] = (gating * dot(hidden_split, down_ref[:, cols])).astype(BF16)
        grads_ref[:, cols] = (gating * grads_ref[:, cols].astype(F32)).astype(BF16)

    logit_sum = jnp.zeros((count, 1), F32)
    for n in range(FF // CHUNK):
        spread = dot(grads_ref[...], down_ref[n * CHUNK : (n + 1) * CHUNK, :], NT)
        high = spread.astype(BF16)
        low = (spread - high.astype(F32)).astype(BF16)
        hidden_grad = dot(high, split, NT) + dot(low, split, NT)
        logit_sum = logit_sum + jnp.sum(
            hidden_list[n].astype(F32) * spread, axis=1, keepdims=True
        )
        gate_pre = pre_ref[:, n * CHUNK : (n + 1) * CHUNK]
        up_pre = pre_ref[:, FF + n * CHUNK : FF + (n + 1) * CHUNK]
        sigma = 1.0 / (1.0 + jnp.exp(-gate_pre))
        gate_grad = hidden_grad * up_pre * sigma * (1.0 + gate_pre * (1.0 - sigma))
        both_ref[:, n * CHUNK : (n + 1) * CHUNK] = gate_grad.astype(BF16)
        both_ref[:, FF + n * CHUNK : FF + (n + 1) * CHUNK] = (hidden_grad * gate_pre * sigma).astype(BF16)
        grad_down_ref[n * CHUNK : (n + 1) * CHUNK, :] = dot(hidden_list[n], grads_ref[...], TN).astype(BF16)
    logit_grad = logit_sum * (1.0 - gating)

    @pl.loop(0, chunks)
    def _(n):
        cols = pl.ds(pl.multiple_of(n * CHUNK, CHUNK), CHUNK)
        part = dot(both_ref[...], wide_ref[cols, :], NT) + logit_grad * router_ref[mine, cols]
        send_ref[:, :, cols] = interleave(part_ref[:, cols].astype(F32), part)
        rows = rows_ref[:, cols]
        router_out_ref[:, cols] = jnp.sum(logit_grad * rows.astype(F32), axis=0, keepdims=True)
        grad_wide_ref[cols, :] = dot(rows, both_ref[...], TN).astype(BF16)

    def cut(source_ref, matrix, slot, place_in):
        at = slot_base + matrix * MAXB + slot
        row = pl.multiple_of(row_ref[at], 32)
        other = pl.multiple_of(row ^ 32, 32)
        cols = pl.ds(pl.multiple_of(lane_ref[at], 128), 128)
        stay = source_ref[pl.ds(row, 32), cols]
        move = pltpu.roll(source_ref[pl.ds(other, 32), cols], 64, 1)
        packed_ref[place_in] = jnp.where((lane & 64) == 2 * (row & 32), stay, move)

    per = MAXB // OWNERS
    part = packed_ref.shape[0] // OWNERS
    half = 3 * per // 2
    stores = []
    for ahead in (2, 1, 3, 0):
        owner = (me_ref[0] + ahead) & (OWNERS - 1)
        first = ahead * part
        for matrix in range(3):
            source_ref = grad_down_ref if matrix == 2 else grad_wide_ref

            @pl.loop(0, per // UNROLL)
            def _(group, first=first, matrix=matrix, source_ref=source_ref, owner=owner):
                for step in range(UNROLL):
                    s = group * UNROLL + step
                    cut(source_ref, matrix, owner * per + s, first + matrix * per + s)

        start = owner * (D // OWNERS)
        lines = [
            router_out_ref[:, pl.ds(pl.multiple_of(start + at, 128), 128)]
            for at in range(0, D // OWNERS, 128)
        ]
        lines.append(jnp.zeros((32 - len(lines), 128), F32))
        packed_ref[first + 3 * per] = jnp.concatenate(lines, axis=0).astype(BF16)
        cuts = [(0, part)] if ahead == 0 else [(0, half), (half, part - half)]
        for at, (begin, size) in enumerate(cuts):
            number = 0 if ahead == 0 else 2 * ahead - 1 + at
            store = pltpu.make_async_copy(
                packed_ref.at[pl.ds(first + begin, size)], grad_refs[number], out_sems.at[number]
            )
            store.start()
            stores.append(store)
    for store in stores:
        store.wait()


def update_kernel(
    own_ref, left_a_ref, right_a_ref, left_b_ref, right_b_ref,
    own_last_ref, left_last_ref, right_last_ref,
    masters_ref, scores_ref, router_ref, *rest,
    member,
):
    out_ref, scores_out_ref, router_out_ref, lines_ref, total_ref = rest[-5:]
    step, steps = pl.program_id(0), pl.num_programs(0)
    rows = masters_ref.shape[0]

    def gather(left_ref, right_ref):
        for s in range(rows):
            summed = own_ref[s].astype(F32) + left_ref[s].astype(F32) + right_ref[s].astype(F32)
            lines_ref[s // 8, pl.ds(s % 8, 32, stride=8), :] = summed

    @pl.when(step < steps // 2)
    def _():
        gather(left_a_ref, right_a_ref)

    @pl.when(step >= steps // 2)
    def _():
        gather(left_b_ref, right_b_ref)

    for group in range(rows // 8):
        total = jnp.zeros((8, 128), F32)
        here = slice(8 * group, 8 * group + 8)
        for k in range(32):
            cols = slice(128 * k, 128 * k + 128)
            gradient = lines_ref[group, 8 * k : 8 * k + 8, :]
            held = masters_ref[here, cols]
            out_ref[here, cols] = held - LEARN_RATE * gradient
            total = total + held * gradient
        total_ref[pl.ds(pl.multiple_of(step * rows + 8 * group, 8), 8), :] = total

    @pl.when(step == steps - 1)
    def _():
        exact = functools.partial(
            lax.dot_general, dimension_numbers=NT, precision=lax.Precision.HIGHEST, preferred_element_type=F32
        )
        count, experts, per = scores_ref.shape
        mine = iota((experts, per), 0) == member
        for matrix in range(count):
            sums = exact(jnp.ones((8, 128), F32), total_ref[matrix * per : (matrix + 1) * per, :])
            change = jnp.where(mine, jnp.broadcast_to(sums[:1], mine.shape), 0.0)
            scores_out_ref[matrix] = scores_ref[matrix] - SCORE_RATE * change
        last = own_last_ref[0].astype(F32) + left_last_ref[0].astype(F32) + right_last_ref[0].astype(F32)
        last = exact(last, split_matrix(128).astype(F32))
        width = router_ref.shape[1]
        line = jnp.concatenate([last[at : at + 1] for at in range(width // 128)], axis=1)
        held = iota(router_ref.shape, 0) == member
        router_out_ref[...] = jnp.where(held, jnp.broadcast_to(line, router_ref.shape), router_ref[...])


def combine_kernel(picks_ref, *rest, locals_count):
    back_refs = rest[:locals_count]
    out_ref, in_ref, hot_ref = rest[locals_count:]
    count = out_ref.shape[0]

    @pl.when(pl.program_id(0) == 0)
    def _():
        same = one_hot(iota((count, count), 0) == iota((count, count), 1))
        for member in range(locals_count):
            index = pick_columns(picks_ref, member, locals_count)
            hot = one_hot(iota((index.shape[0], count), 1) == index)
            rows = index.shape[0]
            hot_ref[:, member * rows : (member + 1) * rows] = dot(hot, same, TN).astype(BF16)

    split = split_matrix(CHUNK)
    for start in range(0, out_ref.shape[1], CHUNK):
        cols = slice(start, start + CHUNK)
        pairs = [apart(back_ref[:, :, cols]) for back_ref in back_refs]
        out_rows = jnp.concatenate([pair[0].astype(BF16) for pair in pairs], axis=0)
        in_rows = jnp.concatenate([pair[1].astype(BF16) for pair in pairs], axis=0)
        out_ref[:, cols] = dot(hot_ref[...], out_rows).astype(BF16)
        in_ref[:, cols] = dot(dot(hot_ref[...], in_rows).astype(BF16), split, NT).astype(BF16)


def params(mib):
    return pltpu.CompilerParams(vmem_limit_bytes=mib * 1024 * 1024)


def cost(flops, moved):
    return pl.CostEstimate(flops=flops, bytes_accessed=moved, transcendentals=0)


def pick(picks, tokens, grads, locals_count, peers):
    count, width = tokens.shape
    column = pl.BlockSpec((count, STEP), lambda n: (0, n))
    return pl.pallas_call(
        functools.partial(pick_kernel, locals_count=locals_count),
        grid=(width // STEP,),
        in_specs=[pl.BlockSpec(picks.shape, lambda n: (0, 0)), column, column],
        out_specs=[pl.BlockSpec((peers, 16, STEP), lambda n: (0, 0, n))] * locals_count,
        out_shape=[jax.ShapeDtypeStruct((peers, 16, width), BF16)] * locals_count,
        scratch_shapes=[pltpu.VMEM((locals_count * 8 * peers, count), BF16)],
        compiler_params=params(56),
        cost_estimate=cost(0, 1 << 20),
        name="pick",
    )(picks, tokens, grads)


def pack(masters, member, experts):
    mine = masters.shape[0] // experts // 2
    return pl.pallas_call(
        pack_kernel,
        grid=(2,),
        in_specs=[pl.BlockSpec((mine, BS * BS), lambda n: (2 * member + n, 0))],
        out_specs=[pl.BlockSpec((mine, 32, 128), lambda n: (0, 0, 0))] * 2,
        out_shape=[jax.ShapeDtypeStruct((mine, 32, 128), BF16)] * 2,
        scratch_shapes=[pltpu.VMEM((mine // 8, 256, 128), F32)],
        compiler_params=params(56),
        cost_estimate=cost(0, 1 << 20),
        name="pack_%d" % member,
    )(masters)


def run_expert(member, tables, place, pieces, arrived, router_rows):
    peers = arrived.shape[0]
    count = 8 * peers
    whole = pl.BlockSpec(memory_space=pltpu.VMEM)
    scalar = pl.BlockSpec(memory_space=pltpu.SMEM)
    anywhere = pl.BlockSpec(memory_space=pl.ANY)
    part = 3 * MAXB // OWNERS + 1
    half = part // 2
    lengths = [part] + [half, part - half] * 3
    return pl.pallas_call(
        functools.partial(expert_kernel, member=member),
        in_specs=[scalar] * 4 + [whole] * 2 + [anywhere] * len(pieces),
        out_specs=[whole] + [anywhere] * len(lengths),
        out_shape=[jax.ShapeDtypeStruct((peers, 16, D), BF16)]
        + [jax.ShapeDtypeStruct((length, 32, 128), BF16) for length in lengths],
        scratch_shapes=[
            pltpu.VMEM((3 * MAXB + 1, 32, 128), BF16),
            pltpu.VMEM((OWNERS * part, 32, 128), BF16),
            pltpu.SemaphoreType.DMA((len(pieces),)),
            pltpu.SemaphoreType.DMA((len(lengths),)),
            pltpu.VMEM((D, 2 * FF), BF16),
            pltpu.VMEM((FF, D), BF16),
            pltpu.VMEM((count, D), BF16),
            pltpu.VMEM((count, D), BF16),
            pltpu.VMEM((count, 2 * FF), F32),
            pltpu.VMEM((count, D), BF16),
            pltpu.VMEM((count, 2 * FF), BF16),
            pltpu.VMEM((D + BS, 2 * FF), BF16),
            pltpu.VMEM((FF + BS, D), BF16),
            pltpu.VMEM((1, D), F32),
        ],
        compiler_params=params(56),
        cost_estimate=cost(150 * 10**9, 1 << 20),
        name="expert_%d" % member,
    )(*tables, place, arrived, router_rows, *pieces)


def update(member, summed, masters, scores, router_sum, held):
    own, left_a, right_a, left_b, right_b = summed
    mine = own.shape[0] - 1
    steps = 2
    rows = mine // steps
    tile = lambda index: pl.BlockSpec((rows, 32, 128), index)
    early = tile(lambda n: (jnp.minimum(n, steps // 2 - 1), 0, 0))
    late = tile(lambda n: (jnp.maximum(n - steps // 2, 0), 0, 0))
    last = lambda array: pl.BlockSpec((1, 32, 128), lambda n: (array.shape[0] - 1, 0, 0))
    block = pl.BlockSpec((rows, BS * BS), lambda n: (member * steps + n, 0))
    whole = lambda array: pl.BlockSpec(array.shape, lambda n: (0,) * array.ndim)
    return pl.pallas_call(
        functools.partial(update_kernel, member=member),
        grid=(steps,),
        in_specs=[tile(lambda n: (n, 0, 0)), early, early, late, late]
        + [last(own), last(left_b), last(right_b), block, whole(scores), whole(router_sum)]
        + [pl.BlockSpec(memory_space=pl.ANY)] * len(held),
        out_specs=[block, whole(scores), whole(router_sum)],
        out_shape=[
            jax.ShapeDtypeStruct(masters.shape, F32),
            jax.ShapeDtypeStruct(scores.shape, F32),
            jax.ShapeDtypeStruct(router_sum.shape, F32),
        ],
        input_output_aliases={11 + at: at for at in range(len(held))},
        scratch_shapes=[pltpu.VMEM((rows // 8, 256, 128), F32), pltpu.VMEM((mine, 128), F32)],
        compiler_params=params(56),
        cost_estimate=cost(0, 1 << 20),
        name="update_%d" % member,
    )(own, left_a, right_a, left_b, right_b, own, left_b, right_b, masters, scores, router_sum, *held)


def combine(picks, back, count):
    locals_count = len(back)
    peers, _, width = back[0].shape
    column = pl.BlockSpec((count, STEP), lambda n: (0, n))
    return pl.pallas_call(
        functools.partial(combine_kernel, locals_count=locals_count),
        grid=(width // STEP,),
        in_specs=[pl.BlockSpec(picks.shape, lambda n: (0, 0))]
        + [pl.BlockSpec((peers, 16, STEP), lambda n: (0, 0, n))] * locals_count,
        out_specs=[column, column],
        out_shape=[jax.ShapeDtypeStruct((count, width), BF16)] * 2,
        scratch_shapes=[pltpu.VMEM((count, locals_count * 8 * peers), BF16)],
        compiler_params=params(24),
        cost_estimate=cost(150 * 10**9, 1 << 20),
        name="combine",
    )(picks, *back)


def slot_tables(kept, owners, me):
    numbers = jnp.arange(BLOCKS, dtype=jnp.int32)
    slots = jnp.arange(MAXB, dtype=jnp.int32)
    per = MAXB // owners
    matrix = jnp.arange(3, dtype=jnp.int32)[None, :, None]
    ahead = (slots // per - me) % owners
    order = jnp.where(ahead == 0, 0, jnp.where(ahead == owners - 1, 1, ahead + 1))
    place = order * (3 * per) + slots % per + matrix * per
    hits = kept[:, :, None, :] == numbers[None, None, :, None]
    inverse = 3 * MAXB + jnp.sum(jnp.where(hits, place[:, :, None, :] - 3 * MAXB, 0), axis=-1)
    valid = kept < BLOCKS
    block = jnp.where(valid, kept, 0)
    width = jnp.array([FF // BS, FF // BS, D // BS], jnp.int32)[None, :, None]
    block_row, block_col = block // width, block % width
    empty = jnp.where(matrix == 2, FF, D)
    rows = jnp.where(valid, block_row * BS + 32 * (block_col & 1), empty)
    lanes = (block_col >> 1) * 128 + jnp.where(matrix == 1, FF, 0)
    flat = lambda table: table.reshape(-1).astype(jnp.int32)
    return flat(inverse), flat(rows), flat(lanes)


def shift(array, step):
    owners = lax.axis_size("dp")
    return lax.ppermute(array, "dp", [(i, (i + step) % owners) for i in range(owners)])


def gather_first(first, second):
    left_a, right_b = shift(first, 1), shift(second, -1)
    return [first, second, left_a, shift(second, 1), shift(first, -1), right_b]


def gather_second(pieces):
    return list(pieces) + [shift(pieces[2], 1), shift(pieces[5], -1)]


def scatter_first(own, right_a, right_b, far_a, far_b, left_a, left_b):
    moving = [shift(far_a, 1), shift(far_b, -1), shift(right_b, 1), shift(left_a, -1)]
    return own, right_a, left_b, moving


def scatter_second(own, right_a, left_b, moving):
    passing_a, passing_b, from_left_b, from_right_a = moving
    from_left_a = shift(right_a + passing_a, 1)
    from_right_b = shift(left_b + passing_b, -1)
    return own, from_left_a, from_right_a, from_left_b, from_right_b


def body(tokens, out_grad, token_picks, router, kept_blocks, masters, scores):
    locals_count = kept_blocks.shape[0]
    owners = lax.axis_size("dp")
    peers = lax.axis_size("expert")
    me = lax.axis_index("dp").astype(jnp.int32)
    count, width = tokens.shape
    per = masters.shape[2]
    picks = token_picks[0].T
    flat_masters = masters.reshape(locals_count * 3 * per, BS * BS)
    after = lax.optimization_barrier

    def exchange(array):
        return lax.all_to_all(array, "expert", split_axis=0, concat_axis=0, tiled=True)

    sent = list(pick(picks, tokens, out_grad, locals_count, peers))
    sent[0], rest_masters, kept_blocks, router = after((sent[0], flat_masters, kept_blocks, router))
    halves = [pack(rest_masters, member, locals_count) for member in range(locals_count)]
    tables = slot_tables(kept_blocks, owners, me)
    router_rows = router.T.reshape(locals_count, width // BS, 32, 2).transpose(0, 1, 3, 2)
    router_rows = router_rows.reshape(locals_count, width).astype(F32)
    place = me.reshape(1)

    pieces = [gather_first(*halves[0])]
    through, tables, router_rows, halves[1:] = after(((pieces[0][2], pieces[0][5]), tables, router_rows, halves[1:]))
    pieces[0][2], pieces[0][5] = through
    pieces[0] = gather_second(pieces[0])
    arrived = [exchange(sent[0])]
    for member in range(1, locals_count):
        pieces.append(gather_first(*halves[member]))
        rows, arrived[-1] = after((sent[member], arrived[-1]))
        arrived.append(exchange(rows))
    summed, back = [], []
    for member in range(locals_count):
        rows = arrived[member]
        if member:
            rows, send, through = after((rows, send, (pieces[member][2], pieces[member][5])))
            pieces[member][2], pieces[member][5] = through
            pieces[member] = gather_second(pieces[member])
            back.append(exchange(send))
        send, *gradients = run_expert(member, tables, place, pieces[member], rows, router_rows)
        summed.append(scatter_first(*gradients))
    send, back, summed[:-1] = after((send, back, summed[:-1]))
    back.append(exchange(send))
    summed = [scatter_second(*terms) for terms in summed]
    score_sum = scores.transpose(1, 0, 2)
    router_sum = jnp.zeros((locals_count, width // owners), F32)
    held = ()
    for member in range(locals_count - 1):
        new, score_sum, router_sum = update(member, summed[member], flat_masters, score_sum, router_sum, held)
        held = (new,)
    held, picks = after((held, picks))
    layer_out, input_grad = combine(picks, back, count)
    last, layer_out = after((summed[-1], layer_out))
    new, score_sum, router_sum = update(locals_count - 1, last, flat_masters, score_sum, router_sum, held)
    return layer_out, input_grad, new.reshape(masters.shape), score_sum.transpose(1, 0, 2), router_sum.T


def solution(mesh):
    return jax.shard_map(
        body,
        mesh=mesh,
        in_specs=(
            P(("dp", "expert"), None),
            P(("dp", "expert"), None),
            P(("dp", "expert"), None, None),
            P(None, "expert"),
            P("expert", None, None),
            P("expert", None, "dp", None),
            P("expert", None, "dp"),
        ),
        out_specs=(
            P(("dp", "expert"), None),
            P(("dp", "expert"), None),
            P("expert", None, "dp", None),
            P("expert", None, "dp"),
            P("dp", "expert"),
        ),
        check_vma=False,
    )
```

```python
import functools

import jax
import jax.numpy as jnp
from jax import lax
from jax.experimental import pallas as pl
from jax.experimental.pallas import tpu as pltpu
from jax.sharding import PartitionSpec as P

D = 2048
FF = 768
BS = 64
MAXB = 128
OWNERS = 4
BLOCKS = (D // BS) * (FF // BS)
LEARN_RATE = 0.005
SCORE_RATE = 0.05
CHUNK = 256
STEP = 1024
UNROLL = 32
F32 = jnp.float32
BF16 = jnp.bfloat16
NN = (((1,), (0,)), ((), ()))
NT = (((1,), (1,)), ((), ()))
TN = (((0,), (0,)), ((), ()))


def dot(left, right, dims=NN):
    return lax.dot_general(left, right, dims, preferred_element_type=F32)


def iota(shape, dim):
    return lax.broadcasted_iota(jnp.int32, shape, dim)


def one_hot(flag):
    return jnp.where(flag, 1.0, 0.0).astype(BF16)


def split_matrix(size):
    col = iota((size, size), 1)
    source = ((col >> 6) << 6) + 2 * (col & 31) + ((col >> 5) & 1)
    return one_hot(iota((size, size), 0) == source)


def pick_columns(picks_ref, member, locals_count):
    experts = picks_ref.shape[1]
    rows = 8 * experts // locals_count
    expert = (iota((rows, experts), 0) >> 3) * locals_count + member
    spread = one_hot(iota((rows, experts), 1) == expert)
    wide = dot(spread, picks_ref[...].astype(F32).astype(BF16), NT)
    keep = iota(wide.shape, 1) == (iota(wide.shape, 0) & 7)
    return jnp.sum(jnp.where(keep, wide, 0.0), axis=1, keepdims=True).astype(jnp.int32)


def interleave(first, second):
    width = first.shape[1]
    pair = [first.reshape(-1, 8, width), second.reshape(-1, 8, width)]
    return jnp.concatenate(pair, axis=1).astype(BF16)


def apart(block):
    wide = block.astype(F32)
    width = wide.shape[2]
    return wide[:, :8, :].reshape(-1, width), wide[:, 8:, :].reshape(-1, width)


def pick_kernel(picks_ref, tokens_ref, grads_ref, *rest, locals_count):
    out_refs, hot_ref = rest[:locals_count], rest[locals_count]
    rows = hot_ref.shape[0] // locals_count

    @pl.when(pl.program_id(0) == 0)
    def _():
        for member in range(locals_count):
            index = pick_columns(picks_ref, member, locals_count)
            hot_ref[member * rows : (member + 1) * rows, :] = one_hot(
                iota((rows, hot_ref.shape[1]), 1) == index
            )

    split = split_matrix(CHUNK)
    for start in range(0, tokens_ref.shape[1], CHUNK):
        cols = slice(start, start + CHUNK)
        tokens = dot(hot_ref[...], dot(tokens_ref[:, cols], split).astype(BF16))
        grads = dot(hot_ref[...], grads_ref[:, cols])
        for member in range(locals_count):
            mine = slice(member * rows, (member + 1) * rows)
            out_refs[member][:, :, cols] = interleave(tokens[mine], grads[mine])


def pack_kernel(masters_ref, *rest):
    out_refs, lines_ref = rest[:-1], rest[-1]
    for at, out_ref in enumerate(out_refs):

        @pl.when(pl.program_id(0) == at)
        def _(out_ref=out_ref):
            for group in range(masters_ref.shape[0] // 8):
                for k in range(32):
                    lines_ref[group, 8 * k : 8 * k + 8, :] = masters_ref[
                        8 * group : 8 * group + 8, 128 * k : 128 * k + 128
                    ]
                for s in range(8):
                    line = lines_ref[group, pl.ds(s, 32, stride=8), :]
                    out_ref[8 * group + s] = line.astype(BF16)


def expert_kernel(
    inverse_ref, row_ref, lane_ref, me_ref,
    arriving_ref, router_ref, *rest,
    member,
):
    piece_refs, sending_ref, grad_refs = rest[:8], rest[8], rest[9:13]
    (
    copies_ref, packed_ref, arrived_ref, send_ref, sigma_ref, in_sems, out_sems,
    wide_ref, down_ref, rows_ref, grads_ref, pre_ref, part_ref, both_ref,
    grad_wide_ref, grad_down_ref, router_out_ref,
    ) = rest[13:]
    length = piece_refs[0].shape[0]
    loads = [
        pltpu.make_async_copy(piece, copies_ref.at[pl.ds(at * length, length)], in_sems.at[at])
        for at, piece in enumerate(piece_refs)
    ]
    rows_in = pltpu.make_async_copy(arriving_ref, arrived_ref, in_sems.at[len(loads)])
    rows_in.start()
    for load in loads:
        load.start()
    copies_ref[3 * MAXB] = jnp.zeros((32, 128), BF16)
    grad_wide_ref[D:, :] = jnp.zeros((BS, 2 * FF), BF16)
    grad_down_ref[FF:, :] = jnp.zeros((BS, D), BF16)
    base, slot_base = member * 3 * BLOCKS, member * 3 * MAXB
    lane = iota((32, 128), 1)
    half = lane < 64

    count = rows_ref.shape[0]
    chunks = D // CHUNK
    mine = slice(member, member + 1)

    def take(n, logit):
        cols = pl.ds(pl.multiple_of(n * CHUNK, CHUNK), CHUNK)
        rows, grads = apart(arrived_ref[:, :, cols])
        rows_ref[:, cols] = rows.astype(BF16)
        grads_ref[:, cols] = grads.astype(BF16)
        return logit + jnp.sum(rows * router_ref[mine, cols], axis=1, keepdims=True)

    rows_in.wait()
    logit = lax.fori_loop(0, chunks, take, jnp.zeros((count, 1), F32))
    gating = 1.0 / (1.0 + jnp.exp(-logit))

    for load in loads:
        load.wait()

    def place(target_ref, matrix, block, row, col):
        one = copies_ref[inverse_ref[base + matrix * BLOCKS + block]]
        two = copies_ref[inverse_ref[base + matrix * BLOCKS + block + 1]]
        crossed = pltpu.roll(jnp.where(half, two, one), 64, 1)
        target_ref[pl.ds(row, 32), col : col + 128] = jnp.where(half, one, crossed)
        target_ref[pl.ds(row + 32, 32), col : col + 128] = jnp.where(half, crossed, two)

    @pl.loop(0, D // BS)
    def _(r):
        row = pl.multiple_of(r * BS, BS)
        for matrix in range(2):
            for pair in range(FF // BS // 2):
                place(wide_ref, matrix, r * (FF // BS) + 2 * pair, row, matrix * FF + 128 * pair)

    @pl.loop(0, FF // BS)
    def _(r):
        row = pl.multiple_of(r * BS, BS)
        for pair in range(D // BS // 2):
            place(down_ref, 2, r * (D // BS) + 2 * pair, row, 128 * pair)

    @pl.loop(0, 2 * FF // 512)
    def _(n):
        cols = pl.ds(pl.multiple_of(n * 512, 512), 512)
        pre_ref[:, cols] = dot(rows_ref[...], wide_ref[:, cols])

    split = split_matrix(CHUNK)
    hidden_list = []
    for n in range(FF // CHUNK):
        gate_pre = pre_ref[:, n * CHUNK : (n + 1) * CHUNK]
        up_pre = pre_ref[:, FF + n * CHUNK : FF + (n + 1) * CHUNK]
        sigma = 1.0 / (1.0 + jnp.exp(-gate_pre))
        sigma_ref[:, n * CHUNK : (n + 1) * CHUNK] = sigma
        hidden = (gate_pre * sigma * up_pre).astype(BF16)
        hidden_list.append(dot(hidden, split).astype(BF16))
    hidden_split = jnp.concatenate(hidden_list, axis=1)

    @pl.loop(0, D // 512)
    def _(n):
        cols = pl.ds(pl.multiple_of(n * 512, 512), 512)
        part_ref[:, cols] = (gating * dot(hidden_split, down_ref[:, cols])).astype(BF16)
        grads_ref[:, cols] = (gating * grads_ref[:, cols].astype(F32)).astype(BF16)

    logit_sum = jnp.zeros((count, 1), F32)
    for n in range(FF // CHUNK):
        spread = dot(grads_ref[...], down_ref[n * CHUNK : (n + 1) * CHUNK, :], NT)
        high = spread.astype(BF16)
        low = (spread - high.astype(F32)).astype(BF16)
        hidden_grad = dot(high, split, NT) + dot(low, split, NT)
        logit_sum = logit_sum + jnp.sum(
            hidden_list[n].astype(F32) * spread, axis=1, keepdims=True
        )
        gate_pre = pre_ref[:, n * CHUNK : (n + 1) * CHUNK]
        up_pre = pre_ref[:, FF + n * CHUNK : FF + (n + 1) * CHUNK]
        sigma = sigma_ref[:, n * CHUNK : (n + 1) * CHUNK]
        gate_grad = hidden_grad * up_pre * sigma * (1.0 + gate_pre * (1.0 - sigma))
        both_ref[:, n * CHUNK : (n + 1) * CHUNK] = gate_grad.astype(BF16)
        both_ref[:, FF + n * CHUNK : FF + (n + 1) * CHUNK] = (hidden_grad * gate_pre * sigma).astype(BF16)
        grad_down_ref[n * CHUNK : (n + 1) * CHUNK, :] = dot(hidden_list[n], grads_ref[...], TN).astype(BF16)
    logit_grad = logit_sum * (1.0 - gating)

    @pl.loop(0, chunks)
    def _(n):
        cols = pl.ds(pl.multiple_of(n * CHUNK, CHUNK), CHUNK)
        part = dot(both_ref[...], wide_ref[cols, :], NT) + logit_grad * router_ref[mine, cols]
        send_ref[:, :, cols] = interleave(part_ref[:, cols].astype(F32), part)
        rows = rows_ref[:, cols]
        router_out_ref[:, cols] = jnp.sum(logit_grad * rows.astype(F32), axis=0, keepdims=True)
        grad_wide_ref[cols, :] = dot(rows, both_ref[...], TN).astype(BF16)

    rows_out = pltpu.make_async_copy(send_ref, sending_ref, out_sems.at[len(grad_refs)])
    rows_out.start()

    def cut(source_ref, matrix, slot, place_in):
        at = slot_base + matrix * MAXB + slot
        row = pl.multiple_of(row_ref[at], 32)
        other = pl.multiple_of(row ^ 32, 32)
        cols = pl.ds(pl.multiple_of(lane_ref[at], 128), 128)
        stay = source_ref[pl.ds(row, 32), cols]
        move = pltpu.roll(source_ref[pl.ds(other, 32), cols], 64, 1)
        packed_ref[place_in] = jnp.where((lane & 64) == 2 * (row & 32), stay, move)

    per = MAXB // OWNERS
    part = packed_ref.shape[0] // OWNERS
    stores = [rows_out]
    for ahead in (2, 1, 3, 0):
        owner = (me_ref[0] + ahead) & (OWNERS - 1)
        first = ahead * part
        for matrix in range(3):
            source_ref = grad_down_ref if matrix == 2 else grad_wide_ref

            @pl.loop(0, per // UNROLL)
            def _(group, first=first, matrix=matrix, source_ref=source_ref, owner=owner):
                for step in range(UNROLL):
                    s = group * UNROLL + step
                    cut(source_ref, matrix, owner * per + s, first + matrix * per + s)

        start = owner * (D // OWNERS)
        lines = [
            router_out_ref[:, pl.ds(pl.multiple_of(start + at, 128), 128)]
            for at in range(0, D // OWNERS, 128)
        ]
        lines.append(jnp.zeros((32 - len(lines), 128), F32))
        packed_ref[first + 3 * per] = jnp.concatenate(lines, axis=0).astype(BF16)
        store = pltpu.make_async_copy(
            packed_ref.at[pl.ds(first, part)], grad_refs[ahead], out_sems.at[ahead]
        )
        store.start()
        stores.append(store)
    for store in stores:
        store.wait()


def update_kernel(
    own_ref, first_ref, second_ref, own_last_ref, first_last_ref, second_last_ref,
    masters_ref, scores_ref, router_ref, *rest,
    member,
):
    out_ref, scores_out_ref, router_out_ref, lines_ref, total_ref = rest[-5:]
    step, steps = pl.program_id(0), pl.num_programs(0)
    rows = masters_ref.shape[0]
    for s in range(rows):
        summed = own_ref[s].astype(F32) + first_ref[s].astype(F32) + second_ref[s].astype(F32)
        lines_ref[s // 8, pl.ds(s % 8, 32, stride=8), :] = summed

    for group in range(rows // 8):
        total = jnp.zeros((8, 128), F32)
        here = slice(8 * group, 8 * group + 8)
        for k in range(32):
            cols = slice(128 * k, 128 * k + 128)
            gradient = lines_ref[group, 8 * k : 8 * k + 8, :]
            held = masters_ref[here, cols]
            out_ref[here, cols] = held - LEARN_RATE * gradient
            total = total + held * gradient
        total_ref[pl.ds(pl.multiple_of(step * rows + 8 * group, 8), 8), :] = total

    @pl.when(step == steps - 1)
    def _():
        exact = functools.partial(
            lax.dot_general, dimension_numbers=NT, precision=lax.Precision.HIGHEST, preferred_element_type=F32
        )
        count, experts, per = scores_ref.shape
        mine = iota((experts, per), 0) == member
        for matrix in range(count):
            sums = exact(jnp.ones((8, 128), F32), total_ref[matrix * per : (matrix + 1) * per, :])
            change = jnp.where(mine, jnp.broadcast_to(sums[:1], mine.shape), 0.0)
            scores_out_ref[matrix] = scores_ref[matrix] - SCORE_RATE * change
        last = own_last_ref[0].astype(F32) + first_last_ref[0].astype(F32) + second_last_ref[0].astype(F32)
        last = exact(last, split_matrix(128).astype(F32))
        width = router_ref.shape[1]
        line = jnp.concatenate([last[at : at + 1] for at in range(width // 128)], axis=1)
        held = iota(router_ref.shape, 0) == member
        router_out_ref[...] = jnp.where(held, jnp.broadcast_to(line, router_ref.shape), router_ref[...])


def combine_kernel(picks_ref, *rest, locals_count):
    back_refs = rest[:locals_count]
    out_ref, in_ref, hot_ref = rest[locals_count:]
    count = out_ref.shape[0]

    @pl.when(pl.program_id(0) == 0)
    def _():
        same = one_hot(iota((count, count), 0) == iota((count, count), 1))
        for member in range(locals_count):
            index = pick_columns(picks_ref, member, locals_count)
            hot = one_hot(iota((index.shape[0], count), 1) == index)
            rows = index.shape[0]
            hot_ref[:, member * rows : (member + 1) * rows] = dot(hot, same, TN).astype(BF16)

    split = split_matrix(CHUNK)
    for start in range(0, out_ref.shape[1], CHUNK):
        cols = slice(start, start + CHUNK)
        pairs = [apart(back_ref[:, :, cols]) for back_ref in back_refs]
        out_rows = jnp.concatenate([pair[0].astype(BF16) for pair in pairs], axis=0)
        in_rows = jnp.concatenate([pair[1].astype(BF16) for pair in pairs], axis=0)
        out_ref[:, cols] = dot(hot_ref[...], out_rows).astype(BF16)
        in_ref[:, cols] = dot(dot(hot_ref[...], in_rows).astype(BF16), split, NT).astype(BF16)


def params(mib):
    return pltpu.CompilerParams(vmem_limit_bytes=mib * 1024 * 1024)


def cost(flops, moved):
    return pl.CostEstimate(flops=flops, bytes_accessed=moved, transcendentals=0)


def pick(picks, tokens, grads, locals_count, peers):
    count, width = tokens.shape
    column = pl.BlockSpec((count, STEP), lambda n: (0, n))
    return pl.pallas_call(
        functools.partial(pick_kernel, locals_count=locals_count),
        grid=(width // STEP,),
        in_specs=[pl.BlockSpec(picks.shape, lambda n: (0, 0)), column, column],
        out_specs=[pl.BlockSpec((peers, 16, STEP), lambda n: (0, 0, n))] * locals_count,
        out_shape=[jax.ShapeDtypeStruct((peers, 16, width), BF16)] * locals_count,
        scratch_shapes=[pltpu.VMEM((locals_count * 8 * peers, count), BF16)],
        compiler_params=params(56),
        cost_estimate=cost(0, 1 << 20),
        name="pick",
    )(picks, tokens, grads)


def pack(masters, member, experts):
    mine = masters.shape[0] // experts // 2
    return pl.pallas_call(
        pack_kernel,
        grid=(2,),
        in_specs=[pl.BlockSpec((mine, BS * BS), lambda n: (2 * member + n, 0))],
        out_specs=[pl.BlockSpec((mine, 32, 128), lambda n: (0, 0, 0))] * 2,
        out_shape=[jax.ShapeDtypeStruct((mine, 32, 128), BF16)] * 2,
        scratch_shapes=[pltpu.VMEM((mine // 8, 256, 128), F32)],
        compiler_params=params(56),
        cost_estimate=cost(0, 1 << 20),
        name="pack_%d" % member,
    )(masters)


def run_expert(member, tables, place, pieces, arrived, router_rows):
    peers = arrived.shape[0]
    count = 8 * peers
    whole = pl.BlockSpec(memory_space=pltpu.VMEM)
    scalar = pl.BlockSpec(memory_space=pltpu.SMEM)
    anywhere = pl.BlockSpec(memory_space=pl.ANY)
    part = 3 * MAXB // OWNERS + 1
    lengths = [part] * OWNERS
    return pl.pallas_call(
        functools.partial(expert_kernel, member=member),
        in_specs=[scalar] * 4 + [anywhere, whole] + [anywhere] * len(pieces),
        out_specs=[anywhere] * (1 + len(lengths)),
        out_shape=[jax.ShapeDtypeStruct((peers, 16, D), BF16)]
        + [jax.ShapeDtypeStruct((length, 32, 128), BF16) for length in lengths],
        scratch_shapes=[
            pltpu.VMEM((3 * MAXB + 1, 32, 128), BF16),
            pltpu.VMEM((OWNERS * part, 32, 128), BF16),
            pltpu.VMEM((peers, 16, D), BF16),
            pltpu.VMEM((peers, 16, D), BF16),
            pltpu.VMEM((count, FF), F32),
            pltpu.SemaphoreType.DMA((len(pieces) + 1,)),
            pltpu.SemaphoreType.DMA((len(lengths) + 1,)),
            pltpu.VMEM((D, 2 * FF), BF16),
            pltpu.VMEM((FF, D), BF16),
            pltpu.VMEM((count, D), BF16),
            pltpu.VMEM((count, D), BF16),
            pltpu.VMEM((count, 2 * FF), F32),
            pltpu.VMEM((count, D), BF16),
            pltpu.VMEM((count, 2 * FF), BF16),
            pltpu.VMEM((D + BS, 2 * FF), BF16),
            pltpu.VMEM((FF + BS, D), BF16),
            pltpu.VMEM((1, D), F32),
        ],
        compiler_params=params(56),
        cost_estimate=cost(150 * 10**9, 1 << 20),
        name="expert_%d" % member,
    )(*tables, place, arrived, router_rows, *pieces)


def update(member, summed, masters, scores, router_sum, held):
    own, first, second = summed
    mine = own.shape[0] - 1
    steps = 2
    rows = mine // steps
    tile = pl.BlockSpec((rows, 32, 128), lambda n: (n, 0, 0))
    last = pl.BlockSpec((1, 32, 128), lambda n: (mine, 0, 0))
    block = pl.BlockSpec((rows, BS * BS), lambda n: (member * steps + n, 0))
    whole = lambda array: pl.BlockSpec(array.shape, lambda n: (0,) * array.ndim)
    return pl.pallas_call(
        functools.partial(update_kernel, member=member),
        grid=(steps,),
        in_specs=[tile] * 3
        + [last] * 3
        + [block, whole(scores), whole(router_sum)]
        + [pl.BlockSpec(memory_space=pl.ANY)] * len(held),
        out_specs=[block, whole(scores), whole(router_sum)],
        out_shape=[
            jax.ShapeDtypeStruct(masters.shape, F32),
            jax.ShapeDtypeStruct(scores.shape, F32),
            jax.ShapeDtypeStruct(router_sum.shape, F32),
        ],
        input_output_aliases={9 + at: at for at in range(len(held))},
        scratch_shapes=[pltpu.VMEM((rows // 8, 256, 128), F32), pltpu.VMEM((mine, 128), F32)],
        compiler_params=params(56),
        cost_estimate=cost(0, 1 << 20),
        name="update_%d" % member,
    )(own, first, second, own, first, second, masters, scores, router_sum, *held)


def combine(picks, back, count):
    locals_count = len(back)
    peers, _, width = back[0].shape
    column = pl.BlockSpec((count, STEP), lambda n: (0, n))
    return pl.pallas_call(
        functools.partial(combine_kernel, locals_count=locals_count),
        grid=(width // STEP,),
        in_specs=[pl.BlockSpec(picks.shape, lambda n: (0, 0))]
        + [pl.BlockSpec((peers, 16, STEP), lambda n: (0, 0, n))] * locals_count,
        out_specs=[column, column],
        out_shape=[jax.ShapeDtypeStruct((count, width), BF16)] * 2,
        scratch_shapes=[pltpu.VMEM((count, locals_count * 8 * peers), BF16)],
        compiler_params=params(24),
        cost_estimate=cost(150 * 10**9, 1 << 20),
        name="combine",
    )(picks, *back)


def slot_tables(kept, owners, me):
    numbers = jnp.arange(BLOCKS, dtype=jnp.int32)
    slots = jnp.arange(MAXB, dtype=jnp.int32)
    per = MAXB // owners
    matrix = jnp.arange(3, dtype=jnp.int32)[None, :, None]
    ahead = (slots // per - me) % owners
    order = jnp.where(ahead == 0, 0, jnp.where(ahead == owners - 1, 1, ahead + 1))
    place = order * (3 * per) + slots % per + matrix * per
    hits = kept[:, :, None, :] == numbers[None, None, :, None]
    inverse = 3 * MAXB + jnp.sum(jnp.where(hits, place[:, :, None, :] - 3 * MAXB, 0), axis=-1)
    valid = kept < BLOCKS
    block = jnp.where(valid, kept, 0)
    width = jnp.array([FF // BS, FF // BS, D // BS], jnp.int32)[None, :, None]
    block_row, block_col = block // width, block % width
    empty = jnp.where(matrix == 2, FF, D)
    rows = jnp.where(valid, block_row * BS + 32 * (block_col & 1), empty)
    lanes = (block_col >> 1) * 128 + jnp.where(matrix == 1, FF, 0)
    flat = lambda table: table.reshape(-1).astype(jnp.int32)
    return flat(inverse), flat(rows), flat(lanes)


def shift(array, step):
    owners = lax.axis_size("dp")
    return lax.ppermute(array, "dp", [(i, (i + step) % owners) for i in range(owners)])


def gather_first(first, second):
    left_a, right_b = shift(first, 1), shift(second, -1)
    return [first, second, left_a, shift(second, 1), shift(first, -1), right_b]


def gather_second(pieces):
    return list(pieces) + [shift(pieces[2], 1), shift(pieces[5], -1)]


def scatter_first(step, own, right, far, left):
    ahead, behind = (right, left) if step == 1 else (left, right)
    return own, ahead, [shift(far, step), shift(behind, -step)]


def scatter_second(step, own, ahead, moving):
    passing, direct = moving
    return own, direct, shift(ahead + passing, step)


def body(tokens, out_grad, token_picks, router, kept_blocks, masters, scores):
    locals_count = kept_blocks.shape[0]
    owners = lax.axis_size("dp")
    peers = lax.axis_size("expert")
    me = lax.axis_index("dp").astype(jnp.int32)
    count, width = tokens.shape
    per = masters.shape[2]
    picks = token_picks[0].T
    flat_masters = masters.reshape(locals_count * 3 * per, BS * BS)
    after = lax.optimization_barrier

    def exchange(array):
        return lax.all_to_all(array, "expert", split_axis=0, concat_axis=0, tiled=True)

    sent = list(pick(picks, tokens, out_grad, locals_count, peers))
    sent[0], rest_masters, kept_blocks, router = after((sent[0], flat_masters, kept_blocks, router))
    halves = [pack(rest_masters, member, locals_count) for member in range(locals_count)]
    tables = slot_tables(kept_blocks, owners, me)
    router_rows = router.T.reshape(locals_count, width // BS, 32, 2).transpose(0, 1, 3, 2)
    router_rows = router_rows.reshape(locals_count, width).astype(F32)
    place = me.reshape(1)

    pieces = [gather_first(*halves[0])]
    through, tables, router_rows, halves[1:] = after(((pieces[0][2], pieces[0][5]), tables, router_rows, halves[1:]))
    pieces[0][2], pieces[0][5] = through
    pieces[0] = gather_second(pieces[0])
    arrived = [exchange(sent[0])]
    for member in range(1, locals_count):
        pieces.append(gather_first(*halves[member]))
        rows, arrived[-1] = after((sent[member], arrived[-1]))
        arrived.append(exchange(rows))
    summed, back = [], []
    for member in range(locals_count):
        rows = arrived[member]
        if member:
            rows, send, through = after((rows, send, (pieces[member][2], pieces[member][5])))
            pieces[member][2], pieces[member][5] = through
            pieces[member] = gather_second(pieces[member])
            back.append(exchange(send))
        send, *gradients = run_expert(member, tables, place, pieces[member], rows, router_rows)
        summed.append(scatter_first(1 - 2 * (member % 2), *gradients))
    send, back, summed[:-1] = after((send, back, summed[:-1]))
    back.append(exchange(send))
    summed = [scatter_second(1 - 2 * (member % 2), *terms) for member, terms in enumerate(summed)]
    score_sum = scores.transpose(1, 0, 2)
    router_sum = jnp.zeros((locals_count, width // owners), F32)
    held = ()
    for member in range(locals_count - 1):
        new, score_sum, router_sum = update(member, summed[member], flat_masters, score_sum, router_sum, held)
        held = (new,)
    held, picks = after((held, picks))
    layer_out, input_grad = combine(picks, back, count)
    last, layer_out = after((summed[-1], layer_out))
    new, score_sum, router_sum = update(locals_count - 1, last, flat_masters, score_sum, router_sum, held)
    return layer_out, input_grad, new.reshape(masters.shape), score_sum.transpose(1, 0, 2), router_sum.T


def solution(mesh):
    return jax.shard_map(
        body,
        mesh=mesh,
        in_specs=(
            P(("dp", "expert"), None),
            P(("dp", "expert"), None),
            P(("dp", "expert"), None, None),
            P(None, "expert"),
            P("expert", None, None),
            P("expert", None, "dp", None),
            P("expert", None, "dp"),
        ),
        out_specs=(
            P(("dp", "expert"), None),
            P(("dp", "expert"), None),
            P("expert", None, "dp", None),
            P("expert", None, "dp"),
            P("dp", "expert"),
        ),
        check_vma=False,
    )
```

```python
import functools

import jax
import jax.numpy as jnp
from jax import lax
from jax.experimental import pallas as pl
from jax.experimental.pallas import tpu as pltpu
from jax.sharding import PartitionSpec as P

D = 2048
FF = 768
BS = 64
MAXB = 128
OWNERS = 4
BLOCKS = (D // BS) * (FF // BS)
LEARN_RATE = 0.005
SCORE_RATE = 0.05
CHUNK = 256
STEP = 1024
UNROLL = 32
F32 = jnp.float32
BF16 = jnp.bfloat16
NN = (((1,), (0,)), ((), ()))
NT = (((1,), (1,)), ((), ()))
TN = (((0,), (0,)), ((), ()))


def dot(left, right, dims=NN):
    return lax.dot_general(left, right, dims, preferred_element_type=F32)


def iota(shape, dim):
    return lax.broadcasted_iota(jnp.int32, shape, dim)


def one_hot(flag):
    return jnp.where(flag, 1.0, 0.0).astype(BF16)


def split_matrix(size):
    col = iota((size, size), 1)
    source = ((col >> 6) << 6) + 2 * (col & 31) + ((col >> 5) & 1)
    return one_hot(iota((size, size), 0) == source)


def pick_columns(picks_ref, member, locals_count):
    experts = picks_ref.shape[1]
    rows = 8 * experts // locals_count
    expert = (iota((rows, experts), 0) >> 3) * locals_count + member
    spread = one_hot(iota((rows, experts), 1) == expert)
    wide = dot(spread, picks_ref[...].astype(F32).astype(BF16), NT)
    keep = iota(wide.shape, 1) == (iota(wide.shape, 0) & 7)
    return jnp.sum(jnp.where(keep, wide, 0.0), axis=1, keepdims=True).astype(jnp.int32)


def interleave(first, second):
    width = first.shape[1]
    pair = [first.reshape(-1, 8, width), second.reshape(-1, 8, width)]
    return jnp.concatenate(pair, axis=1).astype(BF16)


def apart(block):
    wide = block.astype(F32)
    width = wide.shape[2]
    return wide[:, :8, :].reshape(-1, width), wide[:, 8:, :].reshape(-1, width)


def pick_kernel(picks_ref, tokens_ref, grads_ref, *rest, locals_count):
    out_refs, hot_ref = rest[:locals_count], rest[locals_count]
    rows = hot_ref.shape[0] // locals_count

    @pl.when(pl.program_id(0) == 0)
    def _():
        for member in range(locals_count):
            index = pick_columns(picks_ref, member, locals_count)
            hot_ref[member * rows : (member + 1) * rows, :] = one_hot(
                iota((rows, hot_ref.shape[1]), 1) == index
            )

    split = split_matrix(CHUNK)
    for start in range(0, tokens_ref.shape[1], CHUNK):
        cols = slice(start, start + CHUNK)
        tokens = dot(hot_ref[...], dot(tokens_ref[:, cols], split).astype(BF16))
        grads = dot(hot_ref[...], grads_ref[:, cols])
        for member in range(locals_count):
            mine = slice(member * rows, (member + 1) * rows)
            out_refs[member][:, :, cols] = interleave(tokens[mine], grads[mine])


def pack_kernel(masters_ref, *rest):
    out_refs, lines_ref = rest[:-1], rest[-1]
    for at, out_ref in enumerate(out_refs):

        @pl.when(pl.program_id(0) == at)
        def _(out_ref=out_ref):
            for group in range(masters_ref.shape[0] // 8):
                for k in range(32):
                    lines_ref[group, 8 * k : 8 * k + 8, :] = masters_ref[
                        8 * group : 8 * group + 8, 128 * k : 128 * k + 128
                    ]
                for s in range(8):
                    line = lines_ref[group, pl.ds(s, 32, stride=8), :]
                    out_ref[8 * group + s] = line.astype(BF16)


def expert_kernel(
    inverse_ref, row_ref, lane_ref, me_ref,
    arriving_ref, router_ref, *rest,
    member,
):
    piece_refs, sending_ref, grad_refs = rest[:8], rest[8], rest[9:13]
    (
    copies_ref, packed_ref, arrived_ref, send_ref, sigma_ref, in_sems, out_sems,
    wide_ref, down_ref, rows_ref, grads_ref, pre_ref, part_ref, both_ref,
    grad_wide_ref, grad_down_ref, router_out_ref,
    ) = rest[13:]
    length = piece_refs[0].shape[0]
    loads = [
        pltpu.make_async_copy(piece, copies_ref.at[pl.ds(at * length, length)], in_sems.at[at])
        for at, piece in enumerate(piece_refs)
    ]
    rows_in = pltpu.make_async_copy(arriving_ref, arrived_ref, in_sems.at[len(loads)])
    rows_in.start()
    for load in loads:
        load.start()
    copies_ref[3 * MAXB] = jnp.zeros((32, 128), BF16)
    grad_wide_ref[D:, :] = jnp.zeros((BS, 2 * FF), BF16)
    grad_down_ref[FF:, :] = jnp.zeros((BS, D), BF16)
    base, slot_base = member * 3 * BLOCKS, member * 3 * MAXB
    lane = iota((32, 128), 1)
    half = lane < 64

    count = rows_ref.shape[0]
    chunks = D // CHUNK
    mine = slice(member, member + 1)

    def take(n, logit):
        cols = pl.ds(pl.multiple_of(n * CHUNK, CHUNK), CHUNK)
        rows, grads = apart(arrived_ref[:, :, cols])
        rows_ref[:, cols] = rows.astype(BF16)
        grads_ref[:, cols] = grads.astype(BF16)
        return logit + jnp.sum(rows * router_ref[mine, cols], axis=1, keepdims=True)

    rows_in.wait()
    logit = lax.fori_loop(0, chunks, take, jnp.zeros((count, 1), F32))
    gating = 1.0 / (1.0 + jnp.exp(-logit))

    for load in loads:
        load.wait()

    def place(target_ref, matrix, block, row, col):
        one = copies_ref[inverse_ref[base + matrix * BLOCKS + block]]
        two = copies_ref[inverse_ref[base + matrix * BLOCKS + block + 1]]
        crossed = pltpu.roll(jnp.where(half, two, one), 64, 1)
        target_ref[pl.ds(row, 32), col : col + 128] = jnp.where(half, one, crossed)
        target_ref[pl.ds(row + 32, 32), col : col + 128] = jnp.where(half, crossed, two)

    @pl.loop(0, D // BS)
    def _(r):
        row = pl.multiple_of(r * BS, BS)
        for matrix in range(2):
            for pair in range(FF // BS // 2):
                place(wide_ref, matrix, r * (FF // BS) + 2 * pair, row, matrix * FF + 128 * pair)

    @pl.loop(0, FF // BS)
    def _(r):
        row = pl.multiple_of(r * BS, BS)
        for pair in range(D // BS // 2):
            place(down_ref, 2, r * (D // BS) + 2 * pair, row, 128 * pair)

    @pl.loop(0, 2 * FF // 512)
    def _(n):
        cols = pl.ds(pl.multiple_of(n * 512, 512), 512)
        pre_ref[:, cols] = dot(rows_ref[...], wide_ref[:, cols])

    split = split_matrix(CHUNK)
    hidden_list = []
    for n in range(FF // CHUNK):
        gate_pre = pre_ref[:, n * CHUNK : (n + 1) * CHUNK]
        up_pre = pre_ref[:, FF + n * CHUNK : FF + (n + 1) * CHUNK]
        sigma = 1.0 / (1.0 + jnp.exp(-gate_pre))
        sigma_ref[:, n * CHUNK : (n + 1) * CHUNK] = sigma
        hidden = (gate_pre * sigma * up_pre).astype(BF16)
        hidden_list.append(dot(hidden, split).astype(BF16))
    hidden_split = jnp.concatenate(hidden_list, axis=1)

    @pl.loop(0, D // 512)
    def _(n):
        cols = pl.ds(pl.multiple_of(n * 512, 512), 512)
        part_ref[:, cols] = (gating * dot(hidden_split, down_ref[:, cols])).astype(BF16)
        grads_ref[:, cols] = (gating * grads_ref[:, cols].astype(F32)).astype(BF16)

    logit_sum = jnp.zeros((count, 1), F32)
    for n in range(FF // CHUNK):
        spread = dot(grads_ref[...], down_ref[n * CHUNK : (n + 1) * CHUNK, :], NT)
        high = spread.astype(BF16)
        low = (spread - high.astype(F32)).astype(BF16)
        hidden_grad = dot(high, split, NT) + dot(low, split, NT)
        logit_sum = logit_sum + jnp.sum(
            hidden_list[n].astype(F32) * spread, axis=1, keepdims=True
        )
        gate_pre = pre_ref[:, n * CHUNK : (n + 1) * CHUNK]
        up_pre = pre_ref[:, FF + n * CHUNK : FF + (n + 1) * CHUNK]
        sigma = sigma_ref[:, n * CHUNK : (n + 1) * CHUNK]
        gate_grad = hidden_grad * up_pre * sigma * (1.0 + gate_pre * (1.0 - sigma))
        both_ref[:, n * CHUNK : (n + 1) * CHUNK] = gate_grad.astype(BF16)
        both_ref[:, FF + n * CHUNK : FF + (n + 1) * CHUNK] = (hidden_grad * gate_pre * sigma).astype(BF16)
        grad_down_ref[n * CHUNK : (n + 1) * CHUNK, :] = dot(hidden_list[n], grads_ref[...], TN).astype(BF16)
    logit_grad = logit_sum * (1.0 - gating)

    @pl.loop(0, chunks)
    def _(n):
        cols = pl.ds(pl.multiple_of(n * CHUNK, CHUNK), CHUNK)
        part = dot(both_ref[...], wide_ref[cols, :], NT) + logit_grad * router_ref[mine, cols]
        send_ref[:, :, cols] = interleave(part_ref[:, cols].astype(F32), part)
        rows = rows_ref[:, cols]
        router_out_ref[:, cols] = jnp.sum(logit_grad * rows.astype(F32), axis=0, keepdims=True)
        grad_wide_ref[cols, :] = dot(rows, both_ref[...], TN).astype(BF16)

    rows_out = pltpu.make_async_copy(send_ref, sending_ref, out_sems.at[len(grad_refs)])
    rows_out.start()

    def cut(source_ref, matrix, slot, place_in):
        at = slot_base + matrix * MAXB + slot
        row = pl.multiple_of(row_ref[at], 32)
        other = pl.multiple_of(row ^ 32, 32)
        cols = pl.ds(pl.multiple_of(lane_ref[at], 128), 128)
        stay = source_ref[pl.ds(row, 32), cols]
        move = pltpu.roll(source_ref[pl.ds(other, 32), cols], 64, 1)
        packed_ref[place_in] = jnp.where((lane & 64) == 2 * (row & 32), stay, move)

    per = MAXB // OWNERS
    part = packed_ref.shape[0] // OWNERS
    stores = [rows_out]
    for ahead in (2, 1, 3, 0):
        owner = (me_ref[0] + ahead) & (OWNERS - 1)
        first = ahead * part
        for matrix in range(3):
            source_ref = grad_down_ref if matrix == 2 else grad_wide_ref

            @pl.loop(0, per // UNROLL)
            def _(group, first=first, matrix=matrix, source_ref=source_ref, owner=owner):
                for step in range(UNROLL):
                    s = group * UNROLL + step
                    cut(source_ref, matrix, owner * per + s, first + matrix * per + s)

        start = owner * (D // OWNERS)
        lines = [
            router_out_ref[:, pl.ds(pl.multiple_of(start + at, 128), 128)]
            for at in range(0, D // OWNERS, 128)
        ]
        lines.append(jnp.zeros((32 - len(lines), 128), F32))
        packed_ref[first + 3 * per] = jnp.concatenate(lines, axis=0).astype(BF16)
        store = pltpu.make_async_copy(
            packed_ref.at[pl.ds(first, part)], grad_refs[ahead], out_sems.at[ahead]
        )
        store.start()
        stores.append(store)
    for store in stores:
        store.wait()


def update_kernel(
    own_ref, first_ref, second_ref, own_last_ref, first_last_ref, second_last_ref,
    masters_ref, scores_ref, router_ref, *rest,
    member,
):
    out_ref, scores_out_ref, router_out_ref, lines_ref, total_ref = rest[-5:]
    step, steps = pl.program_id(0), pl.num_programs(0)
    rows = masters_ref.shape[0]
    for s in range(rows):
        summed = own_ref[s].astype(F32) + first_ref[s].astype(F32) + second_ref[s].astype(F32)
        lines_ref[s // 8, pl.ds(s % 8, 32, stride=8), :] = summed

    for group in range(rows // 8):
        total = jnp.zeros((8, 128), F32)
        here = slice(8 * group, 8 * group + 8)
        for k in range(32):
            cols = slice(128 * k, 128 * k + 128)
            gradient = lines_ref[group, 8 * k : 8 * k + 8, :]
            held = masters_ref[here, cols]
            out_ref[here, cols] = held - LEARN_RATE * gradient
            total = total + held * gradient
        total_ref[pl.ds(pl.multiple_of(step * rows + 8 * group, 8), 8), :] = total

    @pl.when(step == steps - 1)
    def _():
        exact = functools.partial(
            lax.dot_general, dimension_numbers=NT, precision=lax.Precision.HIGHEST, preferred_element_type=F32
        )
        count, experts, per = scores_ref.shape
        mine = iota((experts, per), 0) == member
        for matrix in range(count):
            sums = exact(jnp.ones((8, 128), F32), total_ref[matrix * per : (matrix + 1) * per, :])
            change = jnp.where(mine, jnp.broadcast_to(sums[:1], mine.shape), 0.0)
            scores_out_ref[matrix] = scores_ref[matrix] - SCORE_RATE * change
        last = own_last_ref[0].astype(F32) + first_last_ref[0].astype(F32) + second_last_ref[0].astype(F32)
        last = exact(last, split_matrix(128).astype(F32))
        width = router_ref.shape[1]
        line = jnp.concatenate([last[at : at + 1] for at in range(width // 128)], axis=1)
        held = iota(router_ref.shape, 0) == member
        router_out_ref[...] = jnp.where(held, jnp.broadcast_to(line, router_ref.shape), router_ref[...])


def combine_kernel(picks_ref, *rest, locals_count):
    back_refs = rest[:locals_count]
    out_ref, in_ref, hot_ref = rest[locals_count:]
    count = out_ref.shape[0]

    @pl.when(pl.program_id(0) == 0)
    def _():
        same = one_hot(iota((count, count), 0) == iota((count, count), 1))
        for member in range(locals_count):
            index = pick_columns(picks_ref, member, locals_count)
            hot = one_hot(iota((index.shape[0], count), 1) == index)
            rows = index.shape[0]
            hot_ref[:, member * rows : (member + 1) * rows] = dot(hot, same, TN).astype(BF16)

    split = split_matrix(CHUNK)
    for start in range(0, out_ref.shape[1], CHUNK):
        cols = slice(start, start + CHUNK)
        pairs = [apart(back_ref[:, :, cols]) for back_ref in back_refs]
        out_rows = jnp.concatenate([pair[0].astype(BF16) for pair in pairs], axis=0)
        in_rows = jnp.concatenate([pair[1].astype(BF16) for pair in pairs], axis=0)
        out_ref[:, cols] = dot(hot_ref[...], out_rows).astype(BF16)
        in_ref[:, cols] = dot(dot(hot_ref[...], in_rows).astype(BF16), split, NT).astype(BF16)


def params(mib):
    return pltpu.CompilerParams(vmem_limit_bytes=mib * 1024 * 1024)


def cost(flops, moved):
    return pl.CostEstimate(flops=flops, bytes_accessed=moved, transcendentals=0)


def pick(picks, tokens, grads, locals_count, peers):
    count, width = tokens.shape
    column = pl.BlockSpec((count, STEP), lambda n: (0, n))
    return pl.pallas_call(
        functools.partial(pick_kernel, locals_count=locals_count),
        grid=(width // STEP,),
        in_specs=[pl.BlockSpec(picks.shape, lambda n: (0, 0)), column, column],
        out_specs=[pl.BlockSpec((peers, 16, STEP), lambda n: (0, 0, n))] * locals_count,
        out_shape=[jax.ShapeDtypeStruct((peers, 16, width), BF16)] * locals_count,
        scratch_shapes=[pltpu.VMEM((locals_count * 8 * peers, count), BF16)],
        compiler_params=params(56),
        cost_estimate=cost(0, 1 << 20),
        name="pick",
    )(picks, tokens, grads)


def pack(masters, member, experts):
    mine = masters.shape[0] // experts // 2
    return pl.pallas_call(
        pack_kernel,
        grid=(2,),
        in_specs=[pl.BlockSpec((mine, BS * BS), lambda n: (2 * member + n, 0))],
        out_specs=[pl.BlockSpec((mine, 32, 128), lambda n: (0, 0, 0))] * 2,
        out_shape=[jax.ShapeDtypeStruct((mine, 32, 128), BF16)] * 2,
        scratch_shapes=[pltpu.VMEM((mine // 8, 256, 128), F32)],
        compiler_params=params(56),
        cost_estimate=cost(0, 1 << 20),
        name="pack_%d" % member,
    )(masters)


def run_expert(member, tables, place, pieces, arrived, router_rows):
    peers = arrived.shape[0]
    count = 8 * peers
    whole = pl.BlockSpec(memory_space=pltpu.VMEM)
    scalar = pl.BlockSpec(memory_space=pltpu.SMEM)
    anywhere = pl.BlockSpec(memory_space=pl.ANY)
    part = 3 * MAXB // OWNERS + 1
    lengths = [part] * OWNERS
    return pl.pallas_call(
        functools.partial(expert_kernel, member=member),
        in_specs=[scalar] * 4 + [anywhere, whole] + [anywhere] * len(pieces),
        out_specs=[anywhere] * (1 + len(lengths)),
        out_shape=[jax.ShapeDtypeStruct((peers, 16, D), BF16)]
        + [jax.ShapeDtypeStruct((length, 32, 128), BF16) for length in lengths],
        scratch_shapes=[
            pltpu.VMEM((3 * MAXB + 1, 32, 128), BF16),
            pltpu.VMEM((OWNERS * part, 32, 128), BF16),
            pltpu.VMEM((peers, 16, D), BF16),
            pltpu.VMEM((peers, 16, D), BF16),
            pltpu.VMEM((count, FF), F32),
            pltpu.SemaphoreType.DMA((len(pieces) + 1,)),
            pltpu.SemaphoreType.DMA((len(lengths) + 1,)),
            pltpu.VMEM((D, 2 * FF), BF16),
            pltpu.VMEM((FF, D), BF16),
            pltpu.VMEM((count, D), BF16),
            pltpu.VMEM((count, D), BF16),
            pltpu.VMEM((count, 2 * FF), F32),
            pltpu.VMEM((count, D), BF16),
            pltpu.VMEM((count, 2 * FF), BF16),
            pltpu.VMEM((D + BS, 2 * FF), BF16),
            pltpu.VMEM((FF + BS, D), BF16),
            pltpu.VMEM((1, D), F32),
        ],
        compiler_params=params(46),
        cost_estimate=cost(150 * 10**9, 1 << 20),
        name="expert_%d" % member,
    )(*tables, place, arrived, router_rows, *pieces)


def update(member, summed, masters, scores, router_sum, held):
    own, first, second = summed
    mine = own.shape[0] - 1
    steps = 2
    rows = mine // steps
    tile = pl.BlockSpec((rows, 32, 128), lambda n: (n, 0, 0))
    last = pl.BlockSpec((1, 32, 128), lambda n: (mine, 0, 0))
    block = pl.BlockSpec((rows, BS * BS), lambda n: (member * steps + n, 0))
    whole = lambda array: pl.BlockSpec(array.shape, lambda n: (0,) * array.ndim)
    return pl.pallas_call(
        functools.partial(update_kernel, member=member),
        grid=(steps,),
        in_specs=[tile] * 3
        + [last] * 3
        + [block, whole(scores), whole(router_sum)]
        + [pl.BlockSpec(memory_space=pl.ANY)] * len(held),
        out_specs=[block, whole(scores), whole(router_sum)],
        out_shape=[
            jax.ShapeDtypeStruct(masters.shape, F32),
            jax.ShapeDtypeStruct(scores.shape, F32),
            jax.ShapeDtypeStruct(router_sum.shape, F32),
        ],
        input_output_aliases={9 + at: at for at in range(len(held))},
        scratch_shapes=[pltpu.VMEM((rows // 8, 256, 128), F32), pltpu.VMEM((mine, 128), F32)],
        compiler_params=params(56),
        cost_estimate=cost(0, 1 << 20),
        name="update_%d" % member,
    )(own, first, second, own, first, second, masters, scores, router_sum, *held)


def combine(picks, back, count):
    locals_count = len(back)
    peers, _, width = back[0].shape
    column = pl.BlockSpec((count, STEP), lambda n: (0, n))
    return pl.pallas_call(
        functools.partial(combine_kernel, locals_count=locals_count),
        grid=(width // STEP,),
        in_specs=[pl.BlockSpec(picks.shape, lambda n: (0, 0))]
        + [pl.BlockSpec((peers, 16, STEP), lambda n: (0, 0, n))] * locals_count,
        out_specs=[column, column],
        out_shape=[jax.ShapeDtypeStruct((count, width), BF16)] * 2,
        scratch_shapes=[pltpu.VMEM((count, locals_count * 8 * peers), BF16)],
        compiler_params=params(24),
        cost_estimate=cost(150 * 10**9, 1 << 20),
        name="combine",
    )(picks, *back)


def slot_tables(kept, owners, me):
    numbers = jnp.arange(BLOCKS, dtype=jnp.int32)
    slots = jnp.arange(MAXB, dtype=jnp.int32)
    per = MAXB // owners
    matrix = jnp.arange(3, dtype=jnp.int32)[None, :, None]
    ahead = (slots // per - me) % owners
    order = jnp.where(ahead == 0, 0, jnp.where(ahead == owners - 1, 1, ahead + 1))
    place = order * (3 * per) + slots % per + matrix * per
    hits = kept[:, :, None, :] == numbers[None, None, :, None]
    inverse = 3 * MAXB + jnp.sum(jnp.where(hits, place[:, :, None, :] - 3 * MAXB, 0), axis=-1)
    valid = kept < BLOCKS
    block = jnp.where(valid, kept, 0)
    width = jnp.array([FF // BS, FF // BS, D // BS], jnp.int32)[None, :, None]
    block_row, block_col = block // width, block % width
    empty = jnp.where(matrix == 2, FF, D)
    rows = jnp.where(valid, block_row * BS + 32 * (block_col & 1), empty)
    lanes = (block_col >> 1) * 128 + jnp.where(matrix == 1, FF, 0)
    flat = lambda table: table.reshape(-1).astype(jnp.int32)
    return flat(inverse), flat(rows), flat(lanes)


def shift(array, step):
    owners = lax.axis_size("dp")
    return lax.ppermute(array, "dp", [(i, (i + step) % owners) for i in range(owners)])


def gather_first(first, second):
    left_a, right_b = shift(first, 1), shift(second, -1)
    return [first, second, left_a, shift(second, 1), shift(first, -1), right_b]


def gather_second(pieces):
    return list(pieces) + [shift(pieces[2], 1), shift(pieces[5], -1)]


def scatter_first(step, own, right, far, left):
    ahead, behind = (right, left) if step == 1 else (left, right)
    return own, ahead, [shift(far, step), shift(behind, -step)]


def scatter_second(step, own, ahead, moving):
    passing, direct = moving
    return own, direct, shift(ahead + passing, step)


def body(tokens, out_grad, token_picks, router, kept_blocks, masters, scores):
    locals_count = kept_blocks.shape[0]
    owners = lax.axis_size("dp")
    peers = lax.axis_size("expert")
    me = lax.axis_index("dp").astype(jnp.int32)
    count, width = tokens.shape
    per = masters.shape[2]
    picks = token_picks[0].T
    flat_masters = masters.reshape(locals_count * 3 * per, BS * BS)
    after = lax.optimization_barrier

    def exchange(array):
        return lax.all_to_all(array, "expert", split_axis=0, concat_axis=0, tiled=True)

    sent = list(pick(picks, tokens, out_grad, locals_count, peers))
    sent[0], rest_masters, kept_blocks, router = after((sent[0], flat_masters, kept_blocks, router))
    halves = [pack(rest_masters, member, locals_count) for member in range(locals_count)]
    tables = slot_tables(kept_blocks, owners, me)
    router_rows = router.T.reshape(locals_count, width // BS, 32, 2).transpose(0, 1, 3, 2)
    router_rows = router_rows.reshape(locals_count, width).astype(F32)
    place = me.reshape(1)

    pieces = [gather_first(*halves[0])]
    through, tables, router_rows, halves[1:] = after(((pieces[0][2], pieces[0][5]), tables, router_rows, halves[1:]))
    pieces[0][2], pieces[0][5] = through
    pieces[0] = gather_second(pieces[0])
    arrived = [exchange(sent[0])]
    for member in range(1, locals_count):
        pieces.append(gather_first(*halves[member]))
        rows, arrived[-1] = after((sent[member], arrived[-1]))
        arrived.append(exchange(rows))
    summed, back = [], []
    for member in range(locals_count):
        rows = arrived[member]
        if member:
            rows, send, through = after((rows, send, (pieces[member][2], pieces[member][5])))
            pieces[member][2], pieces[member][5] = through
            pieces[member] = gather_second(pieces[member])
            back.append(exchange(send))
        send, *gradients = run_expert(member, tables, place, pieces[member], rows, router_rows)
        summed.append(scatter_first(1 - 2 * (member % 2), *gradients))
    send, back, summed[:-1] = after((send, back, summed[:-1]))
    back.append(exchange(send))
    summed = [scatter_second(1 - 2 * (member % 2), *terms) for member, terms in enumerate(summed)]
    score_sum = scores.transpose(1, 0, 2)
    router_sum = jnp.zeros((locals_count, width // owners), F32)
    held = ()
    for member in range(locals_count - 1):
        new, score_sum, router_sum = update(member, summed[member], flat_masters, score_sum, router_sum, held)
        held = (new,)
    held, picks = after((held, picks))
    layer_out, input_grad = combine(picks, back, count)
    last, layer_out = after((summed[-1], layer_out))
    new, score_sum, router_sum = update(locals_count - 1, last, flat_masters, score_sum, router_sum, held)
    return layer_out, input_grad, new.reshape(masters.shape), score_sum.transpose(1, 0, 2), router_sum.T


def solution(mesh):
    return jax.shard_map(
        body,
        mesh=mesh,
        in_specs=(
            P(("dp", "expert"), None),
            P(("dp", "expert"), None),
            P(("dp", "expert"), None, None),
            P(None, "expert"),
            P("expert", None, None),
            P("expert", None, "dp", None),
            P("expert", None, "dp"),
        ),
        out_specs=(
            P(("dp", "expert"), None),
            P(("dp", "expert"), None),
            P("expert", None, "dp", None),
            P("expert", None, "dp"),
            P("dp", "expert"),
        ),
        check_vma=False,
    )
```

```python
import functools

import jax
import jax.numpy as jnp
from jax import lax
from jax.experimental import pallas as pl
from jax.experimental.pallas import tpu as pltpu
from jax.sharding import PartitionSpec as P

D = 2048
FF = 768
BS = 64
MAXB = 128
OWNERS = 4
BLOCKS = (D // BS) * (FF // BS)
LEARN_RATE = 0.005
SCORE_RATE = 0.05
CHUNK = 256
STEP = 1024
UNROLL = 32
F32 = jnp.float32
BF16 = jnp.bfloat16
NN = (((1,), (0,)), ((), ()))
NT = (((1,), (1,)), ((), ()))
TN = (((0,), (0,)), ((), ()))


def dot(left, right, dims=NN):
    return lax.dot_general(left, right, dims, preferred_element_type=F32)


def iota(shape, dim):
    return lax.broadcasted_iota(jnp.int32, shape, dim)


def one_hot(flag):
    return jnp.where(flag, 1.0, 0.0).astype(BF16)


def split_matrix(size):
    col = iota((size, size), 1)
    source = ((col >> 6) << 6) + 2 * (col & 31) + ((col >> 5) & 1)
    return one_hot(iota((size, size), 0) == source)


def pick_columns(picks_ref, member, locals_count):
    experts = picks_ref.shape[1]
    rows = 8 * experts // locals_count
    expert = (iota((rows, experts), 0) >> 3) * locals_count + member
    spread = one_hot(iota((rows, experts), 1) == expert)
    wide = dot(spread, picks_ref[...].astype(F32).astype(BF16), NT)
    keep = iota(wide.shape, 1) == (iota(wide.shape, 0) & 7)
    return jnp.sum(jnp.where(keep, wide, 0.0), axis=1, keepdims=True).astype(jnp.int32)


def interleave(first, second):
    width = first.shape[1]
    pair = [first.reshape(-1, 8, width), second.reshape(-1, 8, width)]
    return jnp.concatenate(pair, axis=1).astype(BF16)


def apart(block):
    wide = block.astype(F32)
    width = wide.shape[2]
    return wide[:, :8, :].reshape(-1, width), wide[:, 8:, :].reshape(-1, width)


def pick_kernel(picks_ref, tokens_ref, grads_ref, *rest, locals_count):
    out_refs, hot_ref = rest[:locals_count], rest[locals_count]
    rows = hot_ref.shape[0] // locals_count

    @pl.when(pl.program_id(0) == 0)
    def _():
        for member in range(locals_count):
            index = pick_columns(picks_ref, member, locals_count)
            hot_ref[member * rows : (member + 1) * rows, :] = one_hot(
                iota((rows, hot_ref.shape[1]), 1) == index
            )

    split = split_matrix(CHUNK)
    for start in range(0, tokens_ref.shape[1], CHUNK):
        cols = slice(start, start + CHUNK)
        tokens = dot(hot_ref[...], dot(tokens_ref[:, cols], split).astype(BF16))
        grads = dot(hot_ref[...], grads_ref[:, cols])
        for member in range(locals_count):
            mine = slice(member * rows, (member + 1) * rows)
            out_refs[member][:, :, cols] = interleave(tokens[mine], grads[mine])


def pack_kernel(masters_ref, *rest):
    out_refs, lines_ref = rest[:-1], rest[-1]
    for at, out_ref in enumerate(out_refs):

        @pl.when(pl.program_id(0) == at)
        def _(out_ref=out_ref):
            for group in range(masters_ref.shape[0] // 8):
                for k in range(32):
                    lines_ref[group, 8 * k : 8 * k + 8, :] = masters_ref[
                        8 * group : 8 * group + 8, 128 * k : 128 * k + 128
                    ]
                for s in range(8):
                    line = lines_ref[group, pl.ds(s, 32, stride=8), :]
                    out_ref[8 * group + s] = line.astype(BF16)


def expert_kernel(
    inverse_ref, row_ref, lane_ref, me_ref,
    arriving_ref, router_ref, *rest,
    member,
):
    piece_refs, sending_ref, grad_refs = rest[:8], rest[8], rest[9:13]
    (
    copies_ref, packed_ref, arrived_ref, send_ref, sigma_ref, in_sems, out_sems,
    wide_ref, down_ref, rows_ref, grads_ref, pre_ref, part_ref, both_ref,
    grad_wide_ref, grad_down_ref, router_out_ref,
    ) = rest[13:]
    length = piece_refs[0].shape[0]
    loads = [
        pltpu.make_async_copy(piece, copies_ref.at[pl.ds(at * length, length)], in_sems.at[at])
        for at, piece in enumerate(piece_refs)
    ]
    rows_in = pltpu.make_async_copy(arriving_ref, arrived_ref, in_sems.at[len(loads)])
    rows_in.start()
    for load in loads:
        load.start()
    copies_ref[3 * MAXB] = jnp.zeros((32, 128), BF16)
    grad_wide_ref[D:, :] = jnp.zeros((BS, 2 * FF), BF16)
    grad_down_ref[FF:, :] = jnp.zeros((BS, D), BF16)
    base, slot_base = member * 3 * BLOCKS, member * 3 * MAXB
    lane = iota((32, 128), 1)
    half = lane < 64

    count = rows_ref.shape[0]
    chunks = D // CHUNK
    mine = slice(member, member + 1)

    def take(n, logit):
        cols = pl.ds(pl.multiple_of(n * CHUNK, CHUNK), CHUNK)
        rows, grads = apart(arrived_ref[:, :, cols])
        rows_ref[:, cols] = rows.astype(BF16)
        grads_ref[:, cols] = grads.astype(BF16)
        return logit + jnp.sum(rows * router_ref[mine, cols], axis=1, keepdims=True)

    rows_in.wait()
    logit = lax.fori_loop(0, chunks, take, jnp.zeros((count, 1), F32))
    gating = 1.0 / (1.0 + jnp.exp(-logit))

    for load in loads:
        load.wait()

    def place(target_ref, matrix, block, row, col):
        one = copies_ref[inverse_ref[base + matrix * BLOCKS + block]]
        two = copies_ref[inverse_ref[base + matrix * BLOCKS + block + 1]]
        crossed = pltpu.roll(jnp.where(half, two, one), 64, 1)
        target_ref[pl.ds(row, 32), col : col + 128] = jnp.where(half, one, crossed)
        target_ref[pl.ds(row + 32, 32), col : col + 128] = jnp.where(half, crossed, two)

    @pl.loop(0, D // BS, unroll=2)
    def _(r):
        row = pl.multiple_of(r * BS, BS)
        for matrix in range(2):
            for pair in range(FF // BS // 2):
                place(wide_ref, matrix, r * (FF // BS) + 2 * pair, row, matrix * FF + 128 * pair)

    @pl.loop(0, FF // BS, unroll=2)
    def _(r):
        row = pl.multiple_of(r * BS, BS)
        for pair in range(D // BS // 2):
            place(down_ref, 2, r * (D // BS) + 2 * pair, row, 128 * pair)

    @pl.loop(0, 2 * FF // 512, unroll=3)
    def _(n):
        cols = pl.ds(pl.multiple_of(n * 512, 512), 512)
        pre_ref[:, cols] = dot(rows_ref[...], wide_ref[:, cols])

    split = split_matrix(CHUNK)
    hidden_list = []
    for n in range(FF // CHUNK):
        gate_pre = pre_ref[:, n * CHUNK : (n + 1) * CHUNK]
        up_pre = pre_ref[:, FF + n * CHUNK : FF + (n + 1) * CHUNK]
        sigma = 1.0 / (1.0 + jnp.exp(-gate_pre))
        sigma_ref[:, n * CHUNK : (n + 1) * CHUNK] = sigma
        hidden = (gate_pre * sigma * up_pre).astype(BF16)
        hidden_list.append(dot(hidden, split).astype(BF16))
    hidden_split = jnp.concatenate(hidden_list, axis=1)

    @pl.loop(0, D // 512)
    def _(n):
        cols = pl.ds(pl.multiple_of(n * 512, 512), 512)
        part_ref[:, cols] = (gating * dot(hidden_split, down_ref[:, cols])).astype(BF16)
        grads_ref[:, cols] = (gating * grads_ref[:, cols].astype(F32)).astype(BF16)

    logit_sum = jnp.zeros((count, 1), F32)
    for n in range(FF // CHUNK):
        spread = dot(grads_ref[...], down_ref[n * CHUNK : (n + 1) * CHUNK, :], NT)
        high = spread.astype(BF16)
        low = (spread - high.astype(F32)).astype(BF16)
        hidden_grad = dot(high, split, NT) + dot(low, split, NT)
        logit_sum = logit_sum + jnp.sum(
            hidden_list[n].astype(F32) * spread, axis=1, keepdims=True
        )
        gate_pre = pre_ref[:, n * CHUNK : (n + 1) * CHUNK]
        up_pre = pre_ref[:, FF + n * CHUNK : FF + (n + 1) * CHUNK]
        sigma = sigma_ref[:, n * CHUNK : (n + 1) * CHUNK]
        gate_grad = hidden_grad * up_pre * sigma * (1.0 + gate_pre * (1.0 - sigma))
        both_ref[:, n * CHUNK : (n + 1) * CHUNK] = gate_grad.astype(BF16)
        both_ref[:, FF + n * CHUNK : FF + (n + 1) * CHUNK] = (hidden_grad * gate_pre * sigma).astype(BF16)
        grad_down_ref[n * CHUNK : (n + 1) * CHUNK, :] = dot(hidden_list[n], grads_ref[...], TN).astype(BF16)
    logit_grad = logit_sum * (1.0 - gating)

    @pl.loop(0, chunks)
    def _(n):
        cols = pl.ds(pl.multiple_of(n * CHUNK, CHUNK), CHUNK)
        part = dot(both_ref[...], wide_ref[cols, :], NT) + logit_grad * router_ref[mine, cols]
        send_ref[:, :, cols] = interleave(part_ref[:, cols].astype(F32), part)
        rows = rows_ref[:, cols]
        router_out_ref[:, cols] = jnp.sum(logit_grad * rows.astype(F32), axis=0, keepdims=True)
        grad_wide_ref[cols, :] = dot(rows, both_ref[...], TN).astype(BF16)

    rows_out = pltpu.make_async_copy(send_ref, sending_ref, out_sems.at[len(grad_refs)])
    rows_out.start()

    def cut(source_ref, matrix, slot, place_in):
        at = slot_base + matrix * MAXB + slot
        row = pl.multiple_of(row_ref[at], 32)
        other = pl.multiple_of(row ^ 32, 32)
        cols = pl.ds(pl.multiple_of(lane_ref[at], 128), 128)
        stay = source_ref[pl.ds(row, 32), cols]
        move = pltpu.roll(source_ref[pl.ds(other, 32), cols], 64, 1)
        packed_ref[place_in] = jnp.where((lane & 64) == 2 * (row & 32), stay, move)

    per = MAXB // OWNERS
    part = packed_ref.shape[0] // OWNERS
    stores = [rows_out]
    for ahead in (2, 1, 3, 0):
        owner = (me_ref[0] + ahead) & (OWNERS - 1)
        first = ahead * part
        for matrix in range(3):
            source_ref = grad_down_ref if matrix == 2 else grad_wide_ref

            @pl.loop(0, per // UNROLL)
            def _(group, first=first, matrix=matrix, source_ref=source_ref, owner=owner):
                for step in range(UNROLL):
                    s = group * UNROLL + step
                    cut(source_ref, matrix, owner * per + s, first + matrix * per + s)

        start = owner * (D // OWNERS)
        lines = [
            router_out_ref[:, pl.ds(pl.multiple_of(start + at, 128), 128)]
            for at in range(0, D // OWNERS, 128)
        ]
        lines.append(jnp.zeros((32 - len(lines), 128), F32))
        packed_ref[first + 3 * per] = jnp.concatenate(lines, axis=0).astype(BF16)
        store = pltpu.make_async_copy(
            packed_ref.at[pl.ds(first, part)], grad_refs[ahead], out_sems.at[ahead]
        )
        store.start()
        stores.append(store)
    for store in stores:
        store.wait()


def update_kernel(
    own_ref, first_ref, second_ref, own_last_ref, first_last_ref, second_last_ref,
    masters_ref, scores_ref, router_ref, *rest,
    member,
):
    out_ref, scores_out_ref, router_out_ref, lines_ref, total_ref = rest[-5:]
    step, steps = pl.program_id(0), pl.num_programs(0)
    rows = masters_ref.shape[0]
    for s in range(rows):
        summed = own_ref[s].astype(F32) + first_ref[s].astype(F32) + second_ref[s].astype(F32)
        lines_ref[s // 8, pl.ds(s % 8, 32, stride=8), :] = summed

    for group in range(rows // 8):
        total = jnp.zeros((8, 128), F32)
        here = slice(8 * group, 8 * group + 8)
        for k in range(32):
            cols = slice(128 * k, 128 * k + 128)
            gradient = lines_ref[group, 8 * k : 8 * k + 8, :]
            held = masters_ref[here, cols]
            out_ref[here, cols] = held - LEARN_RATE * gradient
            total = total + held * gradient
        total_ref[pl.ds(pl.multiple_of(step * rows + 8 * group, 8), 8), :] = total

    @pl.when(step == steps - 1)
    def _():
        exact = functools.partial(
            lax.dot_general, dimension_numbers=NT, precision=lax.Precision.HIGHEST, preferred_element_type=F32
        )
        count, experts, per = scores_ref.shape
        mine = iota((experts, per), 0) == member
        for matrix in range(count):
            sums = exact(jnp.ones((8, 128), F32), total_ref[matrix * per : (matrix + 1) * per, :])
            change = jnp.where(mine, jnp.broadcast_to(sums[:1], mine.shape), 0.0)
            scores_out_ref[matrix] = scores_ref[matrix] - SCORE_RATE * change
        last = own_last_ref[0].astype(F32) + first_last_ref[0].astype(F32) + second_last_ref[0].astype(F32)
        last = exact(last, split_matrix(128).astype(F32))
        width = router_ref.shape[1]
        line = jnp.concatenate([last[at : at + 1] for at in range(width // 128)], axis=1)
        held = iota(router_ref.shape, 0) == member
        router_out_ref[...] = jnp.where(held, jnp.broadcast_to(line, router_ref.shape), router_ref[...])


def combine_kernel(picks_ref, *rest, locals_count):
    back_refs = rest[:locals_count]
    out_ref, in_ref, hot_ref = rest[locals_count:]
    count = out_ref.shape[0]

    @pl.when(pl.program_id(0) == 0)
    def _():
        same = one_hot(iota((count, count), 0) == iota((count, count), 1))
        for member in range(locals_count):
            index = pick_columns(picks_ref, member, locals_count)
            hot = one_hot(iota((index.shape[0], count), 1) == index)
            rows = index.shape[0]
            hot_ref[:, member * rows : (member + 1) * rows] = dot(hot, same, TN).astype(BF16)

    split = split_matrix(CHUNK)
    for start in range(0, out_ref.shape[1], CHUNK):
        cols = slice(start, start + CHUNK)
        pairs = [apart(back_ref[:, :, cols]) for back_ref in back_refs]
        out_rows = jnp.concatenate([pair[0].astype(BF16) for pair in pairs], axis=0)
        in_rows = jnp.concatenate([pair[1].astype(BF16) for pair in pairs], axis=0)
        out_ref[:, cols] = dot(hot_ref[...], out_rows).astype(BF16)
        in_ref[:, cols] = dot(dot(hot_ref[...], in_rows).astype(BF16), split, NT).astype(BF16)


def params(mib):
    return pltpu.CompilerParams(vmem_limit_bytes=mib * 1024 * 1024)


def cost(flops, moved):
    return pl.CostEstimate(flops=flops, bytes_accessed=moved, transcendentals=0)


def pick(picks, tokens, grads, locals_count, peers):
    count, width = tokens.shape
    column = pl.BlockSpec((count, STEP), lambda n: (0, n))
    return pl.pallas_call(
        functools.partial(pick_kernel, locals_count=locals_count),
        grid=(width // STEP,),
        in_specs=[pl.BlockSpec(picks.shape, lambda n: (0, 0)), column, column],
        out_specs=[pl.BlockSpec((peers, 16, STEP), lambda n: (0, 0, n))] * locals_count,
        out_shape=[jax.ShapeDtypeStruct((peers, 16, width), BF16)] * locals_count,
        scratch_shapes=[pltpu.VMEM((locals_count * 8 * peers, count), BF16)],
        compiler_params=params(56),
        cost_estimate=cost(0, 1 << 20),
        name="pick",
    )(picks, tokens, grads)


def pack(masters, member, experts):
    mine = masters.shape[0] // experts // 2
    return pl.pallas_call(
        pack_kernel,
        grid=(2,),
        in_specs=[pl.BlockSpec((mine, BS * BS), lambda n: (2 * member + n, 0))],
        out_specs=[pl.BlockSpec((mine, 32, 128), lambda n: (0, 0, 0))] * 2,
        out_shape=[jax.ShapeDtypeStruct((mine, 32, 128), BF16)] * 2,
        scratch_shapes=[pltpu.VMEM((mine // 8, 256, 128), F32)],
        compiler_params=params(56),
        cost_estimate=cost(0, 1 << 20),
        name="pack_%d" % member,
    )(masters)


def run_expert(member, tables, place, pieces, arrived, router_rows):
    peers = arrived.shape[0]
    count = 8 * peers
    whole = pl.BlockSpec(memory_space=pltpu.VMEM)
    scalar = pl.BlockSpec(memory_space=pltpu.SMEM)
    anywhere = pl.BlockSpec(memory_space=pl.ANY)
    part = 3 * MAXB // OWNERS + 1
    lengths = [part] * OWNERS
    return pl.pallas_call(
        functools.partial(expert_kernel, member=member),
        in_specs=[scalar] * 4 + [anywhere, whole] + [anywhere] * len(pieces),
        out_specs=[anywhere] * (1 + len(lengths)),
        out_shape=[jax.ShapeDtypeStruct((peers, 16, D), BF16)]
        + [jax.ShapeDtypeStruct((length, 32, 128), BF16) for length in lengths],
        scratch_shapes=[
            pltpu.VMEM((3 * MAXB + 1, 32, 128), BF16),
            pltpu.VMEM((OWNERS * part, 32, 128), BF16),
            pltpu.VMEM((peers, 16, D), BF16),
            pltpu.VMEM((peers, 16, D), BF16),
            pltpu.VMEM((count, FF), F32),
            pltpu.SemaphoreType.DMA((len(pieces) + 1,)),
            pltpu.SemaphoreType.DMA((len(lengths) + 1,)),
            pltpu.VMEM((D, 2 * FF), BF16),
            pltpu.VMEM((FF, D), BF16),
            pltpu.VMEM((count, D), BF16),
            pltpu.VMEM((count, D), BF16),
            pltpu.VMEM((count, 2 * FF), F32),
            pltpu.VMEM((count, D), BF16),
            pltpu.VMEM((count, 2 * FF), BF16),
            pltpu.VMEM((D + BS, 2 * FF), BF16),
            pltpu.VMEM((FF + BS, D), BF16),
            pltpu.VMEM((1, D), F32),
        ],
        compiler_params=params(51),
        cost_estimate=cost(150 * 10**9, 1 << 20),
        name="expert_%d" % member,
    )(*tables, place, arrived, router_rows, *pieces)


def update(member, summed, masters, scores, router_sum, held):
    own, first, second = summed
    mine = own.shape[0] - 1
    steps = 2
    rows = mine // steps
    tile = pl.BlockSpec((rows, 32, 128), lambda n: (n, 0, 0))
    last = pl.BlockSpec((1, 32, 128), lambda n: (mine, 0, 0))
    block = pl.BlockSpec((rows, BS * BS), lambda n: (member * steps + n, 0))
    whole = lambda array: pl.BlockSpec(array.shape, lambda n: (0,) * array.ndim)
    return pl.pallas_call(
        functools.partial(update_kernel, member=member),
        grid=(steps,),
        in_specs=[tile] * 3
        + [last] * 3
        + [block, whole(scores), whole(router_sum)]
        + [pl.BlockSpec(memory_space=pl.ANY)] * len(held),
        out_specs=[block, whole(scores), whole(router_sum)],
        out_shape=[
            jax.ShapeDtypeStruct(masters.shape, F32),
            jax.ShapeDtypeStruct(scores.shape, F32),
            jax.ShapeDtypeStruct(router_sum.shape, F32),
        ],
        input_output_aliases={9 + at: at for at in range(len(held))},
        scratch_shapes=[pltpu.VMEM((rows // 8, 256, 128), F32), pltpu.VMEM((mine, 128), F32)],
        compiler_params=params(56),
        cost_estimate=cost(0, 1 << 20),
        name="update_%d" % member,
    )(own, first, second, own, first, second, masters, scores, router_sum, *held)


def combine(picks, back, count):
    locals_count = len(back)
    peers, _, width = back[0].shape
    column = pl.BlockSpec((count, STEP), lambda n: (0, n))
    return pl.pallas_call(
        functools.partial(combine_kernel, locals_count=locals_count),
        grid=(width // STEP,),
        in_specs=[pl.BlockSpec(picks.shape, lambda n: (0, 0))]
        + [pl.BlockSpec((peers, 16, STEP), lambda n: (0, 0, n))] * locals_count,
        out_specs=[column, column],
        out_shape=[jax.ShapeDtypeStruct((count, width), BF16)] * 2,
        scratch_shapes=[pltpu.VMEM((count, locals_count * 8 * peers), BF16)],
        compiler_params=params(24),
        cost_estimate=cost(150 * 10**9, 1 << 20),
        name="combine",
    )(picks, *back)


def slot_tables(kept, owners, me):
    numbers = jnp.arange(BLOCKS, dtype=jnp.int32)
    slots = jnp.arange(MAXB, dtype=jnp.int32)
    per = MAXB // owners
    matrix = jnp.arange(3, dtype=jnp.int32)[None, :, None]
    ahead = (slots // per - me) % owners
    order = jnp.where(ahead == 0, 0, jnp.where(ahead == owners - 1, 1, ahead + 1))
    place = order * (3 * per) + slots % per + matrix * per
    hits = kept[:, :, None, :] == numbers[None, None, :, None]
    inverse = 3 * MAXB + jnp.sum(jnp.where(hits, place[:, :, None, :] - 3 * MAXB, 0), axis=-1)
    valid = kept < BLOCKS
    block = jnp.where(valid, kept, 0)
    width = jnp.array([FF // BS, FF // BS, D // BS], jnp.int32)[None, :, None]
    block_row, block_col = block // width, block % width
    empty = jnp.where(matrix == 2, FF, D)
    rows = jnp.where(valid, block_row * BS + 32 * (block_col & 1), empty)
    lanes = (block_col >> 1) * 128 + jnp.where(matrix == 1, FF, 0)
    flat = lambda table: table.reshape(-1).astype(jnp.int32)
    return flat(inverse), flat(rows), flat(lanes)


def shift(array, step):
    owners = lax.axis_size("dp")
    return lax.ppermute(array, "dp", [(i, (i + step) % owners) for i in range(owners)])


def gather_first(first, second):
    left_a, right_b = shift(first, 1), shift(second, -1)
    return [first, second, left_a, shift(second, 1), shift(first, -1), right_b]


def gather_second(pieces):
    return list(pieces) + [shift(pieces[2], 1), shift(pieces[5], -1)]


def scatter_first(step, own, right, far, left):
    ahead, behind = (right, left) if step == 1 else (left, right)
    return own, ahead, [shift(far, step), shift(behind, -step)]


def scatter_second(step, own, ahead, moving):
    passing, direct = moving
    return own, direct, shift(ahead + passing, step)


def body(tokens, out_grad, token_picks, router, kept_blocks, masters, scores):
    locals_count = kept_blocks.shape[0]
    owners = lax.axis_size("dp")
    peers = lax.axis_size("expert")
    me = lax.axis_index("dp").astype(jnp.int32)
    count, width = tokens.shape
    per = masters.shape[2]
    picks = token_picks[0].T
    flat_masters = masters.reshape(locals_count * 3 * per, BS * BS)
    after = lax.optimization_barrier

    def exchange(array):
        return lax.all_to_all(array, "expert", split_axis=0, concat_axis=0, tiled=True)

    sent = list(pick(picks, tokens, out_grad, locals_count, peers))
    sent[0], rest_masters, kept_blocks, router = after((sent[0], flat_masters, kept_blocks, router))
    halves = [pack(rest_masters, member, locals_count) for member in range(locals_count)]
    tables = slot_tables(kept_blocks, owners, me)
    router_rows = router.T.reshape(locals_count, width // BS, 32, 2).transpose(0, 1, 3, 2)
    router_rows = router_rows.reshape(locals_count, width).astype(F32)
    place = me.reshape(1)

    pieces = [gather_first(*halves[0])]
    through, tables, router_rows, halves[1:] = after(((pieces[0][2], pieces[0][5]), tables, router_rows, halves[1:]))
    pieces[0][2], pieces[0][5] = through
    pieces[0] = gather_second(pieces[0])
    arrived = [exchange(sent[0])]
    for member in range(1, locals_count):
        pieces.append(gather_first(*halves[member]))
        rows, arrived[-1] = after((sent[member], arrived[-1]))
        arrived.append(exchange(rows))
    summed, back = [], []
    for member in range(locals_count):
        rows = arrived[member]
        if member:
            rows, send, through = after((rows, send, (pieces[member][2], pieces[member][5])))
            pieces[member][2], pieces[member][5] = through
            pieces[member] = gather_second(pieces[member])
            back.append(exchange(send))
        send, *gradients = run_expert(member, tables, place, pieces[member], rows, router_rows)
        summed.append(scatter_first(1 - 2 * (member % 2), *gradients))
    send, back, summed[:-1] = after((send, back, summed[:-1]))
    back.append(exchange(send))
    summed = [scatter_second(1 - 2 * (member % 2), *terms) for member, terms in enumerate(summed)]
    score_sum = scores.transpose(1, 0, 2)
    router_sum = jnp.zeros((locals_count, width // owners), F32)
    held = ()
    for member in range(locals_count - 1):
        new, score_sum, router_sum = update(member, summed[member], flat_masters, score_sum, router_sum, held)
        held = (new,)
    held, picks = after((held, picks))
    layer_out, input_grad = combine(picks, back, count)
    last, layer_out = after((summed[-1], layer_out))
    new, score_sum, router_sum = update(locals_count - 1, last, flat_masters, score_sum, router_sum, held)
    return layer_out, input_grad, new.reshape(masters.shape), score_sum.transpose(1, 0, 2), router_sum.T


def solution(mesh):
    return jax.shard_map(
        body,
        mesh=mesh,
        in_specs=(
            P(("dp", "expert"), None),
            P(("dp", "expert"), None),
            P(("dp", "expert"), None, None),
            P(None, "expert"),
            P("expert", None, None),
            P("expert", None, "dp", None),
            P("expert", None, "dp"),
        ),
        out_specs=(
            P(("dp", "expert"), None),
            P(("dp", "expert"), None),
            P("expert", None, "dp", None),
            P("expert", None, "dp"),
            P("dp", "expert"),
        ),
        check_vma=False,
    )
```

```python
import functools

import jax
import jax.numpy as jnp
from jax import lax
from jax.experimental import pallas as pl
from jax.experimental.pallas import tpu as pltpu
from jax.sharding import PartitionSpec as P

D = 2048
FF = 768
BS = 64
MAXB = 128
OWNERS = 4
BLOCKS = (D // BS) * (FF // BS)
LEARN_RATE = 0.005
SCORE_RATE = 0.05
CHUNK = 256
STEP = 1024
UNROLL = 32
F32 = jnp.float32
BF16 = jnp.bfloat16
NN = (((1,), (0,)), ((), ()))
NT = (((1,), (1,)), ((), ()))
TN = (((0,), (0,)), ((), ()))


def dot(left, right, dims=NN):
    return lax.dot_general(left, right, dims, preferred_element_type=F32)


def iota(shape, dim):
    return lax.broadcasted_iota(jnp.int32, shape, dim)


def one_hot(flag):
    return jnp.where(flag, 1.0, 0.0).astype(BF16)


def split_matrix(size):
    col = iota((size, size), 1)
    source = ((col >> 6) << 6) + 2 * (col & 31) + ((col >> 5) & 1)
    return one_hot(iota((size, size), 0) == source)


def pick_columns(picks_ref, member, locals_count):
    experts = picks_ref.shape[1]
    rows = 8 * experts // locals_count
    expert = (iota((rows, experts), 0) >> 3) * locals_count + member
    spread = one_hot(iota((rows, experts), 1) == expert)
    wide = dot(spread, picks_ref[...].astype(F32).astype(BF16), NT)
    keep = iota(wide.shape, 1) == (iota(wide.shape, 0) & 7)
    return jnp.sum(jnp.where(keep, wide, 0.0), axis=1, keepdims=True).astype(jnp.int32)


def interleave(first, second):
    width = first.shape[1]
    pair = [first.reshape(-1, 8, width), second.reshape(-1, 8, width)]
    return jnp.concatenate(pair, axis=1).astype(BF16)


def apart(block):
    wide = block.astype(F32)
    width = wide.shape[2]
    return wide[:, :8, :].reshape(-1, width), wide[:, 8:, :].reshape(-1, width)


def pick_kernel(picks_ref, tokens_ref, grads_ref, *rest, locals_count):
    out_refs, hot_ref = rest[:locals_count], rest[locals_count]
    rows = hot_ref.shape[0] // locals_count

    @pl.when(pl.program_id(0) == 0)
    def _():
        for member in range(locals_count):
            index = pick_columns(picks_ref, member, locals_count)
            hot_ref[member * rows : (member + 1) * rows, :] = one_hot(
                iota((rows, hot_ref.shape[1]), 1) == index
            )

    split = split_matrix(CHUNK)
    for start in range(0, tokens_ref.shape[1], CHUNK):
        cols = slice(start, start + CHUNK)
        tokens = dot(hot_ref[...], dot(tokens_ref[:, cols], split).astype(BF16))
        grads = dot(hot_ref[...], grads_ref[:, cols])
        for member in range(locals_count):
            mine = slice(member * rows, (member + 1) * rows)
            out_refs[member][:, :, cols] = interleave(tokens[mine], grads[mine])


def pack_kernel(masters_ref, *rest):
    out_refs, lines_ref = rest[:-1], rest[-1]
    for at, out_ref in enumerate(out_refs):

        @pl.when(pl.program_id(0) == at)
        def _(out_ref=out_ref):
            for group in range(masters_ref.shape[0] // 8):
                for k in range(32):
                    lines_ref[group, 8 * k : 8 * k + 8, :] = masters_ref[
                        8 * group : 8 * group + 8, 128 * k : 128 * k + 128
                    ]
                for s in range(8):
                    line = lines_ref[group, pl.ds(s, 32, stride=8), :]
                    out_ref[8 * group + s] = line.astype(BF16)


def expert_kernel(
    inverse_ref, row_ref, lane_ref, me_ref,
    arriving_ref, router_ref, *rest,
    member,
):
    piece_refs, sending_ref, grad_refs = rest[:8], rest[8], rest[9:13]
    (
    copies_ref, packed_ref, arrived_ref, send_ref, sigma_ref, in_sems, out_sems,
    wide_ref, down_ref, rows_ref, grads_ref, pre_ref, part_ref, both_ref,
    grad_wide_ref, grad_down_ref, router_out_ref,
    ) = rest[13:]
    length = piece_refs[0].shape[0]
    loads = [
        pltpu.make_async_copy(piece, copies_ref.at[pl.ds(at * length, length)], in_sems.at[at])
        for at, piece in enumerate(piece_refs)
    ]
    rows_in = pltpu.make_async_copy(arriving_ref, arrived_ref, in_sems.at[len(loads)])
    rows_in.start()
    for load in loads:
        load.start()
    copies_ref[3 * MAXB] = jnp.zeros((32, 128), BF16)
    grad_wide_ref[D:, :] = jnp.zeros((BS, 2 * FF), BF16)
    grad_down_ref[FF:, :] = jnp.zeros((BS, D), BF16)
    base, slot_base = member * 3 * BLOCKS, member * 3 * MAXB
    lane = iota((32, 128), 1)
    half = lane < 64

    count = rows_ref.shape[0]
    chunks = D // CHUNK
    mine = slice(member, member + 1)

    def take(n, logit):
        cols = pl.ds(pl.multiple_of(n * CHUNK, CHUNK), CHUNK)
        rows, grads = apart(arrived_ref[:, :, cols])
        rows_ref[:, cols] = rows.astype(BF16)
        grads_ref[:, cols] = grads.astype(BF16)
        return logit + jnp.sum(rows * router_ref[mine, cols], axis=1, keepdims=True)

    rows_in.wait()
    logit = lax.fori_loop(0, chunks, take, jnp.zeros((count, 1), F32))
    gating = 1.0 / (1.0 + jnp.exp(-logit))

    for load in loads:
        load.wait()

    def place(target_ref, matrix, block, row, col):
        one = copies_ref[inverse_ref[base + matrix * BLOCKS + block]]
        two = copies_ref[inverse_ref[base + matrix * BLOCKS + block + 1]]
        crossed = pltpu.roll(jnp.where(half, two, one), 64, 1)
        target_ref[pl.ds(row, 32), col : col + 128] = jnp.where(half, one, crossed)
        target_ref[pl.ds(row + 32, 32), col : col + 128] = jnp.where(half, crossed, two)

    @pl.loop(0, D // BS, unroll=2)
    def _(r):
        row = pl.multiple_of(r * BS, BS)
        for matrix in range(2):
            for pair in range(FF // BS // 2):
                place(wide_ref, matrix, r * (FF // BS) + 2 * pair, row, matrix * FF + 128 * pair)

    @pl.loop(0, FF // BS, unroll=2)
    def _(r):
        row = pl.multiple_of(r * BS, BS)
        for pair in range(D // BS // 2):
            place(down_ref, 2, r * (D // BS) + 2 * pair, row, 128 * pair)

    @pl.loop(0, 2 * FF // 512, unroll=3)
    def _(n):
        cols = pl.ds(pl.multiple_of(n * 512, 512), 512)
        pre_ref[:, cols] = dot(rows_ref[...], wide_ref[:, cols])

    split = split_matrix(CHUNK)
    hidden_list = []
    for n in range(FF // CHUNK):
        gate_pre = pre_ref[:, n * CHUNK : (n + 1) * CHUNK]
        up_pre = pre_ref[:, FF + n * CHUNK : FF + (n + 1) * CHUNK]
        sigma = 1.0 / (1.0 + jnp.exp(-gate_pre))
        sigma_ref[:, n * CHUNK : (n + 1) * CHUNK] = sigma
        hidden = (gate_pre * sigma * up_pre).astype(BF16)
        hidden_list.append(dot(hidden, split).astype(BF16))
    hidden_split = jnp.concatenate(hidden_list, axis=1)

    @pl.loop(0, D // 512, unroll=2)
    def _(n):
        cols = pl.ds(pl.multiple_of(n * 512, 512), 512)
        part_ref[:, cols] = (gating * dot(hidden_split, down_ref[:, cols])).astype(BF16)
        grads_ref[:, cols] = (gating * grads_ref[:, cols].astype(F32)).astype(BF16)

    logit_sum = jnp.zeros((count, 1), F32)
    for n in range(FF // CHUNK):
        spread = dot(grads_ref[...], down_ref[n * CHUNK : (n + 1) * CHUNK, :], NT)
        high = spread.astype(BF16)
        low = (spread - high.astype(F32)).astype(BF16)
        hidden_grad = dot(high, split, NT) + dot(low, split, NT)
        logit_sum = logit_sum + jnp.sum(
            hidden_list[n].astype(F32) * spread, axis=1, keepdims=True
        )
        gate_pre = pre_ref[:, n * CHUNK : (n + 1) * CHUNK]
        up_pre = pre_ref[:, FF + n * CHUNK : FF + (n + 1) * CHUNK]
        sigma = sigma_ref[:, n * CHUNK : (n + 1) * CHUNK]
        gate_grad = hidden_grad * up_pre * sigma * (1.0 + gate_pre * (1.0 - sigma))
        both_ref[:, n * CHUNK : (n + 1) * CHUNK] = gate_grad.astype(BF16)
        both_ref[:, FF + n * CHUNK : FF + (n + 1) * CHUNK] = (hidden_grad * gate_pre * sigma).astype(BF16)
        grad_down_ref[n * CHUNK : (n + 1) * CHUNK, :] = dot(hidden_list[n], grads_ref[...], TN).astype(BF16)
    logit_grad = logit_sum * (1.0 - gating)

    @pl.loop(0, chunks, unroll=2)
    def _(n):
        cols = pl.ds(pl.multiple_of(n * CHUNK, CHUNK), CHUNK)
        part = dot(both_ref[...], wide_ref[cols, :], NT) + logit_grad * router_ref[mine, cols]
        send_ref[:, :, cols] = interleave(part_ref[:, cols].astype(F32), part)
        rows = rows_ref[:, cols]
        router_out_ref[:, cols] = jnp.sum(logit_grad * rows.astype(F32), axis=0, keepdims=True)
        grad_wide_ref[cols, :] = dot(rows, both_ref[...], TN).astype(BF16)

    rows_out = pltpu.make_async_copy(send_ref, sending_ref, out_sems.at[len(grad_refs)])
    rows_out.start()

    def cut(source_ref, matrix, slot, place_in):
        at = slot_base + matrix * MAXB + slot
        row = pl.multiple_of(row_ref[at], 32)
        other = pl.multiple_of(row ^ 32, 32)
        cols = pl.ds(pl.multiple_of(lane_ref[at], 128), 128)
        stay = source_ref[pl.ds(row, 32), cols]
        move = pltpu.roll(source_ref[pl.ds(other, 32), cols], 64, 1)
        packed_ref[place_in] = jnp.where((lane & 64) == 2 * (row & 32), stay, move)

    per = MAXB // OWNERS
    part = packed_ref.shape[0] // OWNERS
    stores = [rows_out]
    for ahead in (2, 1, 3, 0):
        owner = (me_ref[0] + ahead) & (OWNERS - 1)
        first = ahead * part
        for matrix in range(3):
            source_ref = grad_down_ref if matrix == 2 else grad_wide_ref

            @pl.loop(0, per // UNROLL)
            def _(group, first=first, matrix=matrix, source_ref=source_ref, owner=owner):
                for step in range(UNROLL):
                    s = group * UNROLL + step
                    cut(source_ref, matrix, owner * per + s, first + matrix * per + s)

        start = owner * (D // OWNERS)
        lines = [
            router_out_ref[:, pl.ds(pl.multiple_of(start + at, 128), 128)]
            for at in range(0, D // OWNERS, 128)
        ]
        lines.append(jnp.zeros((32 - len(lines), 128), F32))
        packed_ref[first + 3 * per] = jnp.concatenate(lines, axis=0).astype(BF16)
        store = pltpu.make_async_copy(
            packed_ref.at[pl.ds(first, part)], grad_refs[ahead], out_sems.at[ahead]
        )
        store.start()
        stores.append(store)
    for store in stores:
        store.wait()


def update_kernel(
    own_ref, first_ref, second_ref, own_last_ref, first_last_ref, second_last_ref,
    masters_ref, scores_ref, router_ref, *rest,
    member,
):
    out_ref, scores_out_ref, router_out_ref, lines_ref, total_ref = rest[-5:]
    step, steps = pl.program_id(0), pl.num_programs(0)
    rows = masters_ref.shape[0]
    for s in range(rows):
        summed = own_ref[s].astype(F32) + first_ref[s].astype(F32) + second_ref[s].astype(F32)
        lines_ref[s // 8, pl.ds(s % 8, 32, stride=8), :] = summed

    for group in range(rows // 8):
        total = jnp.zeros((8, 128), F32)
        here = slice(8 * group, 8 * group + 8)
        for k in range(32):
            cols = slice(128 * k, 128 * k + 128)
            gradient = lines_ref[group, 8 * k : 8 * k + 8, :]
            held = masters_ref[here, cols]
            out_ref[here, cols] = held - LEARN_RATE * gradient
            total = total + held * gradient
        total_ref[pl.ds(pl.multiple_of(step * rows + 8 * group, 8), 8), :] = total

    @pl.when(step == steps - 1)
    def _():
        exact = functools.partial(
            lax.dot_general, dimension_numbers=NT, precision=lax.Precision.HIGHEST, preferred_element_type=F32
        )
        count, experts, per = scores_ref.shape
        mine = iota((experts, per), 0) == member
        for matrix in range(count):
            sums = exact(jnp.ones((8, 128), F32), total_ref[matrix * per : (matrix + 1) * per, :])
            change = jnp.where(mine, jnp.broadcast_to(sums[:1], mine.shape), 0.0)
            scores_out_ref[matrix] = scores_ref[matrix] - SCORE_RATE * change
        last = own_last_ref[0].astype(F32) + first_last_ref[0].astype(F32) + second_last_ref[0].astype(F32)
        last = exact(last, split_matrix(128).astype(F32))
        width = router_ref.shape[1]
        line = jnp.concatenate([last[at : at + 1] for at in range(width // 128)], axis=1)
        held = iota(router_ref.shape, 0) == member
        router_out_ref[...] = jnp.where(held, jnp.broadcast_to(line, router_ref.shape), router_ref[...])


def combine_kernel(picks_ref, *rest, locals_count):
    back_refs = rest[:locals_count]
    out_ref, in_ref, hot_ref = rest[locals_count:]
    count = out_ref.shape[0]

    @pl.when(pl.program_id(0) == 0)
    def _():
        same = one_hot(iota((count, count), 0) == iota((count, count), 1))
        for member in range(locals_count):
            index = pick_columns(picks_ref, member, locals_count)
            hot = one_hot(iota((index.shape[0], count), 1) == index)
            rows = index.shape[0]
            hot_ref[:, member * rows : (member + 1) * rows] = dot(hot, same, TN).astype(BF16)

    split = split_matrix(CHUNK)
    for start in range(0, out_ref.shape[1], CHUNK):
        cols = slice(start, start + CHUNK)
        pairs = [apart(back_ref[:, :, cols]) for back_ref in back_refs]
        out_rows = jnp.concatenate([pair[0].astype(BF16) for pair in pairs], axis=0)
        in_rows = jnp.concatenate([pair[1].astype(BF16) for pair in pairs], axis=0)
        out_ref[:, cols] = dot(hot_ref[...], out_rows).astype(BF16)
        in_ref[:, cols] = dot(dot(hot_ref[...], in_rows).astype(BF16), split, NT).astype(BF16)


def params(mib):
    return pltpu.CompilerParams(vmem_limit_bytes=mib * 1024 * 1024)


def cost(flops, moved):
    return pl.CostEstimate(flops=flops, bytes_accessed=moved, transcendentals=0)


def pick(picks, tokens, grads, locals_count, peers):
    count, width = tokens.shape
    column = pl.BlockSpec((count, STEP), lambda n: (0, n))
    return pl.pallas_call(
        functools.partial(pick_kernel, locals_count=locals_count),
        grid=(width // STEP,),
        in_specs=[pl.BlockSpec(picks.shape, lambda n: (0, 0)), column, column],
        out_specs=[pl.BlockSpec((peers, 16, STEP), lambda n: (0, 0, n))] * locals_count,
        out_shape=[jax.ShapeDtypeStruct((peers, 16, width), BF16)] * locals_count,
        scratch_shapes=[pltpu.VMEM((locals_count * 8 * peers, count), BF16)],
        compiler_params=params(56),
        cost_estimate=cost(0, 1 << 20),
        name="pick",
    )(picks, tokens, grads)


def pack(masters, member, experts):
    mine = masters.shape[0] // experts // 2
    return pl.pallas_call(
        pack_kernel,
        grid=(2,),
        in_specs=[pl.BlockSpec((mine, BS * BS), lambda n: (2 * member + n, 0))],
        out_specs=[pl.BlockSpec((mine, 32, 128), lambda n: (0, 0, 0))] * 2,
        out_shape=[jax.ShapeDtypeStruct((mine, 32, 128), BF16)] * 2,
        scratch_shapes=[pltpu.VMEM((mine // 8, 256, 128), F32)],
        compiler_params=params(56),
        cost_estimate=cost(0, 1 << 20),
        name="pack_%d" % member,
    )(masters)


def run_expert(member, tables, place, pieces, arrived, router_rows):
    peers = arrived.shape[0]
    count = 8 * peers
    whole = pl.BlockSpec(memory_space=pltpu.VMEM)
    scalar = pl.BlockSpec(memory_space=pltpu.SMEM)
    anywhere = pl.BlockSpec(memory_space=pl.ANY)
    part = 3 * MAXB // OWNERS + 1
    lengths = [part] * OWNERS
    return pl.pallas_call(
        functools.partial(expert_kernel, member=member),
        in_specs=[scalar] * 4 + [anywhere, whole] + [anywhere] * len(pieces),
        out_specs=[anywhere] * (1 + len(lengths)),
        out_shape=[jax.ShapeDtypeStruct((peers, 16, D), BF16)]
        + [jax.ShapeDtypeStruct((length, 32, 128), BF16) for length in lengths],
        scratch_shapes=[
            pltpu.VMEM((3 * MAXB + 1, 32, 128), BF16),
            pltpu.VMEM((OWNERS * part, 32, 128), BF16),
            pltpu.VMEM((peers, 16, D), BF16),
            pltpu.VMEM((peers, 16, D), BF16),
            pltpu.VMEM((count, FF), F32),
            pltpu.SemaphoreType.DMA((len(pieces) + 1,)),
            pltpu.SemaphoreType.DMA((len(lengths) + 1,)),
            pltpu.VMEM((D, 2 * FF), BF16),
            pltpu.VMEM((FF, D), BF16),
            pltpu.VMEM((count, D), BF16),
            pltpu.VMEM((count, D), BF16),
            pltpu.VMEM((count, 2 * FF), F32),
            pltpu.VMEM((count, D), BF16),
            pltpu.VMEM((count, 2 * FF), BF16),
            pltpu.VMEM((D + BS, 2 * FF), BF16),
            pltpu.VMEM((FF + BS, D), BF16),
            pltpu.VMEM((1, D), F32),
        ],
        compiler_params=params(51),
        cost_estimate=cost(150 * 10**9, 1 << 20),
        name="expert_%d" % member,
    )(*tables, place, arrived, router_rows, *pieces)


def update(member, summed, masters, scores, router_sum, held):
    own, first, second = summed
    mine = own.shape[0] - 1
    steps = 2
    rows = mine // steps
    tile = pl.BlockSpec((rows, 32, 128), lambda n: (n, 0, 0))
    last = pl.BlockSpec((1, 32, 128), lambda n: (mine, 0, 0))
    block = pl.BlockSpec((rows, BS * BS), lambda n: (member * steps + n, 0))
    whole = lambda array: pl.BlockSpec(array.shape, lambda n: (0,) * array.ndim)
    return pl.pallas_call(
        functools.partial(update_kernel, member=member),
        grid=(steps,),
        in_specs=[tile] * 3
        + [last] * 3
        + [block, whole(scores), whole(router_sum)]
        + [pl.BlockSpec(memory_space=pl.ANY)] * len(held),
        out_specs=[block, whole(scores), whole(router_sum)],
        out_shape=[
            jax.ShapeDtypeStruct(masters.shape, F32),
            jax.ShapeDtypeStruct(scores.shape, F32),
            jax.ShapeDtypeStruct(router_sum.shape, F32),
        ],
        input_output_aliases={9 + at: at for at in range(len(held))},
        scratch_shapes=[pltpu.VMEM((rows // 8, 256, 128), F32), pltpu.VMEM((mine, 128), F32)],
        compiler_params=params(56),
        cost_estimate=cost(0, 1 << 20),
        name="update_%d" % member,
    )(own, first, second, own, first, second, masters, scores, router_sum, *held)


def combine(picks, back, count):
    locals_count = len(back)
    peers, _, width = back[0].shape
    column = pl.BlockSpec((count, STEP), lambda n: (0, n))
    return pl.pallas_call(
        functools.partial(combine_kernel, locals_count=locals_count),
        grid=(width // STEP,),
        in_specs=[pl.BlockSpec(picks.shape, lambda n: (0, 0))]
        + [pl.BlockSpec((peers, 16, STEP), lambda n: (0, 0, n))] * locals_count,
        out_specs=[column, column],
        out_shape=[jax.ShapeDtypeStruct((count, width), BF16)] * 2,
        scratch_shapes=[pltpu.VMEM((count, locals_count * 8 * peers), BF16)],
        compiler_params=params(24),
        cost_estimate=cost(150 * 10**9, 1 << 20),
        name="combine",
    )(picks, *back)


def slot_tables(kept, owners, me):
    numbers = jnp.arange(BLOCKS, dtype=jnp.int32)
    slots = jnp.arange(MAXB, dtype=jnp.int32)
    per = MAXB // owners
    matrix = jnp.arange(3, dtype=jnp.int32)[None, :, None]
    ahead = (slots // per - me) % owners
    order = jnp.where(ahead == 0, 0, jnp.where(ahead == owners - 1, 1, ahead + 1))
    place = order * (3 * per) + slots % per + matrix * per
    hits = kept[:, :, None, :] == numbers[None, None, :, None]
    inverse = 3 * MAXB + jnp.sum(jnp.where(hits, place[:, :, None, :] - 3 * MAXB, 0), axis=-1)
    valid = kept < BLOCKS
    block = jnp.where(valid, kept, 0)
    width = jnp.array([FF // BS, FF // BS, D // BS], jnp.int32)[None, :, None]
    block_row, block_col = block // width, block % width
    empty = jnp.where(matrix == 2, FF, D)
    rows = jnp.where(valid, block_row * BS + 32 * (block_col & 1), empty)
    lanes = (block_col >> 1) * 128 + jnp.where(matrix == 1, FF, 0)
    flat = lambda table: table.reshape(-1).astype(jnp.int32)
    return flat(inverse), flat(rows), flat(lanes)


def shift(array, step):
    owners = lax.axis_size("dp")
    return lax.ppermute(array, "dp", [(i, (i + step) % owners) for i in range(owners)])


def gather_first(first, second):
    left_a, right_b = shift(first, 1), shift(second, -1)
    return [first, second, left_a, shift(second, 1), shift(first, -1), right_b]


def gather_second(pieces):
    return list(pieces) + [shift(pieces[2], 1), shift(pieces[5], -1)]


def scatter_first(step, own, right, far, left):
    ahead, behind = (right, left) if step == 1 else (left, right)
    return own, ahead, [shift(far, step), shift(behind, -step)]


def scatter_second(step, own, ahead, moving):
    passing, direct = moving
    return own, direct, shift(ahead + passing, step)


def body(tokens, out_grad, token_picks, router, kept_blocks, masters, scores):
    locals_count = kept_blocks.shape[0]
    owners = lax.axis_size("dp")
    peers = lax.axis_size("expert")
    me = lax.axis_index("dp").astype(jnp.int32)
    count, width = tokens.shape
    per = masters.shape[2]
    picks = token_picks[0].T
    flat_masters = masters.reshape(locals_count * 3 * per, BS * BS)
    after = lax.optimization_barrier

    def exchange(array):
        return lax.all_to_all(array, "expert", split_axis=0, concat_axis=0, tiled=True)

    sent = list(pick(picks, tokens, out_grad, locals_count, peers))
    sent[0], rest_masters, kept_blocks, router = after((sent[0], flat_masters, kept_blocks, router))
    halves = [pack(rest_masters, member, locals_count) for member in range(locals_count)]
    tables = slot_tables(kept_blocks, owners, me)
    router_rows = router.T.reshape(locals_count, width // BS, 32, 2).transpose(0, 1, 3, 2)
    router_rows = router_rows.reshape(locals_count, width).astype(F32)
    place = me.reshape(1)

    pieces = [gather_first(*halves[0])]
    through, tables, router_rows, halves[1:] = after(((pieces[0][2], pieces[0][5]), tables, router_rows, halves[1:]))
    pieces[0][2], pieces[0][5] = through
    pieces[0] = gather_second(pieces[0])
    arrived = [exchange(sent[0])]
    for member in range(1, locals_count):
        pieces.append(gather_first(*halves[member]))
        rows, arrived[-1] = after((sent[member], arrived[-1]))
        arrived.append(exchange(rows))
    summed, back = [], []
    for member in range(locals_count):
        rows = arrived[member]
        if member:
            rows, send, through = after((rows, send, (pieces[member][2], pieces[member][5])))
            pieces[member][2], pieces[member][5] = through
            pieces[member] = gather_second(pieces[member])
            back.append(exchange(send))
        send, *gradients = run_expert(member, tables, place, pieces[member], rows, router_rows)
        summed.append(scatter_first(1 - 2 * (member % 2), *gradients))
    send, back, summed[:-1] = after((send, back, summed[:-1]))
    back.append(exchange(send))
    summed = [scatter_second(1 - 2 * (member % 2), *terms) for member, terms in enumerate(summed)]
    score_sum = scores.transpose(1, 0, 2)
    router_sum = jnp.zeros((locals_count, width // owners), F32)
    held = ()
    for member in range(locals_count - 1):
        new, score_sum, router_sum = update(member, summed[member], flat_masters, score_sum, router_sum, held)
        held = (new,)
    held, picks = after((held, picks))
    layer_out, input_grad = combine(picks, back, count)
    last, layer_out = after((summed[-1], layer_out))
    new, score_sum, router_sum = update(locals_count - 1, last, flat_masters, score_sum, router_sum, held)
    return layer_out, input_grad, new.reshape(masters.shape), score_sum.transpose(1, 0, 2), router_sum.T


def solution(mesh):
    return jax.shard_map(
        body,
        mesh=mesh,
        in_specs=(
            P(("dp", "expert"), None),
            P(("dp", "expert"), None),
            P(("dp", "expert"), None, None),
            P(None, "expert"),
            P("expert", None, None),
            P("expert", None, "dp", None),
            P("expert", None, "dp"),
        ),
        out_specs=(
            P(("dp", "expert"), None),
            P(("dp", "expert"), None),
            P("expert", None, "dp", None),
            P("expert", None, "dp"),
            P("dp", "expert"),
        ),
        check_vma=False,
    )
```
